512 devices in a mesh: fsdp: 128 (over z, x, core), mp: 4 (over y).
Axes of the slice: x: 4, y: 4, z: 16, core: 2. Of those that a mesh axis runs over, the one named last changes fastest.
Arguments:
- gradient: bfloat16 [128, 512, 512], P(None, 'fsdp', 'mp')
- owner_map: int32 [128], replicated, may hold values from 0 to 127, as said below
- left_stats: float32 [384, 512, 512], P('fsdp', 'mp'), as said below
- right_stats: float32 [384, 512, 512], P('fsdp', 'mp'), as said below
- left_root: float32 [384, 512, 512], P('fsdp', 'mp'), as said below
- right_root: float32 [384, 512, 512], P('fsdp', 'mp'), as said below
Outputs:
- update: bfloat16 [128, 512, 512], P(None, 'fsdp', 'mp')
- left_new: float32 [384, 512, 512], P('fsdp', 'mp')
- right_new: float32 [384, 512, 512], P('fsdp', 'mp')
The draws below stay inside these ranges and needn't reach their ends.
Inputs may be any that keep to these rules, and one draw needn't show every extreme that they name: `owner_map`: no index is named by more than 3 entries, and some index by exactly 3. `left_stats`: every block is symmetric. `right_stats`: every block is symmetric. `left_root`: every block is symmetric. `right_root`: every block is symmetric.
All inputs are finite; a program needn't handle non-finite values.
Results may differ from the reference program's by a relative error of at most 0.0014.
Values may be sent and summed in bfloat16 or wider, within the bound.
No kernel may reach another device: no remote copies, remote signals or barrier semaphores. Data moves between devices by JAX's collectives and lax.ppermute only.
A program may use at most 64 MiB of HBM per device.

```python
import math
import jax
import jax.numpy as jnp
from jax import lax

BLOCK = 512
SLOTS = 3
BLOCKS = 128
CELLS = 384


def symmetric_blocks(entries, diag_key, low_value, high_value, spread):
    order = entries.shape[1]
    mirrored = (entries + jnp.swapaxes(entries, 1, 2)) * (spread / math.sqrt(2.0 * order))
    exponent = jax.random.uniform(diag_key, entries.shape[:2], jnp.float32, math.log(low_value), math.log(high_value))
    indices = jnp.arange(order)
    identity = (indices[:, None] == indices[None, :]).astype(jnp.float32)
    return mirrored + jnp.exp(exponent)[:, :, None] * identity[None, :, :]


def coherent_part(pattern, strength):
    order = pattern.shape[1]
    return strength / math.sqrt(order) * pattern[:, :, None] * pattern[:, None, :]


def draw_gradient(key, part):
    key = jax.random.fold_in(key, 5)
    subkeys = jax.random.split(key, 3)
    block_shape = (BLOCKS, BLOCK, BLOCK)
    row_scale = 0.3 * jnp.exp(jax.random.uniform(subkeys[1], (BLOCKS, BLOCK, 1), jnp.float32, 0.0, math.log(10.0)))
    col_scale = 0.3 * jnp.exp(jax.random.uniform(subkeys[2], (BLOCKS, 1, BLOCK), jnp.float32, 0.0, math.log(10.0)))
    rising = jnp.exp(math.log(3.0) * (jnp.arange(BLOCK, dtype=jnp.float32) / BLOCK - 0.5))[None, :, None]
    entries = jax.random.normal(subkeys[0], block_shape, jnp.float32)
    return (entries * row_scale * col_scale * rising).astype(jnp.bfloat16)


def draw_owner_map(key, part):
    key = jax.random.fold_in(key, 11)
    first_key, second_key = jax.random.split(key)
    shuffled = jax.random.permutation(first_key, CELLS).astype(jnp.int32)
    position = jnp.argsort(shuffled).astype(jnp.int32)
    full_owner = shuffled[0] // SLOTS
    cell_range = jnp.arange(CELLS, dtype=jnp.int32)
    scores = jnp.where(cell_range // SLOTS == full_owner, -1, position)
    chosen = jnp.argsort(scores, stable=True)[:BLOCKS].astype(jnp.int32)
    owners = chosen // SLOTS
    reorder = jax.random.permutation(second_key, BLOCKS)
    return owners[reorder].astype(jnp.int32)


def draw_left_stats(key, part):
    key = jax.random.fold_in(key, 21)
    first_key, second_key = jax.random.split(key)
    block_shape = (CELLS, BLOCK, BLOCK)
    entries = jax.random.normal(first_key, block_shape, jnp.float32)
    return symmetric_blocks(entries, second_key, 1.0, 3.0, 0.45)


def draw_right_stats(key, part):
    key = jax.random.fold_in(key, 22)
    first_key, second_key = jax.random.split(key)
    block_shape = (CELLS, BLOCK, BLOCK)
    entries = jax.random.normal(first_key, block_shape, jnp.float32)
    return symmetric_blocks(entries, second_key, 1.0, 3.0, 0.45)


def draw_left_root(key, part):
    key = jax.random.fold_in(key, 23)
    first_key, second_key, third_key = jax.random.split(key, 3)
    block_shape = (CELLS, BLOCK, BLOCK)
    entries = jax.random.normal(first_key, block_shape, jnp.float32)
    pattern = jax.random.normal(third_key, (CELLS, BLOCK), jnp.float32)
    return symmetric_blocks(entries, second_key, 1.0, 4.0, 0.45) + coherent_part(pattern, 0.7)


def draw_right_root(key, part):
    key = jax.random.fold_in(key, 24)
    first_key, second_key, third_key = jax.random.split(key, 3)
    block_shape = (CELLS, BLOCK, BLOCK)
    entries = jax.random.normal(first_key, block_shape, jnp.float32)
    pattern = jax.random.normal(third_key, (CELLS, BLOCK), jnp.float32)
    return symmetric_blocks(entries, second_key, 1.0, 4.0, 0.45) + coherent_part(pattern, 0.7)


def setup_inputs(seed: int = 0) -> dict:
    keys = jax.random.split(jax.random.key(seed), 7)
    gradient = draw_gradient(jax.random.fold_in(keys[6], 71), 0)
    owner_map = draw_owner_map(jax.random.fold_in(keys[6], 71), 0)
    left_stats = draw_left_stats(jax.random.fold_in(keys[6], 71), 0)
    right_stats = draw_right_stats(jax.random.fold_in(keys[6], 71), 0)
    left_root = draw_left_root(jax.random.fold_in(keys[6], 71), 0)
    right_root = draw_right_root(jax.random.fold_in(keys[6], 71), 0)
    return dict(gradient=gradient, owner_map=owner_map, left_stats=left_stats, right_stats=right_stats, left_root=left_root, right_root=right_root)


decay_rate = 0.95

def cell_index(owner_map, capacity):
    total_rows = owner_map.shape[0]
    positions = jnp.arange(total_rows, dtype=jnp.int32)
    same_owner = owner_map[None, :] == owner_map[:, None]
    earlier = positions[None, :] < positions[:, None]
    ranks = lax.optimization_barrier(jnp.sum((same_owner & earlier).astype(jnp.int32), axis=1)).astype(jnp.int32)
    return (owner_map * capacity + ranks).astype(jnp.int32)

def reference(gradient, owner_map, left_stats, right_stats, left_root, right_root):
    cell_ids = cell_index(owner_map, SLOTS)
    highest = lax.Precision.HIGHEST

    def precondition(block_id):
        target = cell_ids[block_id]
        matrix = gradient[block_id]
        left_term = jnp.dot(matrix, matrix.T, preferred_element_type=jnp.float32)
        right_term = jnp.dot(matrix.T, matrix, preferred_element_type=jnp.float32)
        left_next = decay_rate * left_stats[target] + (1.0 - decay_rate) / BLOCK * left_term
        right_next = decay_rate * right_stats[target] + (1.0 - decay_rate) / BLOCK * right_term
        widened = matrix.astype(jnp.float32)
        inner = jnp.dot(left_root[target], widened, precision=highest)
        result = jnp.dot(inner, right_root[target], precision=highest)
        return (left_next, right_next, result)
    left_all, right_all, results = lax.map(precondition, jnp.arange(BLOCKS, dtype=jnp.int32))
    left_new = left_stats.at[cell_ids].set(left_all)
    right_new = right_stats.at[cell_ids].set(right_all)
    grad_squares = lax.optimization_barrier(jnp.sum(jnp.square(gradient.astype(jnp.float32)), axis=(1, 2)))
    result_squares = lax.optimization_barrier(jnp.sum(jnp.square(results), axis=(1, 2)))
    half_count = BLOCKS // 2
    gate_scale = jnp.sqrt(jnp.sum(grad_squares[:half_count]) / jnp.sum(result_squares[:half_count]))
    up_scale = jnp.sqrt(jnp.sum(grad_squares[half_count:]) / jnp.sum(result_squares[half_count:]))
    up_block = jnp.arange(BLOCKS, dtype=jnp.int32) >= half_count
    scales = jnp.where(up_block, up_scale, gate_scale)
    update = (results * scales[:, None, None]).astype(jnp.bfloat16)
    return (update, left_new, right_new)
```

```python
import jax
import jax.numpy as jnp
from jax import lax
from jax.sharding import PartitionSpec as P

decay_rate = 0.95
code_top = 32767.0


def cell_index(owner_map, capacity):
    total_rows = owner_map.shape[0]
    positions = jnp.arange(total_rows, dtype=jnp.int32)
    same_owner = owner_map[None, :] == owner_map[:, None]
    earlier = positions[None, :] < positions[:, None]
    ranks = jnp.sum((same_owner & earlier).astype(jnp.int32), axis=1)
    return owner_map * capacity + ranks


def ring_gather(own, axis_name, split_axis):
    up = [(i, (i + 1) % 4) for i in range(4)]
    down = [(i, (i - 1) % 4) for i in range(4)]
    first, second = jnp.split(own, 2, axis=split_axis)
    prev_a = lax.ppermute(first, axis_name, up)
    next_b = lax.ppermute(second, axis_name, down)
    prev_b = lax.ppermute(second, axis_name, up)
    next_a = lax.ppermute(first, axis_name, down)
    far_a = lax.ppermute(prev_a, axis_name, up)
    far_b = lax.ppermute(next_b, axis_name, down)
    join = lambda a, b: jnp.concatenate([a, b], axis=split_axis)
    return [own, join(next_a, next_b), join(far_a, far_b), join(prev_a, prev_b)]


def direct_gather(own, axis_name):
    shift = lambda k: lax.ppermute(own, axis_name, [(i, (i - k) % 4) for i in range(4)])
    return [own, shift(1), shift(2), shift(3)]


def rolled(array, start, axis):
    twice = jnp.concatenate([array, array], axis=axis)
    return lax.dynamic_slice_in_dim(twice, start, array.shape[axis], axis)


def fsdp_shift(delta, stride, size):
    pairs = []
    for i in range(128):
        place = i // stride % size
        pairs.append((i, i + ((place + delta) % size - place) * stride))
    return pairs


def part_gather(array, stride, size):
    place = lax.axis_index("fsdp") // stride % size
    got = [array]
    for delta in range(1, size):
        got.append(lax.ppermute(array, "fsdp", fsdp_shift(-delta, stride, size)))
    return rolled(jnp.stack(got), (size - place) % size, 0)


def split_two(array):
    high = lax.reduce_precision(array, 8, 7)
    return high.astype(jnp.bfloat16), (array - high).astype(jnp.bfloat16)


def dot32(spec, a, b):
    return jnp.einsum(spec, a, b, preferred_element_type=jnp.float32)


def on_device(gradient, owner_map, left_stats, right_stats, left_root, right_root):
    fsdp_size = lax.axis_size("fsdp")
    block_count, row_share, col_share = gradient.shape
    capacity, part_rows, block_size = left_stats.shape
    my_owner = lax.axis_index("fsdp")
    my_part = lax.axis_index("mp")
    row_start = my_part * part_rows
    left_parts = direct_gather(left_root, "mp")

    cell_ids = cell_index(owner_map, capacity)
    cell_count = fsdp_size * capacity
    one_hot = cell_ids[None, :] == jnp.arange(cell_count, dtype=jnp.int32)[:, None]
    flat_grad = gradient.reshape(block_count, row_share * col_share)
    packed = jnp.dot(
        one_hot.astype(jnp.bfloat16), flat_grad, preferred_element_type=jnp.float32
    ).astype(jnp.bfloat16)
    packed = packed.reshape(cell_count, row_share, col_share)
    owned = lax.all_to_all(packed, "fsdp", split_axis=0, concat_axis=1, tiled=True)

    up_block = jnp.arange(block_count, dtype=jnp.int32) >= block_count // 2
    my_cells = my_owner * capacity + jnp.arange(capacity, dtype=jnp.int32)
    holding = cell_ids[None, :] == my_cells[:, None]
    occupied = jnp.any(holding, axis=1)
    cell_up = jnp.any(holding & up_block[None, :], axis=1)

    turned = jnp.concatenate(ring_gather(owned, "mp", 1), axis=2)
    right_high, right_low = split_two(rolled(right_root, row_start, 2))
    half = dot32("sij,skj->sik", turned, right_high) + dot32("sij,skj->sik", turned, right_low)
    half_high, half_low = split_two(half)
    left_high, left_low = split_two(jnp.concatenate(left_parts, axis=1))
    result = (
        dot32("ski,sij->skj", left_high, half_high)
        + dot32("ski,sij->skj", left_high, half_low)
        + dot32("ski,sij->skj", left_low, half_high)
    )
    result = rolled(result, block_size - row_start, 1)
    result = jnp.where(occupied[:, None, None], result, 0.0)

    top = jnp.maximum(jnp.max(jnp.abs(result), axis=(1, 2)), 1e-30)
    root = jnp.sqrt(jnp.abs(result) * (code_top * code_top / top)[:, None, None])
    code = jnp.round(jnp.where(result < 0, -root, root)).astype(jnp.int16)

    upd_terms = jnp.sum(jnp.square(result), axis=(1, 2))
    owned_terms = jnp.sum(jnp.square(owned.astype(jnp.float32)), axis=(1, 2))
    owned_terms = jnp.where(occupied, owned_terms, 0.0)
    sums = jnp.stack(
        [
            jnp.sum(jnp.where(cell_up, 0.0, owned_terms)),
            jnp.sum(jnp.where(cell_up, owned_terms, 0.0)),
            jnp.sum(jnp.where(cell_up, 0.0, upd_terms)),
            jnp.sum(jnp.where(cell_up, upd_terms, 0.0)),
        ]
    )
    sums = sum(direct_gather(sums, "mp"))
    facts = jnp.concatenate([sums, top, jnp.zeros((1,), jnp.float32)])
    all_facts = part_gather(part_gather(facts, 1, 8), 8, 16)
    all_facts = all_facts.reshape(fsdp_size, 8)

    message = code.reshape(capacity, fsdp_size, row_share, col_share)
    arrived = lax.all_to_all(message, "fsdp", split_axis=1, concat_axis=1, tiled=True)

    top_rows = lax.dynamic_slice_in_dim(turned, row_start, part_rows, 1)
    left_acc = dot32("skc,sjc->skj", top_rows, turned)
    right_acc = rolled(dot32("sik,sij->skj", owned, turned), block_size - row_start, 2)
    scaled_gain = (1.0 - decay_rate) / block_size
    filled = occupied[:, None, None]
    left_new = jnp.where(filled, decay_rate * left_stats + scaled_gain * left_acc, left_stats)
    right_new = jnp.where(filled, decay_rate * right_stats + scaled_gain * right_acc, right_stats)

    sums = jnp.sum(all_facts[:, :4], axis=0)
    gate_scale = jnp.sqrt(sums[0] / sums[2])
    up_scale = jnp.sqrt(sums[1] / sums[3])
    my_tops = all_facts[:, 4 : 4 + capacity].reshape(cell_count)
    code_step = my_tops[cell_ids] / (code_top * code_top)

    slot = cell_ids % capacity
    picked = arrived[slot, cell_ids // capacity].astype(jnp.float32)
    returned = picked * jnp.abs(picked) * code_step[:, None, None]
    scales = jnp.where(up_block, up_scale, gate_scale)
    update = (returned * scales[:, None, None]).astype(jnp.bfloat16)
    return (update, left_new, right_new)


def solution(mesh):
    placed = (
        P(None, "fsdp", "mp"),
        P(),
        P("fsdp", "mp", None),
        P("fsdp", "mp", None),
        P("fsdp", "mp", None),
        P("fsdp", "mp", None),
    )
    return jax.shard_map(
        on_device,
        mesh=mesh,
        in_specs=placed,
        out_specs=(P(None, "fsdp", "mp"), P("fsdp", "mp", None), P("fsdp", "mp", None)),
        check_vma=False,
    )
```

```python
import functools

import jax
import jax.numpy as jnp
from jax import lax
from jax.experimental import pallas as pl
from jax.experimental.pallas import tpu as pltpu
from jax.sharding import PartitionSpec as P

decay_rate = 0.95
code_top = 32767.0
parts = 4
near = 8
far = 16


def cell_index(owner_map, capacity):
    total_rows = owner_map.shape[0]
    positions = jnp.arange(total_rows, dtype=jnp.int32)
    same_owner = owner_map[None, :] == owner_map[:, None]
    earlier = positions[None, :] < positions[:, None]
    ranks = jnp.sum((same_owner & earlier).astype(jnp.int32), axis=1)
    return owner_map * capacity + ranks


far_groups = [[z * near + n for z in range(far)] for n in range(near)]
plane_groups = [[(z * near + n) * parts + m for n in range(near) for m in range(parts)] for z in range(far)]


def exchange(array, axis_name, groups):
    return lax.all_to_all(
        array, axis_name, split_axis=0, concat_axis=0, axis_index_groups=groups, tiled=True
    )


def dot32(spec, a, b):
    return jnp.einsum(spec, a, b, preferred_element_type=jnp.float32)


def split_two(array):
    high = array.astype(jnp.bfloat16)
    return high, (array - high.astype(jnp.float32)).astype(jnp.bfloat16)


def roots_kernel(
    part_ref, left_ref, own_ref, one_ref, two_ref, three_ref,
    left_high_ref, left_low_ref, right_high_ref, right_low_ref,
):
    part = part_ref[0]
    width = own_ref.shape[1]

    def span(step):
        at = lax.rem(part + step, parts)
        return pl.ds(pl.multiple_of(at * width, width), width)

    def put(row, col, block):
        high, low = split_two(block)
        right_high_ref[0, span(row), span(col)] = high
        right_low_ref[0, span(row), span(col)] = low

    def put_pair(row, col, block):
        put(row, col, block)
        put(col, row, block.T)

    put(0, 0, own_ref[0, :, span(0)])
    for step in range(1, parts):
        put_pair(0, step, own_ref[0, :, span(step)])
    put(1, 1, one_ref[0, :, :width])
    put_pair(1, 3, one_ref[0, :, width:])
    put(2, 2, two_ref[0, :, :width])
    put_pair(2, 1, two_ref[0, :, width:])
    put(3, 3, three_ref[0, :, :width])
    put_pair(3, 2, three_ref[0, :, width:])
    left_high_ref[0], left_low_ref[0] = split_two(left_ref[0].T)


def spread_roots(part, left_root, right_root, others):
    slots, width, order = right_root.shape
    by_slot = lambda *shape: pl.BlockSpec((1,) + shape, lambda s, *_: (s, 0, 0))
    of = lambda *shape: jax.ShapeDtypeStruct((slots,) + shape, jnp.bfloat16)
    return pl.pallas_call(
        roots_kernel,
        grid_spec=pltpu.PrefetchScalarGridSpec(
            num_scalar_prefetch=1,
            grid=(slots,),
            in_specs=[by_slot(width, order)] * 2 + [by_slot(width, 2 * width)] * 3,
            out_specs=[by_slot(order, width)] * 2 + [by_slot(order, order)] * 2,
        ),
        out_shape=[of(order, width)] * 2 + [of(order, order)] * 2,
        compiler_params=pltpu.CompilerParams(vmem_limit_bytes=32 * 1024 * 1024),
        cost_estimate=pl.CostEstimate(flops=0, bytes_accessed=8 * 1024 * 1024, transcendentals=0),
    )(part.reshape(1), left_root, right_root, *others)


def power(exponent):
    half = jnp.floor(exponent * 0.5)
    return jnp.exp2(half), jnp.exp2(exponent - half)


def coded(value):
    value = jnp.maximum(value, 1e-37)
    exponent = jnp.floor(jnp.log2(value)) + 1.0
    one, two = power(-exponent)
    share = value * one * two * 16384.0
    high = jnp.floor(share)
    return exponent, high, jnp.floor((share - high) * 16384.0)


def decoded(exponent, high, low):
    one, two = power(exponent - 14.0)
    return jnp.where(high > 0, (high + low * (1.0 / 16384.0)) * one * two, 0.0)


def precondition_kernel(
    place_ref, taken_ref, grad_ref, left_high_ref, left_low_ref, right_high_ref, right_low_ref,
    message_ref, line_ref,
):
    slot = pl.program_id(0)
    tn = (((0,), (0,)), ((), ()))
    nn = (((1,), (0,)), ((), ()))
    dot = functools.partial(lax.dot_general, preferred_element_type=jnp.float32)
    order = left_high_ref.shape[1]
    grad = jnp.concatenate([grad_ref[:, m].reshape(order, -1) for m in range(parts)], axis=1)
    half = dot(left_high_ref[0], grad, tn) + dot(left_low_ref[0], grad, tn)
    half_high, half_low = split_two(half)
    right_high = right_high_ref[0]
    result = dot(half_high, right_high, nn) + dot(half_low, right_high, nn) + dot(half_high, right_low_ref[0], nn)
    taken = taken_ref[slot]
    result = jnp.where(taken > 0, result, 0.0)
    size = jnp.abs(result)
    top = jnp.maximum(jnp.max(size), 1e-30)
    root = jnp.sqrt(size * (code_top * code_top / top))
    code = jnp.round(jnp.where(result < 0, -root, root)).astype(jnp.int32)
    wide_rows, deep = message_ref.shape[3], message_ref.shape[2]
    for step in range(far // parts):
        for device in range(near):
            for m in range(parts):
                row = (step * near + device) * deep
                message_ref[device * parts + m, step * 3 + slot] = code[
                    row : row + deep, m * wide_rows : (m + 1) * wide_rows
                ].astype(jnp.int16)

    wide = grad.astype(jnp.float32)
    grad_sum = jnp.where(taken > 0, jnp.sum(wide * wide), 0.0) * (1.0 / parts)
    upd_sum = jnp.sum(result * result)

    @pl.when(slot == 0)
    def _():
        line_ref[...] = jnp.zeros_like(line_ref)

    lane = lax.broadcasted_iota(jnp.int32, (8, 128), 1)
    at = lane - place_ref[0] * 16
    sum_at = at - place_ref[1] * 4
    is_up = jnp.where(taken > 1, 1, 0)
    line_ref[0] += jnp.where(sum_at == is_up, grad_sum, 0.0) + jnp.where(sum_at == 2 + is_up, upd_sum, 0.0)
    line_ref[1] += jnp.where((at >= 3 * slot) & (at < 3 * slot + 3), top, 0.0)

    @pl.when(slot == pl.num_programs(0) - 1)
    def _():
        row = lax.broadcasted_iota(jnp.int32, (8, 128), 0)
        in_sums = (sum_at >= 0) & (sum_at < 4)
        in_tops = (at >= 0) & (at < 9)
        exponent, high, low = coded(line_ref[0])
        sums = jnp.where(in_sums, jnp.where(row == 0, exponent, jnp.where(row == 1, high, low)), 0.0)
        exponent, high, low = coded(line_ref[1])
        step = at - 3 * jnp.where(at >= 6, 2, jnp.where(at >= 3, 1, 0))
        tops = jnp.where(in_tops, jnp.where(step == 0, exponent, jnp.where(step == 1, high, low)), 0.0)
        facts = jnp.where(row < 3, sums, tops)[:deep].astype(jnp.int32).astype(jnp.int16)
        for device in range(near * parts):
            message_ref[device, message_ref.shape[1] - 1] = facts


def precondition(place, taken, landed, roots):
    slots, width = taken.shape[0], landed.shape[2]
    rows = landed.shape[1] // slots
    order = near * rows
    message = (near * parts, slots * far // parts + 1, rows // far, width)
    by_slot = lambda *shape: pl.BlockSpec((1,) + shape, lambda s, *_: (s, 0, 0))
    return pl.pallas_call(
        precondition_kernel,
        grid_spec=pltpu.PrefetchScalarGridSpec(
            num_scalar_prefetch=2,
            grid=(slots,),
            in_specs=[pl.BlockSpec((near, parts, rows, width), lambda s, *_: (0, 0, s, 0))]
            + [by_slot(order, width)] * 2
            + [by_slot(order, order)] * 2,
            out_specs=pl.BlockSpec(message, lambda s, *_: (0, 0, 0, 0)),
            scratch_shapes=[pltpu.VMEM((2, 8, 128), jnp.float32)],
        ),
        out_shape=jax.ShapeDtypeStruct(message, jnp.int16),
        compiler_params=pltpu.CompilerParams(vmem_limit_bytes=32 * 1024 * 1024),
        cost_estimate=pl.CostEstimate(
            flops=10 * slots * order * order * width, bytes_accessed=6 * 1024 * 1024, transcendentals=0
        ),
    )(place, taken, landed.reshape(near, parts, slots * rows, width), *roots)


def repack_kernel(back_ref, ahead_ref):
    cells = ahead_ref.shape[1] - 1
    slots = cells // near
    last = back_ref.shape[1] - 1
    for m in range(parts):
        for step in range(far // parts):
            for device in range(near):
                ahead_ref[m * (far // parts) + step, device * slots : (device + 1) * slots] = back_ref[
                    device * parts + m, step * slots : (step + 1) * slots
                ]
    wide = lambda device, m: back_ref[device * parts + m, last].astype(jnp.int32)
    by_part = [functools.reduce(jnp.add, [wide(device, m) for device in range(near)]) for m in range(parts)]
    plane = functools.reduce(jnp.add, by_part)
    row = lax.broadcasted_iota(jnp.int32, plane.shape, 0)
    for m in range(parts):
        facts = jnp.where(row < 3, plane, by_part[m]).astype(jnp.int16)
        for step in range(far // parts):
            ahead_ref[m * (far // parts) + step, cells] = facts


def repack(back):
    slots = (back.shape[1] - 1) // (far // parts)
    return pl.pallas_call(
        repack_kernel,
        out_shape=jax.ShapeDtypeStruct((far, near * slots + 1) + back.shape[2:], back.dtype),
        in_specs=[pl.BlockSpec(memory_space=pltpu.VMEM)],
        out_specs=pl.BlockSpec(memory_space=pltpu.VMEM),
        compiler_params=pltpu.CompilerParams(vmem_limit_bytes=16 * 1024 * 1024),
        cost_estimate=pl.CostEstimate(flops=0, bytes_accessed=1 << 20, transcendentals=0),
    )(back)


def finish_kernel(at_ref, spot_ref, up_ref, arrived_ref, update_ref, factor_ref):
    cells = arrived_ref.shape[1] - 1
    facts = [arrived_ref[z, cells].astype(jnp.int32).astype(jnp.float32) for z in range(far)]
    row = lambda r: jnp.concatenate([fact[r : r + 1] for fact in facts], axis=0)
    sums = jnp.sum(decoded(row(0), row(1), row(2)), axis=0, keepdims=True)
    kind = lax.rem(lax.broadcasted_iota(jnp.int32, sums.shape, 1), 4)
    total = lambda k: jnp.sum(jnp.where(kind == k, sums, 0.0), axis=1, keepdims=True)
    gate_scale = jnp.sqrt(total(0) / total(2))
    up_scale = jnp.sqrt(total(1) / total(3))
    tops = row(3)
    lanes = tops.shape[1]
    steps = decoded(tops, pltpu.roll(tops, lanes - 1, 1), pltpu.roll(tops, lanes - 2, 1))
    steps = steps * (1.0 / (code_top * code_top))
    spot = spot_ref[...]
    lane = lax.broadcasted_iota(jnp.int32, spot.shape, 1)
    mine = jnp.zeros(spot.shape, jnp.float32)
    for z in range(far):
        mine += jnp.where(spot == lane + z * lanes, steps[z : z + 1], 0.0)
    step = jnp.sum(mine, axis=1, keepdims=True)
    factor_ref[...] = jnp.where(up_ref[...] > 0, up_scale, gate_scale) * step

    for b in range(update_ref.shape[0]):
        at = at_ref[b]
        code = arrived_ref[at // cells, lax.rem(at, cells)].astype(jnp.int32).astype(jnp.float32)
        update_ref[b] = (code * jnp.abs(code) * factor_ref[b : b + 1, :]).astype(jnp.bfloat16)


def finish(cell_ids, spot, up, arrived):
    blocks = cell_ids.shape[0]
    whole = lambda shape: pl.BlockSpec(shape, lambda i, *_: (0,) * len(shape))
    return pl.pallas_call(
        finish_kernel,
        grid_spec=pltpu.PrefetchScalarGridSpec(
            num_scalar_prefetch=1,
            grid=(1,),
            in_specs=[whole(spot.shape), whole(up.shape), whole(arrived.shape)],
            out_specs=whole((blocks,) + arrived.shape[2:]),
            scratch_shapes=[pltpu.VMEM((blocks, arrived.shape[3]), jnp.float32)],
        ),
        out_shape=jax.ShapeDtypeStruct((blocks,) + arrived.shape[2:], jnp.bfloat16),
        compiler_params=pltpu.CompilerParams(vmem_limit_bytes=16 * 1024 * 1024),
        cost_estimate=pl.CostEstimate(flops=0, bytes_accessed=1 << 20, transcendentals=0),
    )(cell_ids, spot, up, arrived)


def on_device(gradient, owner_map, left_stats, right_stats, left_root, right_root):
    fsdp_size = lax.axis_size("fsdp")
    block_count, row_share, col_share = gradient.shape
    capacity, part_rows, block_size = left_stats.shape
    my_owner = lax.axis_index("fsdp")
    my_part = lax.axis_index("mp")
    row_start = my_part * part_rows
    cell_count = fsdp_size * capacity

    cell_ids = cell_index(owner_map, capacity)
    one_hot = cell_ids[None, :] == jnp.arange(cell_count, dtype=jnp.int32)[:, None]
    flat_grad = gradient.reshape(block_count, row_share * col_share)
    packed = jnp.dot(
        one_hot.astype(jnp.bfloat16), flat_grad, preferred_element_type=jnp.float32
    ).astype(jnp.bfloat16)
    packed = packed.reshape(far, near, capacity, row_share, col_share)
    in_plane = exchange(packed, "fsdp", far_groups)

    def column(step):
        start = (my_part + step) % parts * part_rows
        return lax.dynamic_slice_in_dim(right_root, start, part_rows, 2)

    pair = lambda step: jnp.concatenate([column(0), column(step)], axis=2)
    send = lambda array, k: lax.ppermute(array, "mp", [(i, (i + k) % parts) for i in range(parts)])
    three = send(pair(3), 1)
    two = send(pair(3), 2)
    one = send(pair(2), 3)
    in_plane, one, two, three = lax.optimization_barrier((in_plane, one, two, three))

    fanned = jnp.broadcast_to(
        in_plane.transpose(1, 2, 0, 3, 4)[:, None], (near, parts, capacity, far, row_share, col_share)
    ).reshape(near * parts, capacity * far * row_share, col_share)
    landed = exchange(fanned, ("fsdp", "mp"), plane_groups)

    up_block = jnp.arange(block_count, dtype=jnp.int32) >= block_count // 2
    my_cells = my_owner * capacity + jnp.arange(capacity, dtype=jnp.int32)
    holding = cell_ids[None, :] == my_cells[:, None]
    taken = jnp.max(jnp.where(holding, 1 + up_block.astype(jnp.int32)[None, :], 0), axis=1)

    left_high, left_low, right_high, right_low = spread_roots(my_part, left_root, right_root, (one, two, three))

    def landed_order(array):
        split = array.reshape(capacity, far, near, row_share, part_rows)
        return jnp.swapaxes(split, 1, 2).reshape(capacity, block_size, part_rows)

    place = jnp.stack([my_owner % near, my_part])
    message = precondition(
        place, taken, landed, (landed_order(left_high), landed_order(left_low), right_high, right_low)
    )
    landed, message = lax.optimization_barrier((landed, message))
    back = exchange(message, ("fsdp", "mp"), plane_groups)
    arrived = exchange(repack(back), "fsdp", far_groups)

    landed = landed.reshape(near, parts, capacity, far, row_share, col_share)
    blocks = landed.transpose(2, 3, 0, 4, 1, 5).reshape(capacity, block_size, block_size)
    top_rows = lax.dynamic_slice_in_dim(blocks, row_start, part_rows, 1)
    my_columns = lax.dynamic_slice_in_dim(blocks, row_start, part_rows, 2)
    left_acc = dot32("skc,sjc->skj", top_rows, blocks)
    right_acc = dot32("sik,sij->skj", my_columns, blocks)
    scaled_gain = (1.0 - decay_rate) / block_size
    filled = (taken > 0)[:, None, None]
    left_new = jnp.where(filled, decay_rate * left_stats + scaled_gain * left_acc, left_stats)
    right_new = jnp.where(filled, decay_rate * right_stats + scaled_gain * right_acc, right_stats)

    cells = near * capacity
    spot = cell_ids // cells * 128 + cell_ids % cells // capacity * 16 + cell_ids % capacity * 3
    across = lambda array: jnp.broadcast_to(array.astype(jnp.int32)[:, None], (block_count, 128))
    update = finish(cell_ids, across(spot), across(up_block), arrived)
    return (update, left_new, right_new)


def solution(mesh):
    placed = (
        P(None, "fsdp", "mp"),
        P(),
        P("fsdp", "mp", None),
        P("fsdp", "mp", None),
        P("fsdp", "mp", None),
        P("fsdp", "mp", None),
    )
    return jax.shard_map(
        on_device,
        mesh=mesh,
        in_specs=placed,
        out_specs=(P(None, "fsdp", "mp"), P("fsdp", "mp", None), P("fsdp", "mp", None)),
        check_vma=False,
    )
```

```python
import functools

import jax
import jax.numpy as jnp
from jax import lax
from jax.experimental import pallas as pl
from jax.experimental.pallas import tpu as pltpu
from jax.sharding import PartitionSpec as P

decay_rate = 0.95
code_top = 32767.0
parts = 4
near = 8
far = 16


def cell_index(owner_map, capacity):
    total_rows = owner_map.shape[0]
    positions = jnp.arange(total_rows, dtype=jnp.int32)
    same_owner = owner_map[None, :] == owner_map[:, None]
    earlier = positions[None, :] < positions[:, None]
    ranks = jnp.sum((same_owner & earlier).astype(jnp.int32), axis=1)
    return owner_map * capacity + ranks


far_groups = [[z * near + n for z in range(far)] for n in range(near)]
plane_groups = [[(z * near + n) * parts + m for n in range(near) for m in range(parts)] for z in range(far)]


def exchange(array, axis_name, groups):
    return lax.all_to_all(
        array, axis_name, split_axis=0, concat_axis=0, axis_index_groups=groups, tiled=True
    )


def dot32(spec, a, b):
    return jnp.einsum(spec, a, b, preferred_element_type=jnp.float32)


def split_two(array):
    high = array.astype(jnp.bfloat16)
    return high, (array - high.astype(jnp.float32)).astype(jnp.bfloat16)


def pack_kernel(owner_ref, grad_ref, packed_ref, count_ref):
    blocks = grad_ref.shape[0]
    slots = packed_ref.shape[0] // blocks
    packed_ref[...] = jnp.zeros_like(packed_ref)
    for owner in range(blocks):
        count_ref[owner] = 0
    for b in range(blocks):
        owner = owner_ref[b]
        rank = count_ref[owner]
        count_ref[owner] = rank + 1
        packed_ref[owner * slots + rank] = grad_ref[b]


def pack(owner_map, gradient, slots):
    blocks = gradient.shape[0]
    whole = lambda shape: pl.BlockSpec(shape, lambda i, *_: (0,) * len(shape))
    packed = (blocks * slots,) + gradient.shape[1:]
    return pl.pallas_call(
        pack_kernel,
        grid_spec=pltpu.PrefetchScalarGridSpec(
            num_scalar_prefetch=1,
            grid=(1,),
            in_specs=[whole(gradient.shape)],
            out_specs=whole(packed),
            scratch_shapes=[pltpu.SMEM((blocks,), jnp.int32)],
        ),
        out_shape=jax.ShapeDtypeStruct(packed, gradient.dtype),
        compiler_params=pltpu.CompilerParams(vmem_limit_bytes=16 * 1024 * 1024),
        cost_estimate=pl.CostEstimate(flops=0, bytes_accessed=1 << 20, transcendentals=0),
    )(owner_map, gradient)


def fan_kernel(plane_ref, fan_ref):
    for n in range(near):
        for s in range(plane_ref.shape[2]):
            rows = plane_ref[:, n, s]
            for m in range(parts):
                fan_ref[n, m, s] = rows


def fan(in_plane):
    _, _, slots, rows, width = in_plane.shape
    return pl.pallas_call(
        fan_kernel,
        out_shape=jax.ShapeDtypeStruct((near, parts, slots, far, rows, width), in_plane.dtype),
        in_specs=[pl.BlockSpec(memory_space=pltpu.VMEM)],
        out_specs=pl.BlockSpec(memory_space=pltpu.VMEM),
        compiler_params=pltpu.CompilerParams(vmem_limit_bytes=16 * 1024 * 1024),
        cost_estimate=pl.CostEstimate(flops=0, bytes_accessed=1 << 21, transcendentals=0),
    )(in_plane)


def roots_kernel(
    part_ref, left_ref, own_ref, one_ref, two_ref, three_ref,
    left_high_ref, left_low_ref, right_high_ref, right_low_ref,
):
    part = part_ref[0]
    width = own_ref.shape[1]

    def span(step):
        at = lax.rem(part + step, parts)
        return pl.ds(pl.multiple_of(at * width, width), width)

    def put(row, col, block):
        high, low = split_two(block)
        right_high_ref[0, span(row), span(col)] = high
        right_low_ref[0, span(row), span(col)] = low

    def put_pair(row, col, block):
        put(row, col, block)
        put(col, row, block.T)

    put(0, 0, own_ref[0, :, span(0)])
    for step in range(1, parts):
        put_pair(0, step, own_ref[0, :, span(step)])
    put(1, 1, one_ref[0, :, :width])
    put_pair(1, 3, one_ref[0, :, width : 2 * width])
    put_pair(1, 2, one_ref[0, :, 2 * width :])
    put(2, 2, two_ref[0])
    put(3, 3, three_ref[0, :, :width])
    put_pair(3, 2, three_ref[0, :, width:])
    left_high_ref[0], left_low_ref[0] = split_two(left_ref[0].T)


def spread_roots(part, left_root, right_root, others):
    slots, width, order = right_root.shape
    by_slot = lambda *shape: pl.BlockSpec((1,) + shape, lambda s, *_: (s, 0, 0))
    of = lambda *shape: jax.ShapeDtypeStruct((slots,) + shape, jnp.bfloat16)
    return pl.pallas_call(
        roots_kernel,
        grid_spec=pltpu.PrefetchScalarGridSpec(
            num_scalar_prefetch=1,
            grid=(slots,),
            in_specs=[by_slot(width, order)] * 2 + [by_slot(width, other.shape[2]) for other in others],
            out_specs=[by_slot(order, width)] * 2 + [by_slot(order, order)] * 2,
        ),
        out_shape=[of(order, width)] * 2 + [of(order, order)] * 2,
        compiler_params=pltpu.CompilerParams(vmem_limit_bytes=32 * 1024 * 1024),
        cost_estimate=pl.CostEstimate(flops=0, bytes_accessed=8 * 1024 * 1024, transcendentals=0),
    )(part.reshape(1), left_root, right_root, *others)


def power(exponent):
    half = jnp.floor(exponent * 0.5)
    return jnp.exp2(half), jnp.exp2(exponent - half)


def coded(value):
    value = jnp.maximum(value, 1e-37)
    exponent = jnp.floor(jnp.log2(value)) + 1.0
    one, two = power(-exponent)
    share = value * one * two * 16384.0
    high = jnp.floor(share)
    return exponent, high, jnp.floor((share - high) * 16384.0)


def decoded(exponent, high, low):
    one, two = power(exponent - 14.0)
    return jnp.where(high > 0, (high + low * (1.0 / 16384.0)) * one * two, 0.0)


def precondition_kernel(
    place_ref, taken_ref, grad_ref, left_high_ref, left_low_ref, right_high_ref, right_low_ref,
    message_ref, line_ref,
):
    slot = pl.program_id(0)
    slots = taken_ref.shape[0]
    tn = (((0,), (0,)), ((), ()))
    nn = (((1,), (0,)), ((), ()))
    dot = functools.partial(lax.dot_general, preferred_element_type=jnp.float32)
    order = left_high_ref.shape[1]
    grad = jnp.concatenate([grad_ref[:, m].reshape(order, -1) for m in range(parts)], axis=1)
    half = dot(left_high_ref[0], grad, tn) + dot(left_low_ref[0], grad, tn)
    half_high, half_low = split_two(half)
    right_high = right_high_ref[0]
    result = dot(half_high, right_high, nn) + dot(half_low, right_high, nn) + dot(half_high, right_low_ref[0], nn)
    taken = taken_ref[slot]
    result = jnp.where(taken > 0, result, 0.0)
    size = jnp.abs(result)
    top = jnp.maximum(jnp.max(size), 1e-30)
    root = jnp.sqrt(size * (code_top * code_top / top))
    code = jnp.round(jnp.where(result < 0, -root, root)).astype(jnp.int32)
    wide_rows, deep = message_ref.shape[3], message_ref.shape[2]
    for step in range(far // parts):
        for device in range(near):
            for m in range(parts):
                row = (step * near + device) * deep
                message_ref[device * parts + m, step * slots + slot] = code[
                    row : row + deep, m * wide_rows : (m + 1) * wide_rows
                ].astype(jnp.int16)

    wide = grad.astype(jnp.float32)
    grad_sum = jnp.where(taken > 0, jnp.sum(wide * wide), 0.0) * (1.0 / parts)
    upd_sum = jnp.sum(result * result)

    @pl.when(slot == 0)
    def _():
        line_ref[...] = jnp.zeros_like(line_ref)

    lane = lax.broadcasted_iota(jnp.int32, (8, 128), 1)
    at = lane - place_ref[0] * 16
    sum_at = at - place_ref[1] * 4
    is_up = jnp.where(taken > 1, 1, 0)
    line_ref[0] += jnp.where(sum_at == is_up, grad_sum, 0.0) + jnp.where(sum_at == 2 + is_up, upd_sum, 0.0)
    line_ref[1] += jnp.where((at >= 3 * slot) & (at < 3 * slot + 3), top, 0.0)

    @pl.when(slot == pl.num_programs(0) - 1)
    def _():
        row = lax.broadcasted_iota(jnp.int32, (8, 128), 0)
        in_sums = (sum_at >= 0) & (sum_at < 4)
        in_tops = (at >= 0) & (at < 9)
        exponent, high, low = coded(line_ref[0])
        sums = jnp.where(in_sums, jnp.where(row == 0, exponent, jnp.where(row == 1, high, low)), 0.0)
        exponent, high, low = coded(line_ref[1])
        step = at - 3 * jnp.where(at >= 6, 2, jnp.where(at >= 3, 1, 0))
        tops = jnp.where(in_tops, jnp.where(step == 0, exponent, jnp.where(step == 1, high, low)), 0.0)
        facts = jnp.where(row < 3, sums, tops)[:deep].astype(jnp.int32).astype(jnp.int16)
        for device in range(near * parts):
            message_ref[device, slots * far // parts] = facts


def precondition(place, taken, landed, roots):
    slots, width = taken.shape[0], landed.shape[2]
    rows = landed.shape[1] // slots
    order = near * rows
    message = (near * parts, slots * far // parts + 4, rows // far, width)
    by_slot = lambda *shape: pl.BlockSpec((1,) + shape, lambda s, *_: (s, 0, 0))
    return pl.pallas_call(
        precondition_kernel,
        grid_spec=pltpu.PrefetchScalarGridSpec(
            num_scalar_prefetch=2,
            grid=(slots,),
            in_specs=[pl.BlockSpec((near, parts, rows, width), lambda s, *_: (0, 0, s, 0))]
            + [by_slot(order, width)] * 2
            + [by_slot(order, order)] * 2,
            out_specs=pl.BlockSpec(message, lambda s, *_: (0, 0, 0, 0)),
            scratch_shapes=[pltpu.VMEM((2, 8, 128), jnp.float32)],
        ),
        out_shape=jax.ShapeDtypeStruct(message, jnp.int16),
        compiler_params=pltpu.CompilerParams(vmem_limit_bytes=32 * 1024 * 1024),
        cost_estimate=pl.CostEstimate(
            flops=10 * slots * order * order * width, bytes_accessed=6 * 1024 * 1024, transcendentals=0
        ),
    )(place, taken, landed.reshape(near, parts, slots * rows, width), *roots)


def repack_kernel(back_ref, ahead_ref):
    cells = ahead_ref.shape[1] - 4
    slots = cells // near
    last = back_ref.shape[1] - 4
    for m in range(parts):
        for step in range(far // parts):
            for device in range(near):
                ahead_ref[m * (far // parts) + step, device * slots : (device + 1) * slots] = back_ref[
                    device * parts + m, step * slots : (step + 1) * slots
                ]
    wide = lambda device, m: back_ref[device * parts + m, last].astype(jnp.int32)
    by_part = [functools.reduce(jnp.add, [wide(device, m) for device in range(near)]) for m in range(parts)]
    plane = functools.reduce(jnp.add, by_part)
    row = lax.broadcasted_iota(jnp.int32, plane.shape, 0)
    for m in range(parts):
        facts = jnp.where(row < 3, plane, by_part[m]).astype(jnp.int16)
        for step in range(far // parts):
            ahead_ref[m * (far // parts) + step, cells] = facts


def repack(back):
    slots = (back.shape[1] - 4) // (far // parts)
    return pl.pallas_call(
        repack_kernel,
        out_shape=jax.ShapeDtypeStruct((far, near * slots + 4) + back.shape[2:], back.dtype),
        in_specs=[pl.BlockSpec(memory_space=pltpu.VMEM)],
        out_specs=pl.BlockSpec(memory_space=pltpu.VMEM),
        compiler_params=pltpu.CompilerParams(vmem_limit_bytes=16 * 1024 * 1024),
        cost_estimate=pl.CostEstimate(flops=0, bytes_accessed=1 << 20, transcendentals=0),
    )(back)


def finish_kernel(at_ref, spot_ref, up_ref, arrived_ref, update_ref, factor_ref):
    cells = arrived_ref.shape[1] - 4
    facts = [arrived_ref[z, cells].astype(jnp.int32).astype(jnp.float32) for z in range(far)]
    row = lambda r: jnp.concatenate([fact[r : r + 1] for fact in facts], axis=0)
    sums = jnp.sum(decoded(row(0), row(1), row(2)), axis=0, keepdims=True)
    kind = lax.rem(lax.broadcasted_iota(jnp.int32, sums.shape, 1), 4)
    total = lambda k: jnp.sum(jnp.where(kind == k, sums, 0.0), axis=1, keepdims=True)
    gate_scale = jnp.sqrt(total(0) / total(2))
    up_scale = jnp.sqrt(total(1) / total(3))
    tops = row(3)
    lanes = tops.shape[1]
    steps = decoded(tops, pltpu.roll(tops, lanes - 1, 1), pltpu.roll(tops, lanes - 2, 1))
    steps = steps * (1.0 / (code_top * code_top))
    spot = spot_ref[...]
    lane = lax.broadcasted_iota(jnp.int32, spot.shape, 1)
    mine = jnp.zeros(spot.shape, jnp.float32)
    for z in range(far):
        mine += jnp.where(spot == lane + z * lanes, steps[z : z + 1], 0.0)
    step = jnp.sum(mine, axis=1, keepdims=True)
    factor_ref[...] = jnp.where(up_ref[...] > 0, up_scale, gate_scale) * step

    for b in range(update_ref.shape[0]):
        at = at_ref[b]
        code = arrived_ref[at // cells, lax.rem(at, cells)].astype(jnp.int32).astype(jnp.float32)
        update_ref[b] = (code * jnp.abs(code) * factor_ref[b : b + 1, :]).astype(jnp.bfloat16)


def finish(cell_ids, spot, up, arrived):
    blocks = cell_ids.shape[0]
    whole = lambda shape: pl.BlockSpec(shape, lambda i, *_: (0,) * len(shape))
    return pl.pallas_call(
        finish_kernel,
        grid_spec=pltpu.PrefetchScalarGridSpec(
            num_scalar_prefetch=1,
            grid=(1,),
            in_specs=[whole(spot.shape), whole(up.shape), whole(arrived.shape)],
            out_specs=whole((blocks,) + arrived.shape[2:]),
            scratch_shapes=[pltpu.VMEM((blocks, arrived.shape[3]), jnp.float32)],
        ),
        out_shape=jax.ShapeDtypeStruct((blocks,) + arrived.shape[2:], jnp.bfloat16),
        compiler_params=pltpu.CompilerParams(vmem_limit_bytes=16 * 1024 * 1024),
        cost_estimate=pl.CostEstimate(flops=0, bytes_accessed=1 << 20, transcendentals=0),
    )(cell_ids, spot, up, arrived)


def on_device(gradient, owner_map, left_stats, right_stats, left_root, right_root):
    block_count, row_share, col_share = gradient.shape
    capacity, part_rows, block_size = left_stats.shape
    my_owner = lax.axis_index("fsdp")
    my_part = lax.axis_index("mp")
    row_start = my_part * part_rows

    packed = pack(owner_map, gradient, capacity).reshape(far, near, capacity, row_share, col_share)
    in_plane = exchange(packed, "fsdp", far_groups)

    def column(step):
        start = (my_part + step) % parts * part_rows
        return lax.dynamic_slice_in_dim(right_root, start, part_rows, 2)

    some = lambda *steps: jnp.concatenate([column(step) for step in steps], axis=2)
    send = lambda array, k: lax.ppermute(array, "mp", [(i, (i + k) % parts) for i in range(parts)])
    three = send(some(0, 3), 1)
    two = send(column(0), 2)
    one = send(some(0, 2, 1), 3)
    in_plane, one, two, three, owner_map = lax.optimization_barrier((in_plane, one, two, three, owner_map))

    fanned = fan(in_plane).reshape(near * parts, capacity * far * row_share, col_share)
    landed = exchange(fanned, ("fsdp", "mp"), plane_groups)

    cell_ids = cell_index(owner_map, capacity)
    up_block = jnp.arange(block_count, dtype=jnp.int32) >= block_count // 2
    my_cells = my_owner * capacity + jnp.arange(capacity, dtype=jnp.int32)
    holding = cell_ids[None, :] == my_cells[:, None]
    taken = jnp.max(jnp.where(holding, 1 + up_block.astype(jnp.int32)[None, :], 0), axis=1)

    left_high, left_low, *right_pair = spread_roots(my_part, left_root, right_root, (one, two, three))

    def landed_order(array):
        split = array.reshape(capacity, far, near, row_share, part_rows)
        return jnp.swapaxes(split, 1, 2).reshape(capacity, block_size, part_rows)

    place = jnp.stack([my_owner % near, my_part])
    right_high, right_low = (pltpu.with_memory_space_constraint(x, pltpu.HBM) for x in right_pair)
    message = precondition(
        place, taken, landed, (landed_order(left_high), landed_order(left_low), right_high, right_low)
    )
    landed, message = lax.optimization_barrier((landed, message))
    back = exchange(message, ("fsdp", "mp"), plane_groups)
    arrived = exchange(repack(back), "fsdp", far_groups)

    landed = landed.reshape(near, parts, capacity, far, row_share, col_share)
    blocks = landed.transpose(2, 3, 0, 4, 1, 5).reshape(capacity, block_size, block_size)
    top_rows = lax.dynamic_slice_in_dim(blocks, row_start, part_rows, 1)
    my_columns = lax.dynamic_slice_in_dim(blocks, row_start, part_rows, 2)
    left_acc = dot32("skc,sjc->skj", top_rows, blocks)
    right_acc = dot32("sik,sij->skj", my_columns, blocks)
    scaled_gain = (1.0 - decay_rate) / block_size
    filled = (taken > 0)[:, None, None]
    left_new = jnp.where(filled, decay_rate * left_stats + scaled_gain * left_acc, left_stats)
    right_new = jnp.where(filled, decay_rate * right_stats + scaled_gain * right_acc, right_stats)

    cells = near * capacity
    spot = cell_ids // cells * 128 + cell_ids % cells // capacity * 16 + cell_ids % capacity * 3
    across = lambda array: jnp.broadcast_to(array.astype(jnp.int32)[:, None], (block_count, 128))
    update = finish(cell_ids, across(spot), across(up_block), arrived)
    return (update, left_new, right_new)


def solution(mesh):
    placed = (
        P(None, "fsdp", "mp"),
        P(),
        P("fsdp", "mp", None),
        P("fsdp", "mp", None),
        P("fsdp", "mp", None),
        P("fsdp", "mp", None),
    )
    return jax.shard_map(
        on_device,
        mesh=mesh,
        in_specs=placed,
        out_specs=(P(None, "fsdp", "mp"), P("fsdp", "mp", None), P("fsdp", "mp", None)),
        check_vma=False,
    )
```

```python
import functools

import jax
import jax.numpy as jnp
from jax import lax
from jax.experimental import pallas as pl
from jax.experimental.pallas import tpu as pltpu
from jax.sharding import PartitionSpec as P

decay_rate = 0.95
code_top = 32767.0
parts = 4
near = 8
far = 16


def cell_index(owner_map, capacity):
    total_rows = owner_map.shape[0]
    positions = jnp.arange(total_rows, dtype=jnp.int32)
    same_owner = owner_map[None, :] == owner_map[:, None]
    earlier = positions[None, :] < positions[:, None]
    ranks = jnp.sum((same_owner & earlier).astype(jnp.int32), axis=1)
    return owner_map * capacity + ranks


far_groups = [[z * near + n for z in range(far)] for n in range(near)]
plane_groups = [[(z * near + n) * parts + m for n in range(near) for m in range(parts)] for z in range(far)]


def exchange(array, axis_name, groups):
    return lax.all_to_all(
        array, axis_name, split_axis=0, concat_axis=0, axis_index_groups=groups, tiled=True
    )


def split_two(array):
    high = array.astype(jnp.bfloat16)
    return high, (array - high.astype(jnp.float32)).astype(jnp.bfloat16)


def pack_kernel(owner_ref, grad_ref, packed_ref, count_ref):
    blocks = grad_ref.shape[0]
    slots = packed_ref.shape[0] // blocks
    packed_ref[...] = jnp.zeros_like(packed_ref)
    for owner in range(blocks):
        count_ref[owner] = 0
    for b in range(blocks):
        owner = owner_ref[b]
        rank = count_ref[owner]
        count_ref[owner] = rank + 1
        packed_ref[owner * slots + rank] = grad_ref[b]


def pack(owner_map, gradient, slots):
    blocks = gradient.shape[0]
    packed = (blocks * slots,) + gradient.shape[1:]
    return pl.pallas_call(
        pack_kernel,
        grid_spec=pltpu.PrefetchScalarGridSpec(
            num_scalar_prefetch=1,
            grid=(1,),
            in_specs=[whole(gradient.shape)],
            out_specs=whole(packed),
            scratch_shapes=[pltpu.SMEM((blocks,), jnp.int32)],
        ),
        out_shape=jax.ShapeDtypeStruct(packed, gradient.dtype),
        compiler_params=pltpu.CompilerParams(vmem_limit_bytes=16 * 1024 * 1024),
        cost_estimate=pl.CostEstimate(flops=0, bytes_accessed=1 << 20, transcendentals=0),
    )(owner_map, gradient)


def fan_kernel(plane_ref, fan_ref):
    for n in range(near):
        for slot in range(parts):
            if slot < plane_ref.shape[2]:
                fan_ref[n, slot] = plane_ref[:, n, slot]
            else:
                fan_ref[n, slot] = jnp.zeros(fan_ref.shape[2:], fan_ref.dtype)


def fan(in_plane):
    _, _, slots, rows, width = in_plane.shape
    return pl.pallas_call(
        fan_kernel,
        out_shape=jax.ShapeDtypeStruct((near, parts, far, rows, width), in_plane.dtype),
        in_specs=[pl.BlockSpec(memory_space=pltpu.VMEM)],
        out_specs=pl.BlockSpec(memory_space=pltpu.VMEM),
        compiler_params=pltpu.CompilerParams(vmem_limit_bytes=16 * 1024 * 1024),
        cost_estimate=pl.CostEstimate(flops=0, bytes_accessed=1 << 20, transcendentals=0),
    )(in_plane)


def roots_kernel(
    place_ref, left_ref, right_ref, one_ref, two_ref, three_ref,
    left_high_ref, left_low_ref, right_high_ref, right_low_ref,
):
    part = place_ref[1]
    width = left_ref.shape[1]

    def span(step):
        at = lax.rem(part + step, parts)
        return pl.ds(pl.multiple_of(at * width, width), width)

    def spread(root, own_ref, high_ref, low_ref):
        def put(row, col, block):
            high, low = split_two(block)
            high_ref[span(row), span(col)] = high
            low_ref[span(row), span(col)] = low

        def put_pair(row, col, block):
            put(row, col, block)
            put(col, row, block.T)

        put(0, 0, own_ref[0, :, span(0)])
        for step in range(1, parts):
            put_pair(0, step, own_ref[0, :, span(step)])
        put(1, 1, one_ref[root, :, :width])
        put_pair(1, 3, one_ref[root, :, width : 2 * width])
        put_pair(1, 2, one_ref[root, :, 2 * width :])
        put(2, 2, two_ref[root])
        put(3, 3, three_ref[root, :, :width])
        put_pair(3, 2, three_ref[root, :, width:])

    spread(0, left_ref, left_high_ref, left_low_ref)
    spread(1, right_ref, right_high_ref, right_low_ref)


def whole(shape):
    return pl.BlockSpec(shape, lambda i, *_: (0,) * len(shape))


def spread_roots(place, left_root, right_root, others):
    _, width, order = right_root.shape
    mine = pl.BlockSpec((1, width, order), lambda i, place: (place[2], 0, 0))
    out = jax.ShapeDtypeStruct((order, order), jnp.bfloat16)
    return pl.pallas_call(
        roots_kernel,
        grid_spec=pltpu.PrefetchScalarGridSpec(
            num_scalar_prefetch=1,
            grid=(1,),
            in_specs=[mine, mine] + [whole(other.shape) for other in others],
            out_specs=[whole(out.shape)] * 4,
        ),
        out_shape=[out] * 4,
        compiler_params=pltpu.CompilerParams(vmem_limit_bytes=32 * 1024 * 1024),
        cost_estimate=pl.CostEstimate(flops=0, bytes_accessed=5 << 20, transcendentals=0),
    )(place, left_root, right_root, *others)


def power(exponent):
    half = jnp.floor(exponent * 0.5)
    return jnp.exp2(half), jnp.exp2(exponent - half)


def coded(value):
    value = jnp.maximum(value, 1e-37)
    exponent = jnp.floor(jnp.log2(value)) + 1.0
    one, two = power(-exponent)
    share = value * one * two * 16384.0
    high = jnp.floor(share)
    return exponent, high, jnp.floor((share - high) * 16384.0)


def decoded(exponent, high, low):
    one, two = power(exponent - 14.0)
    return jnp.where(high > 0, (high + low * (1.0 / 16384.0)) * one * two, 0.0)


def square_root_code(value, top):
    root = jnp.sqrt(jnp.abs(value) * (code_top * code_top / top))
    return jnp.round(jnp.where(value < 0, -root, root)).astype(jnp.int32)


tn = (((0,), (0,)), ((), ()))
nn = (((1,), (0,)), ((), ()))
nt = (((1,), (1,)), ((), ()))
dot = functools.partial(lax.dot_general, preferred_element_type=jnp.float32)


def precondition_kernel(
    place_ref, grad_ref, left_high_ref, left_low_ref, right_high_ref, right_low_ref, message_ref
):
    order = left_high_ref.shape[0]
    grad = jnp.concatenate([grad_ref[:, m].reshape(order, -1) for m in range(parts)], axis=1)
    half = dot(left_high_ref[...], grad, tn) + dot(left_low_ref[...], grad, tn)
    half_high, half_low = split_two(half)
    right_high = right_high_ref[...]
    result = dot(half_high, right_high, nn) + dot(half_low, right_high, nn) + dot(half_high, right_low_ref[...], nn)
    taken = place_ref[3]
    result = jnp.where(taken > 0, result, 0.0)
    top = jnp.maximum(jnp.max(jnp.abs(result)), 1e-30)
    code = square_root_code(result, top)
    deep, width = message_ref.shape[2:]
    for z in range(far):
        for device in range(near):
            for m in range(parts):
                row = (z * near + device) * deep
                message_ref[device * parts + m, z] = code[row : row + deep, m * width : (m + 1) * width].astype(
                    jnp.int16
                )

    wide = grad.astype(jnp.float32)
    grad_sum = jnp.where(taken > 0, jnp.sum(wide * wide), 0.0)
    upd_sum = jnp.sum(result * result)
    row = lax.broadcasted_iota(jnp.int32, (8, 128), 0)
    at = lax.broadcasted_iota(jnp.int32, (8, 128), 1) - place_ref[0] * 16
    sum_at = at - place_ref[1] * 4
    top_at = at - place_ref[1] * 3
    is_up = jnp.where(taken > 1, 1, 0)
    exponent, high, low = coded(
        jnp.where(sum_at == is_up, grad_sum, jnp.where(sum_at == 2 + is_up, upd_sum, 0.0))
    )
    in_sums = (sum_at >= 0) & (sum_at < 4)
    sums = jnp.where(in_sums, jnp.where(row == 0, exponent, jnp.where(row == 1, high, low)), 0.0)
    exponent, high, low = coded(jnp.full((8, 128), top))
    in_tops = (top_at >= 0) & (top_at < 3) & (place_ref[1] < parts - 1)
    tops = jnp.where(in_tops, jnp.where(top_at == 0, exponent, jnp.where(top_at == 1, high, low)), 0.0)
    facts = jnp.where(row < 3, sums, tops)[:deep].astype(jnp.int32).astype(jnp.int16)
    for device in range(near * parts):
        message_ref[device, far] = facts


def precondition(place, landed, roots):
    _, rows, width = landed.shape
    order = near * rows
    landed = landed.reshape(near, parts, rows, width)
    message = (near * parts, far + 1, rows // far, width)
    return pl.pallas_call(
        precondition_kernel,
        grid_spec=pltpu.PrefetchScalarGridSpec(
            num_scalar_prefetch=1,
            grid=(1,),
            in_specs=[whole(landed.shape)] + [whole((order, order))] * 4,
            out_specs=whole(message),
        ),
        out_shape=jax.ShapeDtypeStruct(message, jnp.int16),
        compiler_params=pltpu.CompilerParams(vmem_limit_bytes=32 * 1024 * 1024),
        cost_estimate=pl.CostEstimate(flops=10 * order**3, bytes_accessed=4 << 20, transcendentals=0),
    )(place, landed, *roots)


def terms_kernel(place_ref, block_ref, own_ref, one_ref, two_ref, three_ref, term_ref):
    block = block_ref[...]
    out_refs = (own_ref, one_ref, two_ref, three_ref)
    width = own_ref.shape[1] - 16
    row = lax.broadcasted_iota(jnp.int32, (16, block.shape[1]), 0)
    for side in range(2):
        term = dot(block, block, nt if side == 0 else tn)
        top = jnp.maximum(jnp.max(jnp.abs(term)), 1e-30)
        term_ref[...] = square_root_code(term, top)
        exponent, high, low = coded(jnp.full(row.shape, top))
        scale = jnp.where(row == 0, exponent, jnp.where(row == 1, high, low)).astype(jnp.int32).astype(jnp.int16)
        for step in range(parts):
            at = lax.rem(place_ref[1] + step, parts)
            out_refs[step][side, :width] = term_ref[pl.ds(pl.multiple_of(at * width, width), width), :].astype(
                jnp.int16
            )
            out_refs[step][side, width:] = scale


def terms(place, block):
    order = block.shape[0]
    out = jax.ShapeDtypeStruct((2, order // parts + 16, order), jnp.int16)
    return pl.pallas_call(
        terms_kernel,
        grid_spec=pltpu.PrefetchScalarGridSpec(
            num_scalar_prefetch=1,
            grid=(1,),
            in_specs=[whole(block.shape)],
            out_specs=[whole(out.shape)] * parts,
            scratch_shapes=[pltpu.VMEM((order, order), jnp.int32)],
        ),
        out_shape=[out] * parts,
        compiler_params=pltpu.CompilerParams(vmem_limit_bytes=32 * 1024 * 1024),
        cost_estimate=pl.CostEstimate(flops=4 * order**3, bytes_accessed=2 << 20, transcendentals=0),
    )(place, block)


def stats_kernel(place_ref, own_ref, one_ref, two_ref, three_ref, left_ref, right_ref, left_new_ref, right_new_ref):
    slots, width, order = left_ref.shape
    sides = ((left_ref, left_new_ref), (right_ref, right_new_ref))
    for slot in range(slots):
        steps = lax.rem(place_ref[1] + parts - slot, parts)
        taken = place_ref[4 + slot]
        for step, terms_ref in enumerate((own_ref, one_ref, two_ref, three_ref)):

            @pl.when((steps == step) & (taken > 0))
            def _(terms_ref=terms_ref):
                for side, (old_ref, new_ref) in enumerate(sides):
                    code = terms_ref[side, :width].astype(jnp.int32).astype(jnp.float32)
                    scale = terms_ref[side, width:].astype(jnp.int32).astype(jnp.float32)
                    top = decoded(scale[0:1], scale[1:2], scale[2:3])
                    gain = top * ((1.0 - decay_rate) / order / (code_top * code_top))
                    new_ref[slot] = decay_rate * old_ref[slot] + code * jnp.abs(code) * gain

        @pl.when(taken == 0)
        def _():
            for old_ref, new_ref in sides:
                new_ref[slot] = old_ref[slot]


def new_stats(place, coded_terms, left_stats, right_stats):
    out = jax.ShapeDtypeStruct(left_stats.shape, jnp.float32)
    return pl.pallas_call(
        stats_kernel,
        grid_spec=pltpu.PrefetchScalarGridSpec(
            num_scalar_prefetch=1,
            grid=(1,),
            in_specs=[whole(coded_terms[0].shape)] * parts + [whole(out.shape)] * 2,
            out_specs=[whole(out.shape)] * 2,
        ),
        out_shape=[out] * 2,
        compiler_params=pltpu.CompilerParams(vmem_limit_bytes=32 * 1024 * 1024),
        cost_estimate=pl.CostEstimate(flops=0, bytes_accessed=5 << 20, transcendentals=0),
    )(place, *coded_terms, left_stats, right_stats)


def repack_kernel(back_ref, ahead_ref):
    cells = ahead_ref.shape[1] - 1
    slots = cells // near
    for device in range(near):
        for slot in range(slots):
            ahead_ref[:, device * slots + slot] = back_ref[device * parts + slot, :far]
    wide = [back_ref[device, far].astype(jnp.int32) for device in range(near * parts)]
    facts = functools.reduce(jnp.add, wide).astype(jnp.int16)
    for z in range(far):
        ahead_ref[z, cells] = facts


def repack(back, slots):
    return pl.pallas_call(
        repack_kernel,
        out_shape=jax.ShapeDtypeStruct((far, near * slots + 1) + back.shape[2:], back.dtype),
        in_specs=[pl.BlockSpec(memory_space=pltpu.VMEM)],
        out_specs=pl.BlockSpec(memory_space=pltpu.VMEM),
        compiler_params=pltpu.CompilerParams(vmem_limit_bytes=16 * 1024 * 1024),
        cost_estimate=pl.CostEstimate(flops=0, bytes_accessed=1 << 20, transcendentals=0),
    )(back)


def finish_kernel(at_ref, spot_ref, up_ref, arrived_ref, update_ref, factor_ref):
    cells = arrived_ref.shape[1] - 1
    facts = [arrived_ref[z, cells].astype(jnp.int32).astype(jnp.float32) for z in range(far)]
    row = lambda r: jnp.concatenate([fact[r : r + 1] for fact in facts], axis=0)
    sums = jnp.sum(decoded(row(0), row(1), row(2)), axis=0, keepdims=True)
    kind = lax.rem(lax.broadcasted_iota(jnp.int32, sums.shape, 1), 4)
    total = lambda k: jnp.sum(jnp.where(kind == k, sums, 0.0), axis=1, keepdims=True)
    gate_scale = jnp.sqrt(total(0) / total(2))
    up_scale = jnp.sqrt(total(1) / total(3))
    tops = row(3)
    lanes = tops.shape[1]
    steps = decoded(tops, pltpu.roll(tops, lanes - 1, 1), pltpu.roll(tops, lanes - 2, 1))
    steps = steps * (1.0 / (code_top * code_top))
    spot = spot_ref[...]
    lane = lax.broadcasted_iota(jnp.int32, spot.shape, 1)
    mine = jnp.zeros(spot.shape, jnp.float32)
    for z in range(far):
        mine += jnp.where(spot == lane + z * lanes, steps[z : z + 1], 0.0)
    step = jnp.sum(mine, axis=1, keepdims=True)
    factor_ref[...] = jnp.where(up_ref[...] > 0, up_scale, gate_scale) * step

    for b in range(update_ref.shape[0]):
        at = at_ref[b]
        code = arrived_ref[at // cells, lax.rem(at, cells)].astype(jnp.int32).astype(jnp.float32)
        update_ref[b] = (code * jnp.abs(code) * factor_ref[b : b + 1, :]).astype(jnp.bfloat16)


def finish(cell_ids, spot, up, arrived):
    blocks = cell_ids.shape[0]
    return pl.pallas_call(
        finish_kernel,
        grid_spec=pltpu.PrefetchScalarGridSpec(
            num_scalar_prefetch=1,
            grid=(1,),
            in_specs=[whole(spot.shape), whole(up.shape), whole(arrived.shape)],
            out_specs=whole((blocks,) + arrived.shape[2:]),
            scratch_shapes=[pltpu.VMEM((blocks, arrived.shape[3]), jnp.float32)],
        ),
        out_shape=jax.ShapeDtypeStruct((blocks,) + arrived.shape[2:], jnp.bfloat16),
        compiler_params=pltpu.CompilerParams(vmem_limit_bytes=16 * 1024 * 1024),
        cost_estimate=pl.CostEstimate(flops=0, bytes_accessed=1 << 20, transcendentals=0),
    )(cell_ids, spot, up, arrived)


def on_device(gradient, owner_map, left_stats, right_stats, left_root, right_root):
    block_count, row_share, col_share = gradient.shape
    capacity, part_rows, block_size = left_stats.shape
    my_owner = lax.axis_index("fsdp")
    my_part = lax.axis_index("mp")

    packed = pack(owner_map, gradient, capacity).reshape(far, near, capacity, row_share, col_share)
    in_plane = exchange(packed, "fsdp", far_groups)

    def send(steps, k):
        slot = jnp.minimum((my_part + k) % parts, capacity - 1)

        def column(root, step):
            start = (my_part + step) % parts * part_rows
            return lax.dynamic_slice(root, (slot, 0, start), (1, part_rows, part_rows))

        rows = [jnp.concatenate([column(root, step) for step in steps], axis=2) for root in (left_root, right_root)]
        pairs = [(i, (i + k) % parts) for i in range(parts)]
        return lax.ppermute(jnp.concatenate(rows, axis=0), "mp", pairs)

    three = send((0, 3), 1)
    two = send((0,), 2)
    one = send((0, 2, 1), 3)
    in_plane, one, two, three, owner_map = lax.optimization_barrier((in_plane, one, two, three, owner_map))

    fanned = fan(in_plane).reshape(near * parts, far * row_share, col_share)
    landed = exchange(fanned, ("fsdp", "mp"), plane_groups)

    cell_ids = cell_index(owner_map, capacity)
    up_block = jnp.arange(block_count, dtype=jnp.int32) >= block_count // 2
    my_cells = my_owner * capacity + jnp.arange(capacity, dtype=jnp.int32)
    holding = cell_ids[None, :] == my_cells[:, None]
    taken = jnp.max(jnp.where(holding, 1 + up_block.astype(jnp.int32)[None, :], 0), axis=1)
    my_slot = jnp.minimum(my_part, capacity - 1)
    my_taken = jnp.where(my_part < capacity, taken[my_slot], 0)
    place = jnp.concatenate([jnp.stack([my_owner % near, my_part, my_slot, my_taken]), taken])

    roots = spread_roots(place, left_root, right_root, (one, two, three))

    def landed_order(array):
        split = array.reshape(far, near, row_share, block_size)
        return jnp.swapaxes(split, 0, 1).reshape(block_size, block_size)

    roots = (landed_order(roots[0]), landed_order(roots[1]), roots[2], roots[3])
    message = precondition(place, landed, roots)
    landed, message = lax.optimization_barrier((landed, message))
    back = exchange(message, ("fsdp", "mp"), plane_groups)
    arrived = exchange(repack(back, capacity), "fsdp", far_groups)

    block = landed.reshape(near, parts, far, row_share, col_share).transpose(2, 0, 3, 1, 4)
    own_terms, *other_terms = terms(place, block.reshape(block_size, block_size))
    coded_terms = [own_terms]
    for k, other in enumerate(other_terms, 1):
        coded_terms.append(lax.ppermute(other, "mp", [(i, (i + k) % parts) for i in range(parts)]))
    left_new, right_new = new_stats(place, coded_terms, left_stats, right_stats)

    cells = near * capacity
    spot = cell_ids // cells * 128 + cell_ids % cells // capacity * 16 + cell_ids % capacity * 3
    across = lambda array: jnp.broadcast_to(array.astype(jnp.int32)[:, None], (block_count, 128))
    update = finish(cell_ids, across(spot), across(up_block), arrived)
    return (update, left_new, right_new)


def solution(mesh):
    placed = (
        P(None, "fsdp", "mp"),
        P(),
        P("fsdp", "mp", None),
        P("fsdp", "mp", None),
        P("fsdp", "mp", None),
        P("fsdp", "mp", None),
    )
    return jax.shard_map(
        on_device,
        mesh=mesh,
        in_specs=placed,
        out_specs=(P(None, "fsdp", "mp"), P("fsdp", "mp", None), P("fsdp", "mp", None)),
        check_vma=False,
    )
```

```python
import functools

import jax
import jax.numpy as jnp
from jax import lax
from jax.experimental import pallas as pl
from jax.experimental.pallas import tpu as pltpu
from jax.sharding import PartitionSpec as P

decay_rate = 0.95
code_top = 32767.0
parts = 4
near = 8
far = 16


def cell_index(owner_map, capacity):
    total_rows = owner_map.shape[0]
    positions = jnp.arange(total_rows, dtype=jnp.int32)
    same_owner = owner_map[None, :] == owner_map[:, None]
    earlier = positions[None, :] < positions[:, None]
    ranks = jnp.sum((same_owner & earlier).astype(jnp.int32), axis=1)
    return owner_map * capacity + ranks


far_groups = [[z * near + n for z in range(far)] for n in range(near)]
plane_groups = [[(z * near + n) * parts + m for n in range(near) for m in range(parts)] for z in range(far)]


def exchange(array, axis_name, groups):
    return lax.all_to_all(
        array, axis_name, split_axis=0, concat_axis=0, axis_index_groups=groups, tiled=True
    )


def split_two(array):
    high = array.astype(jnp.bfloat16)
    return high, (array - high.astype(jnp.float32)).astype(jnp.bfloat16)


tn = (((0,), (0,)), ((), ()))
nn = (((1,), (0,)), ((), ()))
nt = (((1,), (1,)), ((), ()))
dot = functools.partial(lax.dot_general, preferred_element_type=jnp.float32)


def pack_kernel(owner_ref, grad_ref, packed_ref, count_ref):
    blocks = grad_ref.shape[0]
    slots = packed_ref.shape[0] // blocks
    packed_ref[...] = jnp.zeros_like(packed_ref)
    for owner in range(blocks):
        count_ref[owner] = 0
    for b in range(blocks):
        owner = owner_ref[b]
        rank = count_ref[owner]
        count_ref[owner] = rank + 1
        packed_ref[owner * slots + rank] = grad_ref[b]


def pack(owner_map, gradient, slots):
    blocks = gradient.shape[0]
    packed = (blocks * slots,) + gradient.shape[1:]
    return pl.pallas_call(
        pack_kernel,
        grid_spec=pltpu.PrefetchScalarGridSpec(
            num_scalar_prefetch=1,
            grid=(1,),
            in_specs=[whole(gradient.shape)],
            out_specs=whole(packed),
            scratch_shapes=[pltpu.SMEM((blocks,), jnp.int32)],
        ),
        out_shape=jax.ShapeDtypeStruct(packed, gradient.dtype),
        compiler_params=pltpu.CompilerParams(vmem_limit_bytes=16 * 1024 * 1024),
        cost_estimate=pl.CostEstimate(flops=0, bytes_accessed=1 << 20, transcendentals=0),
    )(owner_map, gradient)


def fan_kernel(plane_ref, fan_ref):
    for n in range(near):
        for slot in range(parts):
            if slot < plane_ref.shape[2]:
                fan_ref[n, slot] = plane_ref[:, n, slot]
            else:
                fan_ref[n, slot] = jnp.zeros(fan_ref.shape[2:], fan_ref.dtype)


def fan(in_plane):
    _, _, slots, rows, width = in_plane.shape
    return pl.pallas_call(
        fan_kernel,
        out_shape=jax.ShapeDtypeStruct((near, parts, far, rows, width), in_plane.dtype),
        in_specs=[pl.BlockSpec(memory_space=pltpu.VMEM)],
        out_specs=pl.BlockSpec(memory_space=pltpu.VMEM),
        compiler_params=pltpu.CompilerParams(vmem_limit_bytes=16 * 1024 * 1024),
        cost_estimate=pl.CostEstimate(flops=0, bytes_accessed=1 << 20, transcendentals=0),
    )(in_plane)


def roots_kernel(
    place_ref, left_ref, right_ref, one_ref, two_ref, three_ref,
    left_high_ref, left_low_ref, right_high_ref, right_low_ref, high_ref, low_ref,
):
    part = place_ref[1]
    width = left_ref.shape[1]

    def span(step):
        at = lax.rem(part + step, parts)
        return pl.ds(pl.multiple_of(at * width, width), width)

    def spread(root, own_ref, high_ref, low_ref):
        def put(row, col, block):
            high, low = split_two(block)
            high_ref[span(row), span(col)] = high
            low_ref[span(row), span(col)] = low

        def put_pair(row, col, block):
            put(row, col, block)
            put(col, row, block.T)

        put(0, 0, own_ref[0, :, span(0)])
        for step in range(1, parts):
            put_pair(0, step, own_ref[0, :, span(step)])
        put(1, 1, one_ref[root, :, :width])
        put_pair(1, 3, one_ref[root, :, width : 2 * width])
        put_pair(1, 2, one_ref[root, :, 2 * width :])
        put(2, 2, two_ref[root])
        put(3, 3, three_ref[root, :, :width])
        put_pair(3, 2, three_ref[root, :, width:])

    spread(0, left_ref, high_ref, low_ref)
    spread(1, right_ref, right_high_ref, right_low_ref)
    row = lax.broadcasted_iota(jnp.int32, (width, width), 0)
    col = lax.broadcasted_iota(jnp.int32, (width, width), 1)
    z = lax.shift_right_logical(row, 2) & (parts - 1)
    source = z * (width // parts) + lax.shift_right_logical(row, 4) * 4 + (row & 3)
    order = jnp.where(col == source, 1.0, 0.0).astype(jnp.bfloat16)
    for m in range(parts):
        cols = slice(m * width, (m + 1) * width)
        left_high_ref[:, cols] = dot(high_ref[:, cols], order, nt).astype(jnp.bfloat16)
        left_low_ref[:, cols] = dot(low_ref[:, cols], order, nt).astype(jnp.bfloat16)


def whole(shape):
    return pl.BlockSpec(shape, lambda i, *_: (0,) * len(shape))


def spread_roots(place, left_root, right_root, others):
    _, width, order = right_root.shape
    mine = pl.BlockSpec((1, width, order), lambda i, place: (place[2], 0, 0))
    out = jax.ShapeDtypeStruct((order, order), jnp.bfloat16)
    return pl.pallas_call(
        roots_kernel,
        grid_spec=pltpu.PrefetchScalarGridSpec(
            num_scalar_prefetch=1,
            grid=(1,),
            in_specs=[mine, mine] + [whole(other.shape) for other in others],
            out_specs=[whole(out.shape)] * 4,
            scratch_shapes=[pltpu.VMEM(out.shape, out.dtype)] * 2,
        ),
        out_shape=[out] * 4,
        compiler_params=pltpu.CompilerParams(vmem_limit_bytes=32 * 1024 * 1024),
        cost_estimate=pl.CostEstimate(flops=0, bytes_accessed=5 << 20, transcendentals=0),
    )(place, left_root, right_root, *others)


def power(exponent):
    half = jnp.floor(exponent * 0.5)
    return jnp.exp2(half), jnp.exp2(exponent - half)


def coded(value):
    value = jnp.maximum(value, 1e-37)
    exponent = jnp.floor(jnp.log2(value)) + 1.0
    one, two = power(-exponent)
    share = value * one * two * 16384.0
    high = jnp.floor(share)
    return exponent, high, jnp.floor((share - high) * 16384.0)


def decoded(exponent, high, low):
    one, two = power(exponent - 14.0)
    return jnp.where(high > 0, (high + low * (1.0 / 16384.0)) * one * two, 0.0)


def square_root_code(value, top):
    root = jnp.sqrt(jnp.abs(value) * (code_top * code_top / top))
    return jnp.round(jnp.where(value < 0, -root, root)).astype(jnp.int32)


def precondition_kernel(
    place_ref, grad_ref, left_high_ref, left_low_ref, right_high_ref, right_low_ref, message_ref
):
    order = left_high_ref.shape[0]
    deep = grad_ref.shape[2] // parts
    rows = [(device, slice(m * deep, (m + 1) * deep)) for m in range(parts) for device in range(near)]
    grad = jnp.concatenate(
        [jnp.concatenate([grad_ref[device, m, at] for device, at in rows], axis=0) for m in range(parts)], axis=1
    )
    half = dot(left_high_ref[...], grad, nn) + dot(left_low_ref[...], grad, nn)
    half_high, half_low = split_two(half)
    right_high = right_high_ref[...]
    result = dot(half_high, right_high, nn) + dot(half_low, right_high, nn) + dot(half_high, right_low_ref[...], nn)
    taken = place_ref[3]
    result = jnp.where(taken > 0, result, 0.0)
    top = jnp.maximum(jnp.max(jnp.abs(result)), 1e-30)
    code = square_root_code(result, top)
    deep, width = message_ref.shape[2:]
    for z in range(far):
        for device in range(near):
            for m in range(parts):
                row = (z * near + device) * deep
                message_ref[device * parts + m, z] = code[row : row + deep, m * width : (m + 1) * width].astype(
                    jnp.int16
                )

    wide = grad.astype(jnp.float32)
    grad_sum = jnp.where(taken > 0, jnp.sum(wide * wide), 0.0)
    upd_sum = jnp.sum(result * result)
    row = lax.broadcasted_iota(jnp.int32, (8, 128), 0)
    at = lax.broadcasted_iota(jnp.int32, (8, 128), 1) - place_ref[0] * 16
    sum_at = at - place_ref[1] * 4
    top_at = at - place_ref[1] * 3
    is_up = jnp.where(taken > 1, 1, 0)
    exponent, high, low = coded(
        jnp.where(sum_at == is_up, grad_sum, jnp.where(sum_at == 2 + is_up, upd_sum, 0.0))
    )
    in_sums = (sum_at >= 0) & (sum_at < 4)
    sums = jnp.where(in_sums, jnp.where(row == 0, exponent, jnp.where(row == 1, high, low)), 0.0)
    exponent, high, low = coded(jnp.full((8, 128), top))
    in_tops = (top_at >= 0) & (top_at < 3) & (place_ref[1] < parts - 1)
    tops = jnp.where(in_tops, jnp.where(top_at == 0, exponent, jnp.where(top_at == 1, high, low)), 0.0)
    facts = jnp.where(row < 3, sums, tops)[:deep].astype(jnp.int32).astype(jnp.int16)
    for device in range(near * parts):
        message_ref[device, far] = facts


def precondition(place, landed, roots):
    _, rows, width = landed.shape
    order = near * rows
    landed = landed.reshape(near, parts, rows, width)
    message = (near * parts, far + 1, rows // far, width)
    return pl.pallas_call(
        precondition_kernel,
        grid_spec=pltpu.PrefetchScalarGridSpec(
            num_scalar_prefetch=1,
            grid=(1,),
            in_specs=[whole(landed.shape)] + [whole((order, order))] * 4,
            out_specs=whole(message),
        ),
        out_shape=jax.ShapeDtypeStruct(message, jnp.int16),
        compiler_params=pltpu.CompilerParams(vmem_limit_bytes=32 * 1024 * 1024),
        cost_estimate=pl.CostEstimate(flops=10 * order**3, bytes_accessed=4 << 20, transcendentals=0),
    )(place, landed, *roots)


def terms_kernel(place_ref, block_ref, own_ref, one_ref, two_ref, three_ref, term_ref):
    block = block_ref[...]
    out_refs = (own_ref, one_ref, two_ref, three_ref)
    width = own_ref.shape[1] - 16
    row = lax.broadcasted_iota(jnp.int32, (16, block.shape[1]), 0)
    for side in range(2):
        term = dot(block, block, nt if side == 0 else tn)
        top = jnp.maximum(jnp.max(jnp.abs(term)), 1e-30)
        term_ref[...] = square_root_code(term, top)
        exponent, high, low = coded(jnp.full(row.shape, top))
        scale = jnp.where(row == 0, exponent, jnp.where(row == 1, high, low)).astype(jnp.int32).astype(jnp.int16)
        for step in range(parts):
            at = lax.rem(place_ref[1] + step, parts)
            out_refs[step][side, :width] = term_ref[pl.ds(pl.multiple_of(at * width, width), width), :].astype(
                jnp.int16
            )
            out_refs[step][side, width:] = scale


def terms(place, block):
    order = block.shape[0]
    out = jax.ShapeDtypeStruct((2, order // parts + 16, order), jnp.int16)
    return pl.pallas_call(
        terms_kernel,
        grid_spec=pltpu.PrefetchScalarGridSpec(
            num_scalar_prefetch=1,
            grid=(1,),
            in_specs=[whole(block.shape)],
            out_specs=[whole(out.shape)] * parts,
            scratch_shapes=[pltpu.VMEM((order, order), jnp.int32)],
        ),
        out_shape=[out] * parts,
        compiler_params=pltpu.CompilerParams(vmem_limit_bytes=32 * 1024 * 1024),
        cost_estimate=pl.CostEstimate(flops=4 * order**3, bytes_accessed=2 << 20, transcendentals=0),
    )(place, block)


def stats_kernel(place_ref, own_ref, one_ref, two_ref, three_ref, left_ref, right_ref, left_new_ref, right_new_ref):
    slots, width, order = left_ref.shape
    sides = ((left_ref, left_new_ref), (right_ref, right_new_ref))
    for slot in range(slots):
        steps = lax.rem(place_ref[1] + parts - slot, parts)
        taken = place_ref[4 + slot]
        for step, terms_ref in enumerate((own_ref, one_ref, two_ref, three_ref)):

            @pl.when((steps == step) & (taken > 0))
            def _(terms_ref=terms_ref):
                for side, (old_ref, new_ref) in enumerate(sides):
                    code = terms_ref[side, :width].astype(jnp.int32).astype(jnp.float32)
                    scale = terms_ref[side, width:].astype(jnp.int32).astype(jnp.float32)
                    top = decoded(scale[0:1], scale[1:2], scale[2:3])
                    gain = top * ((1.0 - decay_rate) / order / (code_top * code_top))
                    new_ref[slot] = decay_rate * old_ref[slot] + code * jnp.abs(code) * gain

        @pl.when(taken == 0)
        def _():
            for old_ref, new_ref in sides:
                new_ref[slot] = old_ref[slot]


def new_stats(place, coded_terms, left_stats, right_stats):
    out = jax.ShapeDtypeStruct(left_stats.shape, jnp.float32)
    return pl.pallas_call(
        stats_kernel,
        grid_spec=pltpu.PrefetchScalarGridSpec(
            num_scalar_prefetch=1,
            grid=(1,),
            in_specs=[whole(coded_terms[0].shape)] * parts + [whole(out.shape)] * 2,
            out_specs=[whole(out.shape)] * 2,
        ),
        out_shape=[out] * 2,
        compiler_params=pltpu.CompilerParams(vmem_limit_bytes=32 * 1024 * 1024),
        cost_estimate=pl.CostEstimate(flops=0, bytes_accessed=5 << 20, transcendentals=0),
    )(place, *coded_terms, left_stats, right_stats)


def repack_kernel(back_ref, ahead_ref):
    cells = ahead_ref.shape[1] - 1
    slots = cells // near
    for device in range(near):
        for slot in range(slots):
            ahead_ref[:, device * slots + slot] = back_ref[device * parts + slot, :far]
    wide = [back_ref[device, far].astype(jnp.int32) for device in range(near * parts)]
    facts = functools.reduce(jnp.add, wide).astype(jnp.int16)
    for z in range(far):
        ahead_ref[z, cells] = facts


def repack(back, slots):
    return pl.pallas_call(
        repack_kernel,
        out_shape=jax.ShapeDtypeStruct((far, near * slots + 1) + back.shape[2:], back.dtype),
        in_specs=[pl.BlockSpec(memory_space=pltpu.VMEM)],
        out_specs=pl.BlockSpec(memory_space=pltpu.VMEM),
        compiler_params=pltpu.CompilerParams(vmem_limit_bytes=16 * 1024 * 1024),
        cost_estimate=pl.CostEstimate(flops=0, bytes_accessed=1 << 20, transcendentals=0),
    )(back)


def finish_kernel(at_ref, spot_ref, up_ref, arrived_ref, update_ref, factor_ref):
    cells = arrived_ref.shape[1] - 1
    facts = [arrived_ref[z, cells].astype(jnp.int32).astype(jnp.float32) for z in range(far)]
    row = lambda r: jnp.concatenate([fact[r : r + 1] for fact in facts], axis=0)
    sums = jnp.sum(decoded(row(0), row(1), row(2)), axis=0, keepdims=True)
    kind = lax.rem(lax.broadcasted_iota(jnp.int32, sums.shape, 1), 4)
    total = lambda k: jnp.sum(jnp.where(kind == k, sums, 0.0), axis=1, keepdims=True)
    gate_scale = jnp.sqrt(total(0) / total(2))
    up_scale = jnp.sqrt(total(1) / total(3))
    tops = row(3)
    lanes = tops.shape[1]
    steps = decoded(tops, pltpu.roll(tops, lanes - 1, 1), pltpu.roll(tops, lanes - 2, 1))
    steps = steps * (1.0 / (code_top * code_top))
    spot = spot_ref[...]
    lane = lax.broadcasted_iota(jnp.int32, spot.shape, 1)
    mine = jnp.zeros(spot.shape, jnp.float32)
    for z in range(far):
        mine += jnp.where(spot == lane + z * lanes, steps[z : z + 1], 0.0)
    step = jnp.sum(mine, axis=1, keepdims=True)
    factor_ref[...] = jnp.where(up_ref[...] > 0, up_scale, gate_scale) * step

    for b in range(update_ref.shape[0]):
        at = at_ref[b]
        code = arrived_ref[at // cells, lax.rem(at, cells)].astype(jnp.int32).astype(jnp.float32)
        update_ref[b] = (code * jnp.abs(code) * factor_ref[b : b + 1, :]).astype(jnp.bfloat16)


def finish(cell_ids, spot, up, arrived):
    blocks = cell_ids.shape[0]
    return pl.pallas_call(
        finish_kernel,
        grid_spec=pltpu.PrefetchScalarGridSpec(
            num_scalar_prefetch=1,
            grid=(1,),
            in_specs=[whole(spot.shape), whole(up.shape), whole(arrived.shape)],
            out_specs=whole((blocks,) + arrived.shape[2:]),
            scratch_shapes=[pltpu.VMEM((blocks, arrived.shape[3]), jnp.float32)],
        ),
        out_shape=jax.ShapeDtypeStruct((blocks,) + arrived.shape[2:], jnp.bfloat16),
        compiler_params=pltpu.CompilerParams(vmem_limit_bytes=16 * 1024 * 1024),
        cost_estimate=pl.CostEstimate(flops=0, bytes_accessed=1 << 20, transcendentals=0),
    )(cell_ids, spot, up, arrived)


def on_device(gradient, owner_map, left_stats, right_stats, left_root, right_root):
    block_count, row_share, col_share = gradient.shape
    capacity, part_rows, block_size = left_stats.shape
    my_owner = lax.axis_index("fsdp")
    my_part = lax.axis_index("mp")

    packed = pack(owner_map, gradient, capacity).reshape(far, near, capacity, row_share, col_share)
    in_plane = exchange(packed, "fsdp", far_groups)

    def send(steps, k):
        slot = jnp.minimum((my_part + k) % parts, capacity - 1)

        def column(root, step):
            start = (my_part + step) % parts * part_rows
            return lax.dynamic_slice(root, (slot, 0, start), (1, part_rows, part_rows))

        rows = [jnp.concatenate([column(root, step) for step in steps], axis=2) for root in (left_root, right_root)]
        pairs = [(i, (i + k) % parts) for i in range(parts)]
        return lax.ppermute(jnp.concatenate(rows, axis=0), "mp", pairs)

    three = send((0, 3), 1)
    two = send((0,), 2)
    one = send((0, 2, 1), 3)
    my_slot = jnp.minimum(my_part, capacity - 1)
    place = jnp.stack([my_owner % near, my_part, my_slot])
    roots = spread_roots(place, left_root, right_root, (one, two, three))
    in_plane, owner_map, *roots = lax.optimization_barrier((in_plane, owner_map, *roots))

    fanned = fan(in_plane).reshape(near * parts, far * row_share, col_share)
    landed = exchange(fanned, ("fsdp", "mp"), plane_groups)

    cell_ids = cell_index(owner_map, capacity)
    up_block = jnp.arange(block_count, dtype=jnp.int32) >= block_count // 2
    my_cells = my_owner * capacity + jnp.arange(capacity, dtype=jnp.int32)
    holding = cell_ids[None, :] == my_cells[:, None]
    taken = jnp.max(jnp.where(holding, 1 + up_block.astype(jnp.int32)[None, :], 0), axis=1)
    my_taken = jnp.where(my_part < capacity, taken[my_slot], 0)
    place = jnp.concatenate([place, my_taken[None], taken])
    message = precondition(place, landed, roots)
    landed, message = lax.optimization_barrier((landed, message))
    back = exchange(message, ("fsdp", "mp"), plane_groups)

    block = landed.reshape(near, parts, far, row_share, col_share).transpose(2, 0, 3, 1, 4)
    made = terms(place, block.reshape(block_size, block_size))
    back, own_terms, *other_terms = lax.optimization_barrier((back, *made))
    coded_terms = [own_terms]
    for k, other in enumerate(other_terms, 1):
        coded_terms.append(lax.ppermute(other, "mp", [(i, (i + k) % parts) for i in range(parts)]))
    arrived = exchange(repack(back, capacity), "fsdp", far_groups)
    left_new, right_new = new_stats(place, coded_terms, left_stats, right_stats)

    cells = near * capacity
    spot = cell_ids // cells * 128 + cell_ids % cells // capacity * 16 + cell_ids % capacity * 3
    across = lambda array: jnp.broadcast_to(array.astype(jnp.int32)[:, None], (block_count, 128))
    update = finish(cell_ids, across(spot), across(up_block), arrived)
    return (update, left_new, right_new)


def solution(mesh):
    placed = (
        P(None, "fsdp", "mp"),
        P(),
        P("fsdp", "mp", None),
        P("fsdp", "mp", None),
        P("fsdp", "mp", None),
        P("fsdp", "mp", None),
    )
    return jax.shard_map(
        on_device,
        mesh=mesh,
        in_specs=placed,
        out_specs=(P(None, "fsdp", "mp"), P("fsdp", "mp", None), P("fsdp", "mp", None)),
        check_vma=False,
    )
```

```python
import functools

import jax
import jax.numpy as jnp
from jax import lax
from jax.experimental import pallas as pl
from jax.experimental.pallas import tpu as pltpu
from jax.sharding import PartitionSpec as P

decay_rate = 0.95
code_top = 32767.0
parts = 4
near = 8
far = 16


def earlier_alike(kind):
    positions = jnp.arange(kind.shape[0], dtype=jnp.int32)
    alike = (kind[None, :] == kind[:, None]) & (positions[None, :] < positions[:, None])
    return jnp.sum(alike.astype(jnp.int32), axis=1)


far_groups = [[z * near + n for z in range(far)] for n in range(near)]
plane_groups = [[(z * near + n) * parts + m for n in range(near) for m in range(parts)] for z in range(far)]


def exchange(array, axis_name, groups):
    return lax.all_to_all(
        array, axis_name, split_axis=0, concat_axis=0, axis_index_groups=groups, tiled=True
    )


def split_two(array):
    high = array.astype(jnp.bfloat16)
    return high, (array - high.astype(jnp.float32)).astype(jnp.bfloat16)


tn = (((0,), (0,)), ((), ()))
nn = (((1,), (0,)), ((), ()))
nt = (((1,), (1,)), ((), ()))
dot = functools.partial(lax.dot_general, preferred_element_type=jnp.float32)


def whole(shape):
    return pl.BlockSpec(shape, lambda i, *_: (0,) * len(shape))


def pack_kernel(owner_ref, grad_ref, packed_ref, count_ref):
    packed_ref[...] = jnp.zeros_like(packed_ref)
    for z in range(far):
        count_ref[z] = 0
    for b in range(grad_ref.shape[0]):
        z = lax.div(owner_ref[b], near)
        rank = count_ref[z]
        count_ref[z] = rank + 1
        packed_ref[z, rank] = grad_ref[b]


def pack(owner_map, gradient, room):
    packed = (far, room) + gradient.shape[1:]
    return pl.pallas_call(
        pack_kernel,
        grid_spec=pltpu.PrefetchScalarGridSpec(
            num_scalar_prefetch=1,
            grid=(1,),
            in_specs=[whole(gradient.shape)],
            out_specs=whole(packed),
            scratch_shapes=[pltpu.SMEM((far,), jnp.int32)],
        ),
        out_shape=jax.ShapeDtypeStruct(packed, gradient.dtype),
        compiler_params=pltpu.CompilerParams(vmem_limit_bytes=16 * 1024 * 1024),
        cost_estimate=pl.CostEstimate(flops=0, bytes_accessed=1 << 20, transcendentals=0),
    )(owner_map, gradient)


def fan_kernel(rank_ref, plane_ref, fan_ref):
    slots = rank_ref.shape[0] // near
    for n in range(near):
        for slot in range(slots):
            rank = jnp.maximum(rank_ref[n * slots + slot], 0)
            fan_ref[n, slot] = plane_ref[:, rank]
        for slot in range(slots, parts):
            fan_ref[n, slot] = jnp.zeros(fan_ref.shape[2:], fan_ref.dtype)


def fan(ranks, in_plane):
    fanned = (near, parts, far) + in_plane.shape[2:]
    return pl.pallas_call(
        fan_kernel,
        grid_spec=pltpu.PrefetchScalarGridSpec(
            num_scalar_prefetch=1, grid=(1,), in_specs=[whole(in_plane.shape)], out_specs=whole(fanned)
        ),
        out_shape=jax.ShapeDtypeStruct(fanned, in_plane.dtype),
        compiler_params=pltpu.CompilerParams(vmem_limit_bytes=16 * 1024 * 1024),
        cost_estimate=pl.CostEstimate(flops=0, bytes_accessed=1 << 20, transcendentals=0),
    )(ranks, in_plane)


def roots_kernel(
    place_ref, left_ref, right_ref, one_ref, two_ref, three_ref,
    left_high_ref, left_low_ref, right_high_ref, right_low_ref, high_ref, low_ref,
):
    part = place_ref[1]
    width = left_ref.shape[1]

    def span(step):
        at = lax.rem(part + step, parts)
        return pl.ds(pl.multiple_of(at * width, width), width)

    def spread(root, own_ref, high_ref, low_ref):
        def put(row, col, block):
            high, low = split_two(block)
            high_ref[span(row), span(col)] = high
            low_ref[span(row), span(col)] = low

        def put_pair(row, col, block):
            put(row, col, block)
            put(col, row, block.T)

        put(0, 0, own_ref[0, :, span(0)])
        for step in range(1, parts):
            put_pair(0, step, own_ref[0, :, span(step)])
        put(1, 1, one_ref[root, :, :width])
        put_pair(1, 3, one_ref[root, :, width : 2 * width])
        put_pair(1, 2, one_ref[root, :, 2 * width :])
        put(2, 2, two_ref[root])
        put(3, 3, three_ref[root, :, :width])
        put_pair(3, 2, three_ref[root, :, width:])

    spread(0, left_ref, high_ref, low_ref)
    spread(1, right_ref, right_high_ref, right_low_ref)
    row = lax.broadcasted_iota(jnp.int32, (width, width), 0)
    col = lax.broadcasted_iota(jnp.int32, (width, width), 1)
    z = lax.shift_right_logical(row, 2) & (parts - 1)
    source = z * (width // parts) + lax.shift_right_logical(row, 4) * 4 + (row & 3)
    order = jnp.where(col == source, 1.0, 0.0).astype(jnp.bfloat16)
    for m in range(parts):
        cols = slice(m * width, (m + 1) * width)
        left_high_ref[:, cols] = dot(high_ref[:, cols], order, nt).astype(jnp.bfloat16)
        left_low_ref[:, cols] = dot(low_ref[:, cols], order, nt).astype(jnp.bfloat16)


def spread_roots(place, left_root, right_root, others):
    _, width, order = right_root.shape
    mine = pl.BlockSpec((1, width, order), lambda i, place: (place[2], 0, 0))
    out = jax.ShapeDtypeStruct((order, order), jnp.bfloat16)
    return pl.pallas_call(
        roots_kernel,
        grid_spec=pltpu.PrefetchScalarGridSpec(
            num_scalar_prefetch=1,
            grid=(1,),
            in_specs=[mine, mine] + [whole(other.shape) for other in others],
            out_specs=[whole(out.shape)] * 4,
            scratch_shapes=[pltpu.VMEM(out.shape, out.dtype)] * 2,
        ),
        out_shape=[out] * 4,
        compiler_params=pltpu.CompilerParams(vmem_limit_bytes=32 * 1024 * 1024),
        cost_estimate=pl.CostEstimate(flops=0, bytes_accessed=5 << 20, transcendentals=0),
    )(place, left_root, right_root, *others)


def power(exponent):
    half = jnp.floor(exponent * 0.5)
    return jnp.exp2(half), jnp.exp2(exponent - half)


def coded(value):
    value = jnp.maximum(value, 1e-37)
    exponent = jnp.floor(jnp.log2(value)) + 1.0
    one, two = power(-exponent)
    share = value * one * two * 16384.0
    high = jnp.floor(share)
    return exponent, high, jnp.floor((share - high) * 16384.0)


def decoded(exponent, high, low):
    one, two = power(exponent - 14.0)
    return jnp.where(high > 0, (high + low * (1.0 / 16384.0)) * one * two, 0.0)


def square_root_code(value, top):
    root = jnp.sqrt(jnp.abs(value) * (code_top * code_top / top))
    return jnp.round(jnp.where(value < 0, -root, root)).astype(jnp.int32)


def precondition_kernel(
    place_ref, grad_ref, left_high_ref, left_low_ref, right_high_ref, right_low_ref, message_ref
):
    order = left_high_ref.shape[0]
    deep = grad_ref.shape[2] // parts
    rows = [(device, slice(m * deep, (m + 1) * deep)) for m in range(parts) for device in range(near)]
    grad = jnp.concatenate(
        [jnp.concatenate([grad_ref[device, m, at] for device, at in rows], axis=0) for m in range(parts)], axis=1
    )
    half = dot(left_high_ref[...], grad, nn) + dot(left_low_ref[...], grad, nn)
    half_high, half_low = split_two(half)
    right_high = right_high_ref[...]
    result = dot(half_high, right_high, nn) + dot(half_low, right_high, nn) + dot(half_high, right_low_ref[...], nn)
    taken = place_ref[3]
    result = jnp.where(taken > 0, result, 0.0)
    top = jnp.maximum(jnp.max(jnp.abs(result)), 1e-30)
    code = square_root_code(result, top)
    deep, width = message_ref.shape[2:]
    for z in range(far):
        for device in range(near):
            for m in range(parts):
                row = (z * near + device) * deep
                message_ref[device * parts + m, z] = code[row : row + deep, m * width : (m + 1) * width].astype(
                    jnp.int16
                )

    wide = grad.astype(jnp.float32)
    grad_sum = jnp.where(taken > 0, jnp.sum(wide * wide), 0.0)
    upd_sum = jnp.sum(result * result)
    row = lax.broadcasted_iota(jnp.int32, (8, 128), 0)
    at = lax.broadcasted_iota(jnp.int32, (8, 128), 1) - place_ref[0] * 16
    sum_at = at - place_ref[1] * 4
    top_at = at - place_ref[1] * 3
    is_up = jnp.where(taken > 1, 1, 0)
    exponent, high, low = coded(
        jnp.where(sum_at == is_up, grad_sum, jnp.where(sum_at == 2 + is_up, upd_sum, 0.0))
    )
    in_sums = (sum_at >= 0) & (sum_at < 4)
    sums = jnp.where(in_sums, jnp.where(row == 0, exponent, jnp.where(row == 1, high, low)), 0.0)
    exponent, high, low = coded(jnp.full((8, 128), top))
    in_tops = (top_at >= 0) & (top_at < 3) & (place_ref[1] < parts - 1)
    tops = jnp.where(in_tops, jnp.where(top_at == 0, exponent, jnp.where(top_at == 1, high, low)), 0.0)
    facts = jnp.where(row < 3, sums, tops)[:deep].astype(jnp.int32).astype(jnp.int16)
    for device in range(near * parts):
        message_ref[device, far] = facts


def precondition(place, landed, roots):
    _, rows, width = landed.shape
    order = near * rows
    landed = landed.reshape(near, parts, rows, width)
    message = (near * parts, far + 1, rows // far, width)
    return pl.pallas_call(
        precondition_kernel,
        grid_spec=pltpu.PrefetchScalarGridSpec(
            num_scalar_prefetch=1,
            grid=(1,),
            in_specs=[whole(landed.shape)] + [whole((order, order))] * 4,
            out_specs=whole(message),
        ),
        out_shape=jax.ShapeDtypeStruct(message, jnp.int16),
        compiler_params=pltpu.CompilerParams(vmem_limit_bytes=32 * 1024 * 1024),
        cost_estimate=pl.CostEstimate(flops=10 * order**3, bytes_accessed=4 << 20, transcendentals=0),
    )(place, landed, *roots)


def terms_kernel(place_ref, block_ref, own_ref, one_ref, two_ref, three_ref, term_ref):
    block = block_ref[...]
    out_refs = (own_ref, one_ref, two_ref, three_ref)
    width = own_ref.shape[1] - 16
    row = lax.broadcasted_iota(jnp.int32, (16, block.shape[1]), 0)
    for side in range(2):
        term = dot(block, block, nt if side == 0 else tn)
        top = jnp.maximum(jnp.max(jnp.abs(term)), 1e-30)
        term_ref[...] = square_root_code(term, top)
        exponent, high, low = coded(jnp.full(row.shape, top))
        scale = jnp.where(row == 0, exponent, jnp.where(row == 1, high, low)).astype(jnp.int32).astype(jnp.int16)
        for step in range(parts):
            at = lax.rem(place_ref[1] + step, parts)
            out_refs[step][side, :width] = term_ref[pl.ds(pl.multiple_of(at * width, width), width), :].astype(
                jnp.int16
            )
            out_refs[step][side, width:] = scale


def terms(place, block):
    order = block.shape[0]
    out = jax.ShapeDtypeStruct((2, order // parts + 16, order), jnp.int16)
    return pl.pallas_call(
        terms_kernel,
        grid_spec=pltpu.PrefetchScalarGridSpec(
            num_scalar_prefetch=1,
            grid=(1,),
            in_specs=[whole(block.shape)],
            out_specs=[whole(out.shape)] * parts,
            scratch_shapes=[pltpu.VMEM((order, order), jnp.int32)],
        ),
        out_shape=[out] * parts,
        compiler_params=pltpu.CompilerParams(vmem_limit_bytes=32 * 1024 * 1024),
        cost_estimate=pl.CostEstimate(flops=4 * order**3, bytes_accessed=2 << 20, transcendentals=0),
    )(place, block)


def stats_kernel(place_ref, own_ref, one_ref, two_ref, three_ref, left_ref, right_ref, left_new_ref, right_new_ref):
    slots, width, order = left_ref.shape
    sides = ((left_ref, left_new_ref), (right_ref, right_new_ref))
    for slot in range(slots):
        steps = lax.rem(place_ref[1] + parts - slot, parts)
        taken = place_ref[4 + slot]
        for step, terms_ref in enumerate((own_ref, one_ref, two_ref, three_ref)):

            @pl.when((steps == step) & (taken > 0))
            def _(terms_ref=terms_ref):
                for side, (old_ref, new_ref) in enumerate(sides):
                    code = terms_ref[side, :width].astype(jnp.int32).astype(jnp.float32)
                    scale = terms_ref[side, width:].astype(jnp.int32).astype(jnp.float32)
                    top = decoded(scale[0:1], scale[1:2], scale[2:3])
                    gain = top * ((1.0 - decay_rate) / order / (code_top * code_top))
                    new_ref[slot] = decay_rate * old_ref[slot] + code * jnp.abs(code) * gain

        @pl.when(taken == 0)
        def _():
            for old_ref, new_ref in sides:
                new_ref[slot] = old_ref[slot]


def new_stats(place, coded_terms, left_stats, right_stats):
    out = jax.ShapeDtypeStruct(left_stats.shape, jnp.float32)
    return pl.pallas_call(
        stats_kernel,
        grid_spec=pltpu.PrefetchScalarGridSpec(
            num_scalar_prefetch=1,
            grid=(1,),
            in_specs=[whole(coded_terms[0].shape)] * parts + [whole(out.shape)] * 2,
            out_specs=[whole(out.shape)] * 2,
        ),
        out_shape=[out] * 2,
        compiler_params=pltpu.CompilerParams(vmem_limit_bytes=32 * 1024 * 1024),
        cost_estimate=pl.CostEstimate(flops=0, bytes_accessed=5 << 20, transcendentals=0),
    )(place, *coded_terms, left_stats, right_stats)


def repack_kernel(rank_ref, back_ref, ahead_ref):
    room = ahead_ref.shape[1] - 1
    slots = rank_ref.shape[0] // near
    for device in range(near):
        for slot in range(slots):
            rank = rank_ref[device * slots + slot]

            @pl.when(rank >= 0)
            def _():
                ahead_ref[:, jnp.maximum(rank, 0)] = back_ref[device * parts + slot, :far]

    wide = [back_ref[device, far].astype(jnp.int32) for device in range(near * parts)]
    facts = functools.reduce(jnp.add, wide).astype(jnp.int16)
    for z in range(far):
        ahead_ref[z, room] = facts


def repack(ranks, back, room):
    ahead = (far, room + 1) + back.shape[2:]
    return pl.pallas_call(
        repack_kernel,
        grid_spec=pltpu.PrefetchScalarGridSpec(
            num_scalar_prefetch=1, grid=(1,), in_specs=[whole(back.shape)], out_specs=whole(ahead)
        ),
        out_shape=jax.ShapeDtypeStruct(ahead, back.dtype),
        compiler_params=pltpu.CompilerParams(vmem_limit_bytes=16 * 1024 * 1024),
        cost_estimate=pl.CostEstimate(flops=0, bytes_accessed=1 << 20, transcendentals=0),
    )(ranks, back)


def finish_kernel(at_ref, spot_ref, up_ref, arrived_ref, update_ref, factor_ref):
    room = arrived_ref.shape[1] - 1
    facts = [arrived_ref[z, room].astype(jnp.int32).astype(jnp.float32) for z in range(far)]
    row = lambda r: jnp.concatenate([fact[r : r + 1] for fact in facts], axis=0)
    sums = jnp.sum(decoded(row(0), row(1), row(2)), axis=0, keepdims=True)
    kind = lax.rem(lax.broadcasted_iota(jnp.int32, sums.shape, 1), 4)
    total = lambda k: jnp.sum(jnp.where(kind == k, sums, 0.0), axis=1, keepdims=True)
    gate_scale = jnp.sqrt(total(0) / total(2))
    up_scale = jnp.sqrt(total(1) / total(3))
    tops = row(3)
    lanes = tops.shape[1]
    steps = decoded(tops, pltpu.roll(tops, lanes - 1, 1), pltpu.roll(tops, lanes - 2, 1))
    steps = steps * (1.0 / (code_top * code_top))
    spot = spot_ref[...]
    lane = lax.broadcasted_iota(jnp.int32, spot.shape, 1)
    mine = jnp.zeros(spot.shape, jnp.float32)
    for z in range(far):
        mine += jnp.where(spot == lane + z * lanes, steps[z : z + 1], 0.0)
    step = jnp.sum(mine, axis=1, keepdims=True)
    factor_ref[...] = jnp.where(up_ref[...] > 0, up_scale, gate_scale) * step

    for b in range(update_ref.shape[0]):
        at = at_ref[b]
        code = arrived_ref[lax.div(at, room), lax.rem(at, room)].astype(jnp.int32).astype(jnp.float32)
        update_ref[b] = (code * jnp.abs(code) * factor_ref[b : b + 1, :]).astype(jnp.bfloat16)


def finish(places, spot, up, arrived):
    blocks = places.shape[0]
    return pl.pallas_call(
        finish_kernel,
        grid_spec=pltpu.PrefetchScalarGridSpec(
            num_scalar_prefetch=1,
            grid=(1,),
            in_specs=[whole(spot.shape), whole(up.shape), whole(arrived.shape)],
            out_specs=whole((blocks,) + arrived.shape[2:]),
            scratch_shapes=[pltpu.VMEM((blocks, arrived.shape[3]), jnp.float32)],
        ),
        out_shape=jax.ShapeDtypeStruct((blocks,) + arrived.shape[2:], jnp.bfloat16),
        compiler_params=pltpu.CompilerParams(vmem_limit_bytes=16 * 1024 * 1024),
        cost_estimate=pl.CostEstimate(flops=0, bytes_accessed=1 << 20, transcendentals=0),
    )(places, spot, up, arrived)


def run(room, gradient, owner_map, left_stats, right_stats, left_root, right_root):
    block_count, row_share, col_share = gradient.shape
    capacity, part_rows, block_size = left_stats.shape
    my_owner = lax.axis_index("fsdp")
    my_part = lax.axis_index("mp")

    in_plane = exchange(pack(owner_map, gradient, room), "fsdp", far_groups)

    def send(steps, k):
        slot = jnp.minimum((my_part + k) % parts, capacity - 1)

        def column(root, step):
            start = (my_part + step) % parts * part_rows
            return lax.dynamic_slice(root, (slot, 0, start), (1, part_rows, part_rows))

        rows = [jnp.concatenate([column(root, step) for step in steps], axis=2) for root in (left_root, right_root)]
        pairs = [(i, (i + k) % parts) for i in range(parts)]
        return lax.ppermute(jnp.concatenate(rows, axis=0), "mp", pairs)

    three = send((0, 3), 1)
    two = send((0,), 2)
    one = send((0, 2, 1), 3)

    cell_ids = owner_map * capacity + earlier_alike(owner_map)
    zone = owner_map // near
    rank = earlier_alike(zone)
    my_cells = my_owner // near * near * capacity + jnp.arange(near * capacity, dtype=jnp.int32)
    my_ranks = jnp.max(jnp.where(cell_ids[None, :] == my_cells[:, None], rank[None, :], -1), axis=1)
    in_plane, one, two, three, my_ranks = lax.optimization_barrier((in_plane, one, two, three, my_ranks))

    my_slot = jnp.minimum(my_part, capacity - 1)
    place = jnp.stack([my_owner % near, my_part, my_slot])
    roots = spread_roots(place, left_root, right_root, (one, two, three))

    fanned = fan(my_ranks, in_plane).reshape(near * parts, far * row_share, col_share)
    landed = exchange(fanned, ("fsdp", "mp"), plane_groups)

    up_block = jnp.arange(block_count, dtype=jnp.int32) >= block_count // 2
    my_cells = my_owner * capacity + jnp.arange(capacity, dtype=jnp.int32)
    holding = cell_ids[None, :] == my_cells[:, None]
    taken = jnp.max(jnp.where(holding, 1 + up_block.astype(jnp.int32)[None, :], 0), axis=1)
    my_taken = jnp.where(my_part < capacity, taken[my_slot], 0)
    place = jnp.concatenate([place, my_taken[None], taken])
    message = precondition(place, landed, roots)
    landed, message = lax.optimization_barrier((landed, message))
    back = exchange(message, ("fsdp", "mp"), plane_groups)

    block = landed.reshape(near, parts, far, row_share, col_share).transpose(2, 0, 3, 1, 4)
    made = terms(place, block.reshape(block_size, block_size))
    back, own_terms, *other_terms = lax.optimization_barrier((back, *made))
    coded_terms = [own_terms]
    for k, other in enumerate(other_terms, 1):
        coded_terms.append(lax.ppermute(other, "mp", [(i, (i + k) % parts) for i in range(parts)]))
    arrived = exchange(repack(my_ranks, back, room), "fsdp", far_groups)
    left_new, right_new = new_stats(place, coded_terms, left_stats, right_stats)

    spot = zone * 128 + owner_map % near * 16 + cell_ids % capacity * 3
    across = lambda array: jnp.broadcast_to(array.astype(jnp.int32)[:, None], (block_count, 128))
    update = finish(zone * room + rank, across(spot), across(up_block), arrived)
    return (update, left_new, right_new)


def on_device(gradient, owner_map, *rest):
    slots = near * rest[0].shape[0]
    room = slots * 2 // 3
    zone = owner_map // near
    held = jnp.sum((zone[None, :] == jnp.arange(far, dtype=jnp.int32)[:, None]).astype(jnp.int32), axis=1)
    return lax.cond(
        jnp.max(held) <= room,
        functools.partial(run, room),
        functools.partial(run, slots),
        gradient,
        owner_map,
        *rest,
    )


def solution(mesh):
    placed = (
        P(None, "fsdp", "mp"),
        P(),
        P("fsdp", "mp", None),
        P("fsdp", "mp", None),
        P("fsdp", "mp", None),
        P("fsdp", "mp", None),
    )
    return jax.shard_map(
        on_device,
        mesh=mesh,
        in_specs=placed,
        out_specs=(P(None, "fsdp", "mp"), P("fsdp", "mp", None), P("fsdp", "mp", None)),
        check_vma=False,
    )
```

```python
import functools

import jax
import jax.numpy as jnp
from jax import lax
from jax.experimental import pallas as pl
from jax.experimental.pallas import tpu as pltpu
from jax.sharding import PartitionSpec as P

decay_rate = 0.95
code_top = 32767.0
parts = 4
near = 8
far = 16


def cell_index(owner_map, capacity):
    total_rows = owner_map.shape[0]
    positions = jnp.arange(total_rows, dtype=jnp.int32)
    same_owner = owner_map[None, :] == owner_map[:, None]
    earlier = positions[None, :] < positions[:, None]
    ranks = jnp.sum((same_owner & earlier).astype(jnp.int32), axis=1)
    return owner_map * capacity + ranks


far_groups = [[z * near + n for z in range(far)] for n in range(near)]
plane_groups = [[(z * near + n) * parts + m for n in range(near) for m in range(parts)] for z in range(far)]


def exchange(array, axis_name, groups):
    return lax.all_to_all(
        array, axis_name, split_axis=0, concat_axis=0, axis_index_groups=groups, tiled=True
    )


def split_two(array):
    high = array.astype(jnp.bfloat16)
    return high, (array - high.astype(jnp.float32)).astype(jnp.bfloat16)


tn = (((0,), (0,)), ((), ()))
nn = (((1,), (0,)), ((), ()))
nt = (((1,), (1,)), ((), ()))
dot = functools.partial(lax.dot_general, preferred_element_type=jnp.float32)


def pack_kernel(owner_ref, far_grad_ref, packed_ref, count_ref, grad_ref, sem):
    blocks = grad_ref.shape[0]
    slots = packed_ref.shape[0] // blocks
    copy = pltpu.make_async_copy(far_grad_ref, grad_ref, sem)
    copy.start()
    packed_ref[...] = jnp.zeros_like(packed_ref)
    for owner in range(blocks):
        count_ref[owner] = 0
    copy.wait()
    for b in range(blocks):
        owner = owner_ref[b]
        rank = count_ref[owner]
        count_ref[owner] = rank + 1
        packed_ref[owner * slots + rank] = grad_ref[b]


def pack(owner_map, gradient, slots):
    blocks = gradient.shape[0]
    packed = (blocks * slots,) + gradient.shape[1:]
    return pl.pallas_call(
        pack_kernel,
        grid_spec=pltpu.PrefetchScalarGridSpec(
            num_scalar_prefetch=1,
            grid=(1,),
            in_specs=[pl.BlockSpec(memory_space=pltpu.HBM)],
            out_specs=whole(packed),
            scratch_shapes=[
                pltpu.SMEM((blocks,), jnp.int32),
                pltpu.VMEM(gradient.shape, gradient.dtype),
                pltpu.SemaphoreType.DMA,
            ],
        ),
        out_shape=jax.ShapeDtypeStruct(packed, gradient.dtype),
        compiler_params=pltpu.CompilerParams(vmem_limit_bytes=16 * 1024 * 1024),
        cost_estimate=pl.CostEstimate(flops=0, bytes_accessed=1 << 20, transcendentals=0),
    )(pltpu.with_memory_space_constraint(owner_map, pltpu.HBM), pltpu.with_memory_space_constraint(gradient, pltpu.HBM))


def fan_kernel(plane_ref, fan_ref):
    for n in range(near):
        for slot in range(parts):
            if slot < plane_ref.shape[2]:
                fan_ref[n, slot] = plane_ref[:, n, slot]
            else:
                fan_ref[n, slot] = jnp.zeros(fan_ref.shape[2:], fan_ref.dtype)


def fan(in_plane):
    _, _, slots, rows, width = in_plane.shape
    return pl.pallas_call(
        fan_kernel,
        out_shape=jax.ShapeDtypeStruct((near, parts, far, rows, width), in_plane.dtype),
        in_specs=[pl.BlockSpec(memory_space=pltpu.VMEM)],
        out_specs=pl.BlockSpec(memory_space=pltpu.VMEM),
        compiler_params=pltpu.CompilerParams(vmem_limit_bytes=16 * 1024 * 1024),
        cost_estimate=pl.CostEstimate(flops=0, bytes_accessed=1 << 20, transcendentals=0),
    )(in_plane)


def roots_kernel(
    place_ref, left_ref, right_ref, one_ref, two_ref, three_ref,
    left_high_ref, left_low_ref, right_high_ref, right_low_ref, high_ref, low_ref,
):
    part = place_ref[1]
    width = left_ref.shape[1]

    def span(step):
        at = lax.rem(part + step, parts)
        return pl.ds(pl.multiple_of(at * width, width), width)

    def spread(root, own_ref, high_ref, low_ref):
        def put(row, col, block):
            high, low = split_two(block)
            high_ref[span(row), span(col)] = high
            low_ref[span(row), span(col)] = low

        def put_pair(row, col, block):
            put(row, col, block)
            put(col, row, block.T)

        put(0, 0, own_ref[0, :, span(0)])
        for step in range(1, parts):
            put_pair(0, step, own_ref[0, :, span(step)])
        put(1, 1, one_ref[root, :, :width])
        put_pair(1, 3, one_ref[root, :, width : 2 * width])
        put_pair(1, 2, one_ref[root, :, 2 * width :])
        put(2, 2, two_ref[root])
        put(3, 3, three_ref[root, :, :width])
        put_pair(3, 2, three_ref[root, :, width:])

    spread(0, left_ref, high_ref, low_ref)
    spread(1, right_ref, right_high_ref, right_low_ref)
    size = high_ref.shape[0]
    row = lax.broadcasted_iota(jnp.int32, (size, size), 0)
    col = lax.broadcasted_iota(jnp.int32, (size, size), 1)
    z = lax.shift_right_logical(row, 2) & (far - 1)
    source = z * (size // far) + lax.shift_right_logical(row, 6) * 4 + (row & 3)
    order = jnp.where(col == source, 1.0, 0.0).astype(jnp.bfloat16)
    left_high_ref[...] = dot(high_ref[...], order, nt).astype(jnp.bfloat16)
    left_low_ref[...] = dot(low_ref[...], order, nt).astype(jnp.bfloat16)


def whole(shape):
    return pl.BlockSpec(shape, lambda i, *_: (0,) * len(shape))


def spread_roots(place, left_root, right_root, others):
    _, width, order = right_root.shape
    mine = pl.BlockSpec((1, width, order), lambda i, place: (place[2], 0, 0))
    out = jax.ShapeDtypeStruct((order, order), jnp.bfloat16)
    return pl.pallas_call(
        roots_kernel,
        grid_spec=pltpu.PrefetchScalarGridSpec(
            num_scalar_prefetch=1,
            grid=(1,),
            in_specs=[mine, mine] + [whole(other.shape) for other in others],
            out_specs=[whole(out.shape)] * 4,
            scratch_shapes=[pltpu.VMEM(out.shape, out.dtype)] * 2,
        ),
        out_shape=[out] * 4,
        compiler_params=pltpu.CompilerParams(vmem_limit_bytes=32 * 1024 * 1024),
        cost_estimate=pl.CostEstimate(flops=0, bytes_accessed=5 << 20, transcendentals=0),
    )(place, left_root, right_root, *others)


def power(exponent):
    half = jnp.floor(exponent * 0.5)
    return jnp.exp2(half), jnp.exp2(exponent - half)


def coded(value):
    value = jnp.maximum(value, 1e-37)
    exponent = jnp.floor(jnp.log2(value)) + 1.0
    one, two = power(-exponent)
    share = value * one * two * 16384.0
    high = jnp.floor(share)
    return exponent, high, jnp.floor((share - high) * 16384.0)


def decoded(exponent, high, low):
    one, two = power(exponent - 14.0)
    return jnp.where(high > 0, (high + low * (1.0 / 16384.0)) * one * two, 0.0)


def square_root_code(value, top):
    root = jnp.sqrt(jnp.abs(value) * (code_top * code_top / top))
    return jnp.round(jnp.where(value < 0, -root, root)).astype(jnp.int32)


def precondition_kernel(
    place_ref, grad_ref, left_high_ref, left_low_ref, right_high_ref, right_low_ref, message_ref, late_ref, sem
):
    order = left_high_ref.shape[0]
    late = pltpu.make_async_copy(right_low_ref, late_ref, sem)
    late.start()
    grad = jnp.concatenate([grad_ref[:, m].reshape(order, -1) for m in range(parts)], axis=1)
    half = dot(left_high_ref[...], grad, nn) + dot(left_low_ref[...], grad, nn)
    half_high, half_low = split_two(half)
    right_high = right_high_ref[...]
    result = dot(half_high, right_high, nn) + dot(half_low, right_high, nn)
    late.wait()
    result += dot(half_high, late_ref[...], nn)
    taken = place_ref[3]
    result = jnp.where(taken > 0, result, 0.0)
    top = jnp.maximum(jnp.max(jnp.abs(result)), 1e-30)
    code = square_root_code(result, top)
    deep, width = message_ref.shape[2:]
    for z in range(far):
        for device in range(near):
            for m in range(parts):
                row = (z * near + device) * deep
                message_ref[device * parts + m, z] = code[row : row + deep, m * width : (m + 1) * width].astype(
                    jnp.int16
                )

    wide = grad.astype(jnp.float32)
    grad_sum = jnp.where(taken > 0, jnp.sum(wide * wide), 0.0)
    upd_sum = jnp.sum(result * result)
    row = lax.broadcasted_iota(jnp.int32, (8, 128), 0)
    at = lax.broadcasted_iota(jnp.int32, (8, 128), 1) - place_ref[0] * 16
    sum_at = at - place_ref[1] * 4
    top_at = at - place_ref[1] * 3
    is_up = jnp.where(taken > 1, 1, 0)
    exponent, high, low = coded(
        jnp.where(sum_at == is_up, grad_sum, jnp.where(sum_at == 2 + is_up, upd_sum, 0.0))
    )
    in_sums = (sum_at >= 0) & (sum_at < 4)
    sums = jnp.where(in_sums, jnp.where(row == 0, exponent, jnp.where(row == 1, high, low)), 0.0)
    exponent, high, low = coded(jnp.full((8, 128), top))
    in_tops = (top_at >= 0) & (top_at < 3) & (place_ref[1] < parts - 1)
    tops = jnp.where(in_tops, jnp.where(top_at == 0, exponent, jnp.where(top_at == 1, high, low)), 0.0)
    facts = jnp.where(row < 3, sums, tops)[:deep].astype(jnp.int32).astype(jnp.int16)
    for device in range(near * parts):
        message_ref[device, far] = facts


def precondition(place, landed, roots):
    _, rows, width = landed.shape
    order = near * rows
    landed = landed.reshape(near, parts, rows, width)
    message = (near * parts, far + 1, rows // far, width)
    return pl.pallas_call(
        precondition_kernel,
        grid_spec=pltpu.PrefetchScalarGridSpec(
            num_scalar_prefetch=1,
            grid=(1,),
            in_specs=[whole(landed.shape)] + [whole((order, order))] * 3 + [pl.BlockSpec(memory_space=pltpu.HBM)],
            out_specs=whole(message),
            scratch_shapes=[pltpu.VMEM((order, order), jnp.bfloat16), pltpu.SemaphoreType.DMA],
        ),
        out_shape=jax.ShapeDtypeStruct(message, jnp.int16),
        compiler_params=pltpu.CompilerParams(vmem_limit_bytes=32 * 1024 * 1024),
        cost_estimate=pl.CostEstimate(flops=10 * order**3, bytes_accessed=4 << 20, transcendentals=0),
    )(place, landed, *roots[:3], pltpu.with_memory_space_constraint(roots[3], pltpu.HBM))


def terms_kernel(place_ref, block_ref, own_ref, one_ref, two_ref, three_ref, term_ref):
    block = block_ref[...]
    out_refs = (own_ref, one_ref, two_ref, three_ref)
    width = own_ref.shape[1] - 16
    row = lax.broadcasted_iota(jnp.int32, (16, block.shape[1]), 0)
    for side in range(2):
        term = dot(block, block, nt if side == 0 else tn)
        top = jnp.maximum(jnp.max(jnp.abs(term)), 1e-30)
        term_ref[...] = square_root_code(term, top)
        exponent, high, low = coded(jnp.full(row.shape, top))
        scale = jnp.where(row == 0, exponent, jnp.where(row == 1, high, low)).astype(jnp.int32).astype(jnp.int16)
        for step in range(parts):
            at = lax.rem(place_ref[1] + step, parts)
            out_refs[step][side, :width] = term_ref[pl.ds(pl.multiple_of(at * width, width), width), :].astype(
                jnp.int16
            )
            out_refs[step][side, width:] = scale


def terms(place, block):
    order = block.shape[0]
    out = jax.ShapeDtypeStruct((2, order // parts + 16, order), jnp.int16)
    return pl.pallas_call(
        terms_kernel,
        grid_spec=pltpu.PrefetchScalarGridSpec(
            num_scalar_prefetch=1,
            grid=(1,),
            in_specs=[whole(block.shape)],
            out_specs=[whole(out.shape)] * parts,
            scratch_shapes=[pltpu.VMEM((order, order), jnp.int32)],
        ),
        out_shape=[out] * parts,
        compiler_params=pltpu.CompilerParams(vmem_limit_bytes=32 * 1024 * 1024),
        cost_estimate=pl.CostEstimate(flops=4 * order**3, bytes_accessed=2 << 20, transcendentals=0),
    )(place, block)


def stats_kernel(place_ref, own_ref, one_ref, two_ref, three_ref, left_ref, right_ref, left_new_ref, right_new_ref):
    slots, width, order = left_ref.shape
    sides = ((left_ref, left_new_ref), (right_ref, right_new_ref))
    for slot in range(slots):
        steps = lax.rem(place_ref[1] + parts - slot, parts)
        taken = place_ref[4 + slot]
        for step, terms_ref in enumerate((own_ref, one_ref, two_ref, three_ref)):

            @pl.when((steps == step) & (taken > 0))
            def _(terms_ref=terms_ref):
                for side, (old_ref, new_ref) in enumerate(sides):
                    code = terms_ref[side, :width].astype(jnp.int32).astype(jnp.float32)
                    scale = terms_ref[side, width:].astype(jnp.int32).astype(jnp.float32)
                    top = decoded(scale[0:1], scale[1:2], scale[2:3])
                    gain = top * ((1.0 - decay_rate) / order / (code_top * code_top))
                    new_ref[slot] = decay_rate * old_ref[slot] + code * jnp.abs(code) * gain

        @pl.when(taken == 0)
        def _():
            for old_ref, new_ref in sides:
                new_ref[slot] = old_ref[slot]


def new_stats(place, coded_terms, left_stats, right_stats):
    out = jax.ShapeDtypeStruct(left_stats.shape, jnp.float32)
    return pl.pallas_call(
        stats_kernel,
        grid_spec=pltpu.PrefetchScalarGridSpec(
            num_scalar_prefetch=1,
            grid=(1,),
            in_specs=[whole(coded_terms[0].shape)] * parts + [whole(out.shape)] * 2,
            out_specs=[whole(out.shape)] * 2,
        ),
        out_shape=[out] * 2,
        compiler_params=pltpu.CompilerParams(vmem_limit_bytes=32 * 1024 * 1024),
        cost_estimate=pl.CostEstimate(flops=0, bytes_accessed=5 << 20, transcendentals=0),
    )(place, *coded_terms, left_stats, right_stats)


def repack_kernel(back_ref, ahead_ref):
    cells = ahead_ref.shape[1] - 1
    slots = cells // near
    for device in range(near):
        for slot in range(slots):
            ahead_ref[:, device * slots + slot] = back_ref[device * parts + slot, :far]
    wide = [back_ref[device, far].astype(jnp.int32) for device in range(near * parts)]
    facts = functools.reduce(jnp.add, wide).astype(jnp.int16)
    for z in range(far):
        ahead_ref[z, cells] = facts


def repack(back, slots):
    return pl.pallas_call(
        repack_kernel,
        out_shape=jax.ShapeDtypeStruct((far, near * slots + 1) + back.shape[2:], back.dtype),
        in_specs=[pl.BlockSpec(memory_space=pltpu.VMEM)],
        out_specs=pl.BlockSpec(memory_space=pltpu.VMEM),
        compiler_params=pltpu.CompilerParams(vmem_limit_bytes=16 * 1024 * 1024),
        cost_estimate=pl.CostEstimate(flops=0, bytes_accessed=1 << 20, transcendentals=0),
    )(back)


def finish_kernel(at_ref, spot_ref, up_ref, arrived_ref, update_ref, factor_ref):
    cells = arrived_ref.shape[1] - 1
    facts = [arrived_ref[z, cells].astype(jnp.int32).astype(jnp.float32) for z in range(far)]
    row = lambda r: jnp.concatenate([fact[r : r + 1] for fact in facts], axis=0)
    sums = jnp.sum(decoded(row(0), row(1), row(2)), axis=0, keepdims=True)
    kind = lax.rem(lax.broadcasted_iota(jnp.int32, sums.shape, 1), 4)
    total = lambda k: jnp.sum(jnp.where(kind == k, sums, 0.0), axis=1, keepdims=True)
    gate_scale = jnp.sqrt(total(0) / total(2))
    up_scale = jnp.sqrt(total(1) / total(3))
    tops = row(3)
    lanes = tops.shape[1]
    steps = decoded(tops, pltpu.roll(tops, lanes - 1, 1), pltpu.roll(tops, lanes - 2, 1))
    steps = steps * (1.0 / (code_top * code_top))
    spot = spot_ref[...]
    lane = lax.broadcasted_iota(jnp.int32, spot.shape, 1)
    mine = jnp.zeros(spot.shape, jnp.float32)
    for z in range(far):
        mine += jnp.where(spot == lane + z * lanes, steps[z : z + 1], 0.0)
    step = jnp.sum(mine, axis=1, keepdims=True)
    factor_ref[...] = jnp.where(up_ref[...] > 0, up_scale, gate_scale) * step

    for b in range(update_ref.shape[0]):
        at = at_ref[b]
        code = arrived_ref[at // cells, lax.rem(at, cells)].astype(jnp.int32).astype(jnp.float32)
        update_ref[b] = (code * jnp.abs(code) * factor_ref[b : b + 1, :]).astype(jnp.bfloat16)


def finish(cell_ids, spot, up, arrived):
    blocks = cell_ids.shape[0]
    return pl.pallas_call(
        finish_kernel,
        grid_spec=pltpu.PrefetchScalarGridSpec(
            num_scalar_prefetch=1,
            grid=(1,),
            in_specs=[whole(spot.shape), whole(up.shape), whole(arrived.shape)],
            out_specs=whole((blocks,) + arrived.shape[2:]),
            scratch_shapes=[pltpu.VMEM((blocks, arrived.shape[3]), jnp.float32)],
        ),
        out_shape=jax.ShapeDtypeStruct((blocks,) + arrived.shape[2:], jnp.bfloat16),
        compiler_params=pltpu.CompilerParams(vmem_limit_bytes=16 * 1024 * 1024),
        cost_estimate=pl.CostEstimate(flops=0, bytes_accessed=1 << 20, transcendentals=0),
    )(cell_ids, spot, up, arrived)


def on_device(gradient, owner_map, left_stats, right_stats, left_root, right_root):
    block_count, row_share, col_share = gradient.shape
    capacity, part_rows, block_size = left_stats.shape
    my_owner = lax.axis_index("fsdp")
    my_part = lax.axis_index("mp")

    packed = pack(owner_map, gradient, capacity).reshape(far, near, capacity, row_share, col_share)
    in_plane = exchange(packed, "fsdp", far_groups)

    def send(steps, k):
        slot = jnp.minimum((my_part + k) % parts, capacity - 1)

        def column(root, step):
            start = (my_part + step) % parts * part_rows
            return lax.dynamic_slice(root, (slot, 0, start), (1, part_rows, part_rows))

        rows = [jnp.concatenate([column(root, step) for step in steps], axis=2) for root in (left_root, right_root)]
        pairs = [(i, (i + k) % parts) for i in range(parts)]
        return lax.ppermute(jnp.concatenate(rows, axis=0), "mp", pairs)

    three = send((0, 3), 1)
    two = send((0,), 2)
    one = send((0, 2, 1), 3)
    my_slot = jnp.minimum(my_part, capacity - 1)
    place = jnp.stack([my_owner % near, my_part, my_slot])
    roots = spread_roots(place, left_root, right_root, (one, two, three))
    in_plane, owner_map, *roots = lax.optimization_barrier((in_plane, owner_map, *roots))

    fanned = fan(in_plane).reshape(near * parts, far * row_share, col_share)
    landed = exchange(fanned, ("fsdp", "mp"), plane_groups)

    cell_ids = cell_index(owner_map, capacity)
    up_block = jnp.arange(block_count, dtype=jnp.int32) >= block_count // 2
    my_cells = my_owner * capacity + jnp.arange(capacity, dtype=jnp.int32)
    holding = cell_ids[None, :] == my_cells[:, None]
    taken = jnp.max(jnp.where(holding, 1 + up_block.astype(jnp.int32)[None, :], 0), axis=1)
    my_taken = jnp.where(my_part < capacity, taken[my_slot], 0)
    place = jnp.concatenate([place, my_taken[None], taken])
    message = precondition(place, landed, roots)
    landed, message = lax.optimization_barrier((landed, message))
    back = exchange(message, ("fsdp", "mp"), plane_groups)

    block = landed.reshape(near, parts, far, row_share, col_share).transpose(2, 0, 3, 1, 4)
    own_terms, *made = terms(place, block.reshape(block_size, block_size))
    send_on = lambda k: lax.ppermute(made[k - 1], "mp", [(i, (i + k) % parts) for i in range(parts)])
    back, *made[1:], own_terms, next_terms = lax.optimization_barrier((back, *made[1:], own_terms, send_on(1)))
    coded_terms = [own_terms, next_terms] + [send_on(k) for k in range(2, parts)]
    arrived = exchange(repack(back, capacity), "fsdp", far_groups)
    left_new, right_new = new_stats(place, coded_terms, left_stats, right_stats)

    cells = near * capacity
    spot = cell_ids // cells * 128 + cell_ids % cells // capacity * 16 + cell_ids % capacity * 3
    across = lambda array: jnp.broadcast_to(array.astype(jnp.int32)[:, None], (block_count, 128))
    update = finish(cell_ids, across(spot), across(up_block), arrived)
    return (update, left_new, right_new)


def solution(mesh):
    placed = (
        P(None, "fsdp", "mp"),
        P(),
        P("fsdp", "mp", None),
        P("fsdp", "mp", None),
        P("fsdp", "mp", None),
        P("fsdp", "mp", None),
    )
    return jax.shard_map(
        on_device,
        mesh=mesh,
        in_specs=placed,
        out_specs=(P(None, "fsdp", "mp"), P("fsdp", "mp", None), P("fsdp", "mp", None)),
        check_vma=False,
    )
```

```python
import functools

import jax
import jax.numpy as jnp
from jax import lax
from jax.experimental import pallas as pl
from jax.experimental.pallas import tpu as pltpu
from jax.sharding import PartitionSpec as P

decay_rate = 0.95
code_top = 32767.0
parts = 4
near = 8
far = 16


def cell_index(owner_map, capacity):
    total_rows = owner_map.shape[0]
    positions = jnp.arange(total_rows, dtype=jnp.int32)
    same_owner = owner_map[None, :] == owner_map[:, None]
    earlier = positions[None, :] < positions[:, None]
    ranks = jnp.sum((same_owner & earlier).astype(jnp.int32), axis=1)
    return owner_map * capacity + ranks


far_groups = [[z * near + n for z in range(far)] for n in range(near)]
plane_groups = [[(z * near + n) * parts + m for n in range(near) for m in range(parts)] for z in range(far)]


def exchange(array, axis_name, groups):
    return lax.all_to_all(
        array, axis_name, split_axis=0, concat_axis=0, axis_index_groups=groups, tiled=True
    )


def split_two(array):
    high = array.astype(jnp.bfloat16)
    return high, (array - high.astype(jnp.float32)).astype(jnp.bfloat16)


tn = (((0,), (0,)), ((), ()))
nn = (((1,), (0,)), ((), ()))
nt = (((1,), (1,)), ((), ()))
dot = functools.partial(lax.dot_general, preferred_element_type=jnp.float32)


def pack_kernel(owner_ref, far_grad_ref, packed_ref, count_ref, grad_ref, sem):
    blocks = grad_ref.shape[0]
    slots = packed_ref.shape[0] // blocks
    copy = pltpu.make_async_copy(far_grad_ref, grad_ref, sem)
    copy.start()
    packed_ref[...] = jnp.zeros_like(packed_ref)
    for owner in range(blocks):
        count_ref[owner] = 0
    copy.wait()
    for b in range(blocks):
        owner = owner_ref[b]
        rank = count_ref[owner]
        count_ref[owner] = rank + 1
        packed_ref[owner * slots + rank] = grad_ref[b]


def pack(owner_map, gradient, slots):
    blocks = gradient.shape[0]
    packed = (blocks * slots,) + gradient.shape[1:]
    return pl.pallas_call(
        pack_kernel,
        grid_spec=pltpu.PrefetchScalarGridSpec(
            num_scalar_prefetch=1,
            grid=(1,),
            in_specs=[pl.BlockSpec(memory_space=pltpu.HBM)],
            out_specs=whole(packed),
            scratch_shapes=[
                pltpu.SMEM((blocks,), jnp.int32),
                pltpu.VMEM(gradient.shape, gradient.dtype),
                pltpu.SemaphoreType.DMA,
            ],
        ),
        out_shape=jax.ShapeDtypeStruct(packed, gradient.dtype),
        compiler_params=pltpu.CompilerParams(vmem_limit_bytes=16 * 1024 * 1024),
        cost_estimate=pl.CostEstimate(flops=0, bytes_accessed=1 << 20, transcendentals=0),
    )(pltpu.with_memory_space_constraint(owner_map, pltpu.HBM), pltpu.with_memory_space_constraint(gradient, pltpu.HBM))


def fan_kernel(plane_ref, fan_ref):
    for n in range(near):
        for slot in range(parts):
            if slot < plane_ref.shape[2]:
                fan_ref[n, slot] = plane_ref[:, n, slot]
            else:
                fan_ref[n, slot] = jnp.zeros(fan_ref.shape[2:], fan_ref.dtype)


def fan(in_plane):
    _, _, slots, rows, width = in_plane.shape
    return pl.pallas_call(
        fan_kernel,
        out_shape=jax.ShapeDtypeStruct((near, parts, far, rows, width), in_plane.dtype),
        in_specs=[pl.BlockSpec(memory_space=pltpu.VMEM)],
        out_specs=pl.BlockSpec(memory_space=pltpu.VMEM),
        compiler_params=pltpu.CompilerParams(vmem_limit_bytes=16 * 1024 * 1024),
        cost_estimate=pl.CostEstimate(flops=0, bytes_accessed=1 << 20, transcendentals=0),
    )(in_plane)


def roots_kernel(
    place_ref, left_ref, right_ref, one_ref, two_ref, three_ref,
    left_high_ref, left_low_ref, right_high_ref, right_low_ref, high_ref, low_ref,
):
    part = place_ref[1]
    width = left_ref.shape[1]

    def span(step):
        at = lax.rem(part + step, parts)
        return pl.ds(pl.multiple_of(at * width, width), width)

    def spread(root, own_ref, high_ref, low_ref):
        def put(row, col, block):
            high, low = split_two(block)
            high_ref[span(row), span(col)] = high
            low_ref[span(row), span(col)] = low

        def put_pair(row, col, block):
            put(row, col, block)
            put(col, row, block.T)

        put(0, 0, own_ref[0, :, span(0)])
        for step in range(1, parts):
            put_pair(0, step, own_ref[0, :, span(step)])
        put(1, 1, one_ref[root, :, :width])
        put_pair(1, 3, one_ref[root, :, width : 2 * width])
        put_pair(1, 2, one_ref[root, :, 2 * width :])
        put(2, 2, two_ref[root])
        put(3, 3, three_ref[root, :, :width])
        put_pair(3, 2, three_ref[root, :, width:])

    spread(0, left_ref, high_ref, low_ref)
    spread(1, right_ref, right_high_ref, right_low_ref)
    size = high_ref.shape[0]
    row = lax.broadcasted_iota(jnp.int32, (size, size), 0)
    col = lax.broadcasted_iota(jnp.int32, (size, size), 1)
    z = lax.shift_right_logical(row, 2) & (far - 1)
    source = z * (size // far) + lax.shift_right_logical(row, 6) * 4 + (row & 3)
    order = jnp.where(col == source, 1.0, 0.0).astype(jnp.bfloat16)
    left_high_ref[...] = dot(high_ref[...], order, nt).astype(jnp.bfloat16)
    left_low_ref[...] = dot(low_ref[...], order, nt).astype(jnp.bfloat16)


in_vmem = pl.BlockSpec(memory_space=pltpu.VMEM)
in_smem = pl.BlockSpec(memory_space=pltpu.SMEM)


def whole(shape):
    return pl.BlockSpec(shape, lambda i, *_: (0,) * len(shape))


def spread_roots(place, left_root, right_root, others):
    _, width, order = right_root.shape
    mine = pl.BlockSpec((1, width, order), lambda i, place: (place[2], 0, 0))
    out = jax.ShapeDtypeStruct((order, order), jnp.bfloat16)
    return pl.pallas_call(
        roots_kernel,
        grid_spec=pltpu.PrefetchScalarGridSpec(
            num_scalar_prefetch=1,
            grid=(1,),
            in_specs=[mine, mine] + [whole(other.shape) for other in others],
            out_specs=[whole(out.shape)] * 4,
            scratch_shapes=[pltpu.VMEM(out.shape, out.dtype)] * 2,
        ),
        out_shape=[out] * 4,
        compiler_params=pltpu.CompilerParams(vmem_limit_bytes=32 * 1024 * 1024),
        cost_estimate=pl.CostEstimate(flops=0, bytes_accessed=5 << 20, transcendentals=0),
    )(place, left_root, right_root, *others)


def power(exponent):
    half = jnp.floor(exponent * 0.5)
    return jnp.exp2(half), jnp.exp2(exponent - half)


def coded(value):
    value = jnp.maximum(value, 1e-37)
    exponent = jnp.floor(jnp.log2(value)) + 1.0
    one, two = power(-exponent)
    share = value * one * two * 16384.0
    high = jnp.floor(share)
    return exponent, high, jnp.floor((share - high) * 16384.0)


def decoded(exponent, high, low):
    one, two = power(exponent - 14.0)
    return jnp.where(high > 0, (high + low * (1.0 / 16384.0)) * one * two, 0.0)


def square_root_code(value, top):
    root = jnp.sqrt(jnp.abs(value) * (code_top * code_top / top))
    return jnp.round(jnp.where(value < 0, -root, root)).astype(jnp.int32)


def precondition_kernel(
    place_ref, grad_ref, left_high_ref, left_low_ref, right_high_ref, right_low_ref, message_ref, late_ref, sem
):
    order = left_high_ref.shape[0]
    late = pltpu.make_async_copy(right_low_ref, late_ref, sem)
    late.start()
    grad = jnp.concatenate([grad_ref[:, m].reshape(order, -1) for m in range(parts)], axis=1)
    half = dot(left_high_ref[...], grad, nn) + dot(left_low_ref[...], grad, nn)
    half_high, half_low = split_two(half)
    right_high = right_high_ref[...]
    result = dot(half_high, right_high, nn) + dot(half_low, right_high, nn)
    late.wait()
    result += dot(half_high, late_ref[...], nn)
    taken = place_ref[3]
    result = jnp.where(taken > 0, result, 0.0)
    top = jnp.maximum(jnp.max(jnp.abs(result)), 1e-30)
    code = square_root_code(result, top)
    deep, width = message_ref.shape[2:]
    for z in range(far):
        for device in range(near):
            for m in range(parts):
                row = (z * near + device) * deep
                message_ref[device * parts + m, z] = code[row : row + deep, m * width : (m + 1) * width].astype(
                    jnp.int16
                )

    wide = grad.astype(jnp.float32)
    grad_sum = jnp.where(taken > 0, jnp.sum(wide * wide), 0.0)
    upd_sum = jnp.sum(result * result)
    row = lax.broadcasted_iota(jnp.int32, (8, 128), 0)
    at = lax.broadcasted_iota(jnp.int32, (8, 128), 1) - place_ref[0] * 16
    sum_at = at - place_ref[1] * 4
    top_at = at - place_ref[1] * 3
    is_up = jnp.where(taken > 1, 1, 0)
    exponent, high, low = coded(
        jnp.where(sum_at == is_up, grad_sum, jnp.where(sum_at == 2 + is_up, upd_sum, 0.0))
    )
    in_sums = (sum_at >= 0) & (sum_at < 4)
    sums = jnp.where(in_sums, jnp.where(row == 0, exponent, jnp.where(row == 1, high, low)), 0.0)
    exponent, high, low = coded(jnp.full((8, 128), top))
    in_tops = (top_at >= 0) & (top_at < 3) & (place_ref[1] < parts - 1)
    tops = jnp.where(in_tops, jnp.where(top_at == 0, exponent, jnp.where(top_at == 1, high, low)), 0.0)
    facts = jnp.where(row < 3, sums, tops)[:deep].astype(jnp.int32).astype(jnp.int16)
    for device in range(near * parts):
        message_ref[device, far] = facts


def precondition(place, landed, roots):
    _, rows, width = landed.shape
    order = near * rows
    landed = landed.reshape(near, parts, rows, width)
    message = (near * parts, far + 1, rows // far, width)
    return pl.pallas_call(
        precondition_kernel,
        in_specs=[in_smem] + [in_vmem] * 4 + [pl.BlockSpec(memory_space=pltpu.HBM)],
        out_specs=in_vmem,
        scratch_shapes=[pltpu.VMEM((order, order), jnp.bfloat16), pltpu.SemaphoreType.DMA],
        out_shape=jax.ShapeDtypeStruct(message, jnp.int16),
        compiler_params=pltpu.CompilerParams(vmem_limit_bytes=32 * 1024 * 1024),
        cost_estimate=pl.CostEstimate(flops=10 * order**3, bytes_accessed=4 << 20, transcendentals=0),
    )(place, landed, *roots[:3], pltpu.with_memory_space_constraint(roots[3], pltpu.HBM))


def terms_kernel(place_ref, block_ref, own_ref, one_ref, two_ref, three_ref, term_ref):
    block = block_ref[...]
    out_refs = (own_ref, one_ref, two_ref, three_ref)
    width = own_ref.shape[1] - 16
    row = lax.broadcasted_iota(jnp.int32, (16, block.shape[1]), 0)
    for side in range(2):
        term = dot(block, block, nt if side == 0 else tn)
        top = jnp.maximum(jnp.max(jnp.abs(term)), 1e-30)
        term_ref[...] = square_root_code(term, top)
        exponent, high, low = coded(jnp.full(row.shape, top))
        scale = jnp.where(row == 0, exponent, jnp.where(row == 1, high, low)).astype(jnp.int32).astype(jnp.int16)
        for step in range(parts):
            at = lax.rem(place_ref[1] + step, parts)
            out_refs[step][side, :width] = term_ref[pl.ds(pl.multiple_of(at * width, width), width), :].astype(
                jnp.int16
            )
            out_refs[step][side, width:] = scale


def terms(place, block):
    order = block.shape[0]
    out = jax.ShapeDtypeStruct((2, order // parts + 16, order), jnp.int16)
    return pl.pallas_call(
        terms_kernel,
        grid_spec=pltpu.PrefetchScalarGridSpec(
            num_scalar_prefetch=1,
            grid=(1,),
            in_specs=[whole(block.shape)],
            out_specs=[whole(out.shape)] * parts,
            scratch_shapes=[pltpu.VMEM((order, order), jnp.int32)],
        ),
        out_shape=[out] * parts,
        compiler_params=pltpu.CompilerParams(vmem_limit_bytes=32 * 1024 * 1024),
        cost_estimate=pl.CostEstimate(flops=4 * order**3, bytes_accessed=2 << 20, transcendentals=0),
    )(place, block)


def stats_kernel(place_ref, own_ref, one_ref, two_ref, three_ref, left_ref, right_ref, left_new_ref, right_new_ref):
    slots, width, order = left_ref.shape
    sides = ((left_ref, left_new_ref), (right_ref, right_new_ref))
    for slot in range(slots):
        steps = lax.rem(place_ref[1] + parts - slot, parts)
        taken = place_ref[4 + slot]
        for step, terms_ref in enumerate((own_ref, one_ref, two_ref, three_ref)):

            @pl.when((steps == step) & (taken > 0))
            def _(terms_ref=terms_ref):
                for side, (old_ref, new_ref) in enumerate(sides):
                    code = terms_ref[side, :width].astype(jnp.int32).astype(jnp.float32)
                    scale = terms_ref[side, width:].astype(jnp.int32).astype(jnp.float32)
                    top = decoded(scale[0:1], scale[1:2], scale[2:3])
                    gain = top * ((1.0 - decay_rate) / order / (code_top * code_top))
                    new_ref[slot] = decay_rate * old_ref[slot] + code * jnp.abs(code) * gain

        @pl.when(taken == 0)
        def _():
            for old_ref, new_ref in sides:
                new_ref[slot] = old_ref[slot]


def new_stats(place, coded_terms, left_stats, right_stats):
    out = jax.ShapeDtypeStruct(left_stats.shape, jnp.float32)
    return pl.pallas_call(
        stats_kernel,
        grid_spec=pltpu.PrefetchScalarGridSpec(
            num_scalar_prefetch=1,
            grid=(1,),
            in_specs=[whole(coded_terms[0].shape)] * parts + [whole(out.shape)] * 2,
            out_specs=[whole(out.shape)] * 2,
        ),
        out_shape=[out] * 2,
        compiler_params=pltpu.CompilerParams(vmem_limit_bytes=32 * 1024 * 1024),
        cost_estimate=pl.CostEstimate(flops=0, bytes_accessed=5 << 20, transcendentals=0),
    )(place, *coded_terms, left_stats, right_stats)


def repack_kernel(back_ref, ahead_ref):
    cells = ahead_ref.shape[1] - 1
    slots = cells // near
    for device in range(near):
        for slot in range(slots):
            ahead_ref[:, device * slots + slot] = back_ref[device * parts + slot, :far]
    wide = [back_ref[device, far].astype(jnp.int32) for device in range(near * parts)]
    facts = functools.reduce(jnp.add, wide).astype(jnp.int16)
    for z in range(far):
        ahead_ref[z, cells] = facts


def repack(back, slots):
    return pl.pallas_call(
        repack_kernel,
        out_shape=jax.ShapeDtypeStruct((far, near * slots + 1) + back.shape[2:], back.dtype),
        in_specs=[pl.BlockSpec(memory_space=pltpu.VMEM)],
        out_specs=pl.BlockSpec(memory_space=pltpu.VMEM),
        compiler_params=pltpu.CompilerParams(vmem_limit_bytes=16 * 1024 * 1024),
        cost_estimate=pl.CostEstimate(flops=0, bytes_accessed=1 << 20, transcendentals=0),
    )(back)


def finish_kernel(at_ref, spot_ref, up_ref, arrived_ref, update_ref, factor_ref):
    cells = arrived_ref.shape[1] - 1
    facts = [arrived_ref[z, cells].astype(jnp.int32).astype(jnp.float32) for z in range(far)]
    row = lambda r: jnp.concatenate([fact[r : r + 1] for fact in facts], axis=0)
    sums = jnp.sum(decoded(row(0), row(1), row(2)), axis=0, keepdims=True)
    kind = lax.rem(lax.broadcasted_iota(jnp.int32, sums.shape, 1), 4)
    total = lambda k: jnp.sum(jnp.where(kind == k, sums, 0.0), axis=1, keepdims=True)
    gate_scale = jnp.sqrt(total(0) / total(2))
    up_scale = jnp.sqrt(total(1) / total(3))
    tops = row(3)
    lanes = tops.shape[1]
    steps = decoded(tops, pltpu.roll(tops, lanes - 1, 1), pltpu.roll(tops, lanes - 2, 1))
    steps = steps * (1.0 / (code_top * code_top))
    spot = spot_ref[...]
    lane = lax.broadcasted_iota(jnp.int32, spot.shape, 1)
    mine = jnp.zeros(spot.shape, jnp.float32)
    for z in range(far):
        mine += jnp.where(spot == lane + z * lanes, steps[z : z + 1], 0.0)
    step = jnp.sum(mine, axis=1, keepdims=True)
    factor_ref[...] = jnp.where(up_ref[...] > 0, up_scale, gate_scale) * step

    for b in range(update_ref.shape[0]):
        at = at_ref[b]
        code = arrived_ref[at // cells, lax.rem(at, cells)].astype(jnp.int32).astype(jnp.float32)
        update_ref[b] = (code * jnp.abs(code) * factor_ref[b : b + 1, :]).astype(jnp.bfloat16)


def finish(cell_ids, spot, up, arrived):
    blocks = cell_ids.shape[0]
    return pl.pallas_call(
        finish_kernel,
        in_specs=[in_smem] + [in_vmem] * 3,
        out_specs=in_vmem,
        scratch_shapes=[pltpu.VMEM((blocks, arrived.shape[3]), jnp.float32)],
        out_shape=jax.ShapeDtypeStruct((blocks,) + arrived.shape[2:], jnp.bfloat16),
        compiler_params=pltpu.CompilerParams(vmem_limit_bytes=16 * 1024 * 1024),
        cost_estimate=pl.CostEstimate(flops=0, bytes_accessed=1 << 20, transcendentals=0),
    )(cell_ids, spot, up, arrived)


def on_device(gradient, owner_map, left_stats, right_stats, left_root, right_root):
    block_count, row_share, col_share = gradient.shape
    capacity, part_rows, block_size = left_stats.shape
    my_owner = lax.axis_index("fsdp")
    my_part = lax.axis_index("mp")

    packed = pack(owner_map, gradient, capacity).reshape(far, near, capacity, row_share, col_share)
    in_plane = exchange(packed, "fsdp", far_groups)

    def send(steps, k):
        slot = jnp.minimum((my_part + k) % parts, capacity - 1)

        def column(root, step):
            start = (my_part + step) % parts * part_rows
            return lax.dynamic_slice(root, (slot, 0, start), (1, part_rows, part_rows))

        rows = [jnp.concatenate([column(root, step) for step in steps], axis=2) for root in (left_root, right_root)]
        pairs = [(i, (i + k) % parts) for i in range(parts)]
        return lax.ppermute(jnp.concatenate(rows, axis=0), "mp", pairs)

    three = send((0, 3), 1)
    two = send((0,), 2)
    one = send((0, 2, 1), 3)
    my_slot = jnp.minimum(my_part, capacity - 1)
    place = jnp.stack([my_owner % near, my_part, my_slot])
    roots = spread_roots(place, left_root, right_root, (one, two, three))
    in_plane, owner_map, *roots = lax.optimization_barrier((in_plane, owner_map, *roots))

    fanned = fan(in_plane).reshape(near * parts, far * row_share, col_share)
    landed = exchange(fanned, ("fsdp", "mp"), plane_groups)

    cell_ids = cell_index(owner_map, capacity)
    up_block = jnp.arange(block_count, dtype=jnp.int32) >= block_count // 2
    my_cells = my_owner * capacity + jnp.arange(capacity, dtype=jnp.int32)
    holding = cell_ids[None, :] == my_cells[:, None]
    taken = jnp.max(jnp.where(holding, 1 + up_block.astype(jnp.int32)[None, :], 0), axis=1)
    my_taken = jnp.where(my_part < capacity, taken[my_slot], 0)
    place = jnp.concatenate([place, my_taken[None], taken])
    message = precondition(place, landed, roots)
    landed, message = lax.optimization_barrier((landed, message))
    back = exchange(message, ("fsdp", "mp"), plane_groups)

    block = landed.reshape(near, parts, far, row_share, col_share).transpose(2, 0, 3, 1, 4)
    own_terms, *other_terms = terms(place, block.reshape(block_size, block_size))
    coded_terms = [own_terms]
    for k, other in enumerate(other_terms, 1):
        coded_terms.append(lax.ppermute(other, "mp", [(i, (i + k) % parts) for i in range(parts)]))
    arrived = exchange(repack(back, capacity), "fsdp", far_groups)
    left_new, right_new = new_stats(place, coded_terms, left_stats, right_stats)

    cells = near * capacity
    spot = cell_ids // cells * 128 + cell_ids % cells // capacity * 16 + cell_ids % capacity * 3
    across = lambda array: jnp.broadcast_to(array.astype(jnp.int32)[:, None], (block_count, 128))
    update = finish(cell_ids, across(spot), across(up_block), arrived)
    return (update, left_new, right_new)


def solution(mesh):
    placed = (
        P(None, "fsdp", "mp"),
        P(),
        P("fsdp", "mp", None),
        P("fsdp", "mp", None),
        P("fsdp", "mp", None),
        P("fsdp", "mp", None),
    )
    return jax.shard_map(
        on_device,
        mesh=mesh,
        in_specs=placed,
        out_specs=(P(None, "fsdp", "mp"), P("fsdp", "mp", None), P("fsdp", "mp", None)),
        check_vma=False,
    )
```

```python
import functools

import jax
import jax.numpy as jnp
from jax import lax
from jax.experimental import pallas as pl
from jax.experimental.pallas import tpu as pltpu
from jax.sharding import PartitionSpec as P

decay_rate = 0.95
code_top = 32767.0
parts = 4
near = 8
far = 16


def cell_index(owner_map, capacity):
    total_rows = owner_map.shape[0]
    positions = jnp.arange(total_rows, dtype=jnp.int32)
    same_owner = owner_map[None, :] == owner_map[:, None]
    earlier = positions[None, :] < positions[:, None]
    ranks = jnp.sum((same_owner & earlier).astype(jnp.int32), axis=1)
    return owner_map * capacity + ranks


far_groups = [[z * near + n for z in range(far)] for n in range(near)]
plane_groups = [[(z * near + n) * parts + m for n in range(near) for m in range(parts)] for z in range(far)]


def exchange(array, axis_name, groups):
    return lax.all_to_all(
        array, axis_name, split_axis=0, concat_axis=0, axis_index_groups=groups, tiled=True
    )


def split_two(array):
    high = array.astype(jnp.bfloat16)
    return high, (array - high.astype(jnp.float32)).astype(jnp.bfloat16)


tn = (((0,), (0,)), ((), ()))
nn = (((1,), (0,)), ((), ()))
nt = (((1,), (1,)), ((), ()))
dot = functools.partial(lax.dot_general, preferred_element_type=jnp.float32)


def pack_kernel(owner_ref, far_grad_ref, packed_ref, count_ref, grad_ref, sem):
    blocks = grad_ref.shape[0]
    slots = packed_ref.shape[0] // blocks
    copy = pltpu.make_async_copy(far_grad_ref, grad_ref, sem)
    copy.start()
    packed_ref[...] = jnp.zeros_like(packed_ref)
    for owner in range(blocks):
        count_ref[owner] = 0
    copy.wait()
    for b in range(blocks):
        owner = owner_ref[b]
        rank = count_ref[owner]
        count_ref[owner] = rank + 1
        packed_ref[owner * slots + rank] = grad_ref[b]


def pack(owner_map, gradient, slots):
    blocks = gradient.shape[0]
    packed = (blocks * slots,) + gradient.shape[1:]
    return pl.pallas_call(
        pack_kernel,
        grid_spec=pltpu.PrefetchScalarGridSpec(
            num_scalar_prefetch=1,
            grid=(1,),
            in_specs=[pl.BlockSpec(memory_space=pltpu.HBM)],
            out_specs=whole(packed),
            scratch_shapes=[
                pltpu.SMEM((blocks,), jnp.int32),
                pltpu.VMEM(gradient.shape, gradient.dtype),
                pltpu.SemaphoreType.DMA,
            ],
        ),
        out_shape=jax.ShapeDtypeStruct(packed, gradient.dtype),
        compiler_params=pltpu.CompilerParams(vmem_limit_bytes=16 * 1024 * 1024),
        cost_estimate=pl.CostEstimate(flops=0, bytes_accessed=1 << 20, transcendentals=0),
    )(pltpu.with_memory_space_constraint(owner_map, pltpu.HBM), pltpu.with_memory_space_constraint(gradient, pltpu.HBM))


def fan_kernel(plane_ref, fan_ref):
    for n in range(near):
        for slot in range(parts):
            if slot < plane_ref.shape[2]:
                fan_ref[n, slot] = plane_ref[:, n, slot]
            else:
                fan_ref[n, slot] = jnp.zeros(fan_ref.shape[2:], fan_ref.dtype)


def fan(in_plane):
    _, _, slots, rows, width = in_plane.shape
    return pl.pallas_call(
        fan_kernel,
        out_shape=jax.ShapeDtypeStruct((near, parts, far, rows, width), in_plane.dtype),
        in_specs=[pl.BlockSpec(memory_space=pltpu.VMEM)],
        out_specs=pl.BlockSpec(memory_space=pltpu.VMEM),
        compiler_params=pltpu.CompilerParams(vmem_limit_bytes=16 * 1024 * 1024),
        cost_estimate=pl.CostEstimate(flops=0, bytes_accessed=1 << 20, transcendentals=0),
    )(in_plane)


def roots_kernel(
    place_ref, left_ref, right_ref, one_ref, two_ref, three_ref,
    left_high_ref, left_low_ref, right_high_ref, right_low_ref, high_ref, low_ref,
):
    part = place_ref[1]
    width = left_ref.shape[1]

    def span(step):
        at = lax.rem(part + step, parts)
        return pl.ds(pl.multiple_of(at * width, width), width)

    def spread(root, own_ref, high_ref, low_ref):
        def put(row, col, block):
            high, low = split_two(block)
            high_ref[span(row), span(col)] = high
            low_ref[span(row), span(col)] = low

        def put_pair(row, col, block):
            put(row, col, block)
            put(col, row, block.T)

        put(0, 0, own_ref[0, :, span(0)])
        for step in range(1, parts):
            put_pair(0, step, own_ref[0, :, span(step)])
        put(1, 1, one_ref[root, :, :width])
        put_pair(1, 3, one_ref[root, :, width : 2 * width])
        put_pair(1, 2, one_ref[root, :, 2 * width :])
        put(2, 2, two_ref[root])
        put(3, 3, three_ref[root, :, :width])
        put_pair(3, 2, three_ref[root, :, width:])

    spread(0, left_ref, high_ref, low_ref)
    spread(1, right_ref, right_high_ref, right_low_ref)
    size = high_ref.shape[0]
    row = lax.broadcasted_iota(jnp.int32, (size, size), 0)
    col = lax.broadcasted_iota(jnp.int32, (size, size), 1)
    z = lax.shift_right_logical(row, 2) & (far - 1)
    source = z * (size // far) + lax.shift_right_logical(row, 6) * 4 + (row & 3)
    order = jnp.where(col == source, 1.0, 0.0).astype(jnp.bfloat16)
    left_high_ref[...] = dot(high_ref[...], order, nt).astype(jnp.bfloat16)
    left_low_ref[...] = dot(low_ref[...], order, nt).astype(jnp.bfloat16)


in_vmem = pl.BlockSpec(memory_space=pltpu.VMEM)
in_smem = pl.BlockSpec(memory_space=pltpu.SMEM)


def whole(shape):
    return pl.BlockSpec(shape, lambda i, *_: (0,) * len(shape))


def spread_roots(place, left_root, right_root, others):
    _, width, order = right_root.shape
    mine = pl.BlockSpec((1, width, order), lambda i, place: (place[2], 0, 0))
    out = jax.ShapeDtypeStruct((order, order), jnp.bfloat16)
    return pl.pallas_call(
        roots_kernel,
        grid_spec=pltpu.PrefetchScalarGridSpec(
            num_scalar_prefetch=1,
            grid=(1,),
            in_specs=[mine, mine] + [whole(other.shape) for other in others],
            out_specs=[whole(out.shape)] * 4,
            scratch_shapes=[pltpu.VMEM(out.shape, out.dtype)] * 2,
        ),
        out_shape=[out] * 4,
        compiler_params=pltpu.CompilerParams(vmem_limit_bytes=32 * 1024 * 1024),
        cost_estimate=pl.CostEstimate(flops=0, bytes_accessed=5 << 20, transcendentals=0),
    )(place, left_root, right_root, *others)


def power(exponent):
    half = jnp.floor(exponent * 0.5)
    return jnp.exp2(half), jnp.exp2(exponent - half)


def coded(value):
    value = jnp.maximum(value, 1e-37)
    exponent = jnp.floor(jnp.log2(value)) + 1.0
    one, two = power(-exponent)
    share = value * one * two * 16384.0
    high = jnp.floor(share)
    return exponent, high, jnp.floor((share - high) * 16384.0)


def decoded(exponent, high, low):
    one, two = power(exponent - 14.0)
    return jnp.where(high > 0, (high + low * (1.0 / 16384.0)) * one * two, 0.0)


def square_root_code(value, top):
    root = jnp.sqrt(jnp.abs(value) * (code_top * code_top / top))
    return jnp.round(jnp.where(value < 0, -root, root)).astype(jnp.int32)


def precondition_kernel(
    place_ref, grad_ref, left_high_ref, left_low_ref, right_high_ref, right_low_ref, message_ref, late_ref, sem
):
    order = left_high_ref.shape[0]
    late = pltpu.make_async_copy(right_low_ref, late_ref, sem)
    late.start()
    grad = jnp.concatenate([grad_ref[:, m].reshape(order, -1) for m in range(parts)], axis=1)
    half = dot(left_high_ref[...], grad, nn) + dot(left_low_ref[...], grad, nn)
    half_high, half_low = split_two(half)
    right_high = right_high_ref[...]
    result = dot(half_high, right_high, nn) + dot(half_low, right_high, nn)
    late.wait()
    result += dot(half_high, late_ref[...], nn)
    taken = place_ref[3]
    result = jnp.where(taken > 0, result, 0.0)
    top = jnp.maximum(jnp.max(jnp.abs(result)), 1e-30)
    code = square_root_code(result, top)
    deep, width = message_ref.shape[2:]
    for z in range(far):
        for device in range(near):
            for m in range(parts):
                row = (z * near + device) * deep
                message_ref[device * parts + m, z] = code[row : row + deep, m * width : (m + 1) * width].astype(
                    jnp.int16
                )

    wide = grad.astype(jnp.float32)
    grad_sum = jnp.where(taken > 0, jnp.sum(wide * wide), 0.0)
    upd_sum = jnp.sum(result * result)
    row = lax.broadcasted_iota(jnp.int32, (8, 128), 0)
    at = lax.broadcasted_iota(jnp.int32, (8, 128), 1) - place_ref[0] * 16
    sum_at = at - place_ref[1] * 4
    top_at = at - place_ref[1] * 3
    is_up = jnp.where(taken > 1, 1, 0)
    exponent, high, low = coded(
        jnp.where(sum_at == is_up, grad_sum, jnp.where(sum_at == 2 + is_up, upd_sum, 0.0))
    )
    in_sums = (sum_at >= 0) & (sum_at < 4)
    sums = jnp.where(in_sums, jnp.where(row == 0, exponent, jnp.where(row == 1, high, low)), 0.0)
    exponent, high, low = coded(jnp.full((8, 128), top))
    in_tops = (top_at >= 0) & (top_at < 3) & (place_ref[1] < parts - 1)
    tops = jnp.where(in_tops, jnp.where(top_at == 0, exponent, jnp.where(top_at == 1, high, low)), 0.0)
    facts = jnp.where(row < 3, sums, tops)[:deep].astype(jnp.int32).astype(jnp.int16)
    for device in range(near * parts):
        message_ref[device, far] = facts


def precondition(place, landed, roots):
    _, rows, width = landed.shape
    order = near * rows
    landed = landed.reshape(near, parts, rows, width)
    message = (near * parts, far + 1, rows // far, width)
    return pl.pallas_call(
        precondition_kernel,
        in_specs=[in_smem] + [in_vmem] * 4 + [pl.BlockSpec(memory_space=pltpu.HBM)],
        out_specs=in_vmem,
        scratch_shapes=[pltpu.VMEM((order, order), jnp.bfloat16), pltpu.SemaphoreType.DMA],
        out_shape=jax.ShapeDtypeStruct(message, jnp.int16),
        compiler_params=pltpu.CompilerParams(vmem_limit_bytes=32 * 1024 * 1024),
        cost_estimate=pl.CostEstimate(flops=10 * order**3, bytes_accessed=4 << 20, transcendentals=0),
    )(place, landed, *roots[:3], pltpu.with_memory_space_constraint(roots[3], pltpu.HBM))


def terms_kernel(place_ref, block_ref, own_ref, one_ref, two_ref, three_ref, term_ref):
    block = block_ref[...]
    out_refs = (own_ref, one_ref, two_ref, three_ref)
    width = own_ref.shape[1] - 16
    row = lax.broadcasted_iota(jnp.int32, (16, block.shape[1]), 0)
    for side in range(2):
        term = dot(block, block, nt if side == 0 else tn)
        top = jnp.maximum(jnp.max(jnp.abs(term)), 1e-30)
        term_ref[...] = square_root_code(term, top)
        exponent, high, low = coded(jnp.full(row.shape, top))
        scale = jnp.where(row == 0, exponent, jnp.where(row == 1, high, low)).astype(jnp.int32).astype(jnp.int16)
        for step in range(parts):
            at = lax.rem(place_ref[1] + step, parts)
            out_refs[step][side, :width] = term_ref[pl.ds(pl.multiple_of(at * width, width), width), :].astype(
                jnp.int16
            )
            out_refs[step][side, width:] = scale


def terms(place, block):
    order = block.shape[0]
    out = jax.ShapeDtypeStruct((2, order // parts + 16, order), jnp.int16)
    return pl.pallas_call(
        terms_kernel,
        grid_spec=pltpu.PrefetchScalarGridSpec(
            num_scalar_prefetch=1,
            grid=(1,),
            in_specs=[whole(block.shape)],
            out_specs=[whole(out.shape)] * parts,
            scratch_shapes=[pltpu.VMEM((order, order), jnp.int32)],
        ),
        out_shape=[out] * parts,
        compiler_params=pltpu.CompilerParams(vmem_limit_bytes=32 * 1024 * 1024),
        cost_estimate=pl.CostEstimate(flops=4 * order**3, bytes_accessed=2 << 20, transcendentals=0),
    )(place, block)


def stats_kernel(place_ref, own_ref, one_ref, two_ref, three_ref, left_ref, right_ref, left_new_ref, right_new_ref):
    slots, width, order = left_ref.shape
    sides = ((left_ref, left_new_ref), (right_ref, right_new_ref))
    for slot in range(slots):
        steps = lax.rem(place_ref[1] + parts - slot, parts)
        taken = place_ref[4 + slot]
        for step, terms_ref in enumerate((own_ref, one_ref, two_ref, three_ref)):

            @pl.when((steps == step) & (taken > 0))
            def _(terms_ref=terms_ref):
                for side, (old_ref, new_ref) in enumerate(sides):
                    code = terms_ref[side, :width].astype(jnp.int32).astype(jnp.float32)
                    scale = terms_ref[side, width:].astype(jnp.int32).astype(jnp.float32)
                    top = decoded(scale[0:1], scale[1:2], scale[2:3])
                    gain = top * ((1.0 - decay_rate) / order / (code_top * code_top))
                    new_ref[slot] = decay_rate * old_ref[slot] + code * jnp.abs(code) * gain

        @pl.when(taken == 0)
        def _():
            for old_ref, new_ref in sides:
                new_ref[slot] = old_ref[slot]


def new_stats(place, coded_terms, left_stats, right_stats):
    out = jax.ShapeDtypeStruct(left_stats.shape, jnp.float32)
    return pl.pallas_call(
        stats_kernel,
        grid_spec=pltpu.PrefetchScalarGridSpec(
            num_scalar_prefetch=1,
            grid=(1,),
            in_specs=[whole(coded_terms[0].shape)] * parts + [whole(out.shape)] * 2,
            out_specs=[whole(out.shape)] * 2,
        ),
        out_shape=[out] * 2,
        compiler_params=pltpu.CompilerParams(vmem_limit_bytes=32 * 1024 * 1024),
        cost_estimate=pl.CostEstimate(flops=0, bytes_accessed=5 << 20, transcendentals=0),
    )(place, *coded_terms, left_stats, right_stats)


def repack_kernel(back_ref, ahead_ref):
    cells = ahead_ref.shape[1] - 1
    slots = cells // near
    for device in range(near):
        for slot in range(slots):
            ahead_ref[:, device * slots + slot] = back_ref[device * parts + slot, :far]
    wide = [back_ref[device, far].astype(jnp.int32) for device in range(near * parts)]
    facts = functools.reduce(jnp.add, wide).astype(jnp.int16)
    for z in range(far):
        ahead_ref[z, cells] = facts


def repack(back, slots):
    return pl.pallas_call(
        repack_kernel,
        out_shape=jax.ShapeDtypeStruct((far, near * slots + 1) + back.shape[2:], back.dtype),
        in_specs=[pl.BlockSpec(memory_space=pltpu.VMEM)],
        out_specs=pl.BlockSpec(memory_space=pltpu.VMEM),
        compiler_params=pltpu.CompilerParams(vmem_limit_bytes=16 * 1024 * 1024),
        cost_estimate=pl.CostEstimate(flops=0, bytes_accessed=1 << 20, transcendentals=0),
    )(back)


def finish_kernel(at_ref, spot_ref, up_ref, arrived_ref, update_ref, factor_ref):
    cells = arrived_ref.shape[1] - 1
    facts = [arrived_ref[z, cells].astype(jnp.int32).astype(jnp.float32) for z in range(far)]
    row = lambda r: jnp.concatenate([fact[r : r + 1] for fact in facts], axis=0)
    sums = jnp.sum(decoded(row(0), row(1), row(2)), axis=0, keepdims=True)
    kind = lax.rem(lax.broadcasted_iota(jnp.int32, sums.shape, 1), 4)
    total = lambda k: jnp.sum(jnp.where(kind == k, sums, 0.0), axis=1, keepdims=True)
    gate_scale = jnp.sqrt(total(0) / total(2))
    up_scale = jnp.sqrt(total(1) / total(3))
    tops = row(3)
    lanes = tops.shape[1]
    steps = decoded(tops, pltpu.roll(tops, lanes - 1, 1), pltpu.roll(tops, lanes - 2, 1))
    steps = steps * (1.0 / (code_top * code_top))
    spot = spot_ref[...]
    lane = lax.broadcasted_iota(jnp.int32, spot.shape, 1)
    mine = jnp.zeros(spot.shape, jnp.float32)
    for z in range(far):
        mine += jnp.where(spot == lane + z * lanes, steps[z : z + 1], 0.0)
    step = jnp.sum(mine, axis=1, keepdims=True)
    factor_ref[...] = jnp.where(up_ref[...] > 0, up_scale, gate_scale) * step

    for b in range(update_ref.shape[0]):
        at = at_ref[b]
        code = arrived_ref[at // cells, lax.rem(at, cells)].astype(jnp.int32).astype(jnp.float32)
        update_ref[b] = (code * jnp.abs(code) * factor_ref[b : b + 1, :]).astype(jnp.bfloat16)


def finish(cell_ids, spot, up, arrived):
    blocks = cell_ids.shape[0]
    return pl.pallas_call(
        finish_kernel,
        in_specs=[in_smem] + [in_vmem] * 3,
        out_specs=in_vmem,
        scratch_shapes=[pltpu.VMEM((blocks, arrived.shape[3]), jnp.float32)],
        out_shape=jax.ShapeDtypeStruct((blocks,) + arrived.shape[2:], jnp.bfloat16),
        compiler_params=pltpu.CompilerParams(vmem_limit_bytes=16 * 1024 * 1024),
        cost_estimate=pl.CostEstimate(flops=0, bytes_accessed=1 << 20, transcendentals=0),
    )(cell_ids, spot, up, arrived)


def on_device(gradient, owner_map, left_stats, right_stats, left_root, right_root):
    block_count, row_share, col_share = gradient.shape
    capacity, part_rows, block_size = left_stats.shape
    my_owner = lax.axis_index("fsdp")
    my_part = lax.axis_index("mp")

    packed = pack(owner_map, gradient, capacity).reshape(far, near, capacity, row_share, col_share)
    in_plane = exchange(packed, "fsdp", far_groups)

    def send(steps, k):
        slot = jnp.minimum((my_part + k) % parts, capacity - 1)

        def column(root, step):
            start = (my_part + step) % parts * part_rows
            return lax.dynamic_slice(root, (slot, 0, start), (1, part_rows, part_rows))

        rows = [jnp.concatenate([column(root, step) for step in steps], axis=2) for root in (left_root, right_root)]
        pairs = [(i, (i + k) % parts) for i in range(parts)]
        return lax.ppermute(jnp.concatenate(rows, axis=0), "mp", pairs)

    three = send((0, 3), 1)
    two = send((0,), 2)
    one = send((0, 2, 1), 3)
    in_plane, one, two, three, owner_map = lax.optimization_barrier((in_plane, one, two, three, owner_map))
    my_slot = jnp.minimum(my_part, capacity - 1)
    place = jnp.stack([my_owner % near, my_part, my_slot])
    roots = spread_roots(place, left_root, right_root, (one, two, three))

    fanned = fan(in_plane).reshape(near * parts, far * row_share, col_share)
    landed = exchange(fanned, ("fsdp", "mp"), plane_groups)

    cell_ids = cell_index(owner_map, capacity)
    up_block = jnp.arange(block_count, dtype=jnp.int32) >= block_count // 2
    my_cells = my_owner * capacity + jnp.arange(capacity, dtype=jnp.int32)
    holding = cell_ids[None, :] == my_cells[:, None]
    taken = jnp.max(jnp.where(holding, 1 + up_block.astype(jnp.int32)[None, :], 0), axis=1)
    my_taken = jnp.where(my_part < capacity, taken[my_slot], 0)
    place = jnp.concatenate([place, my_taken[None], taken])
    message = precondition(place, landed, roots)
    landed, message = lax.optimization_barrier((landed, message))
    back = exchange(message, ("fsdp", "mp"), plane_groups)

    block = landed.reshape(near, parts, far, row_share, col_share).transpose(2, 0, 3, 1, 4)
    own_terms, *other_terms = terms(place, block.reshape(block_size, block_size))
    coded_terms = [own_terms]
    for k, other in enumerate(other_terms, 1):
        coded_terms.append(lax.ppermute(other, "mp", [(i, (i + k) % parts) for i in range(parts)]))
    arrived = exchange(repack(back, capacity), "fsdp", far_groups)
    left_new, right_new = new_stats(place, coded_terms, left_stats, right_stats)

    cells = near * capacity
    spot = cell_ids // cells * 128 + cell_ids % cells // capacity * 16 + cell_ids % capacity * 3
    across = lambda array: jnp.broadcast_to(array.astype(jnp.int32)[:, None], (block_count, 128))
    update = finish(cell_ids, across(spot), across(up_block), arrived)
    return (update, left_new, right_new)


def solution(mesh):
    placed = (
        P(None, "fsdp", "mp"),
        P(),
        P("fsdp", "mp", None),
        P("fsdp", "mp", None),
        P("fsdp", "mp", None),
        P("fsdp", "mp", None),
    )
    return jax.shard_map(
        on_device,
        mesh=mesh,
        in_specs=placed,
        out_specs=(P(None, "fsdp", "mp"), P("fsdp", "mp", None), P("fsdp", "mp", None)),
        check_vma=False,
    )
```

```python
import functools

import jax
import jax.numpy as jnp
from jax import lax
from jax.experimental import pallas as pl
from jax.experimental.pallas import tpu as pltpu
from jax.sharding import PartitionSpec as P

decay_rate = 0.95
code_top = 32767.0
parts = 4
near = 8
far = 16


def cell_index(owner_map, capacity):
    total_rows = owner_map.shape[0]
    positions = jnp.arange(total_rows, dtype=jnp.int32)
    same_owner = owner_map[None, :] == owner_map[:, None]
    earlier = positions[None, :] < positions[:, None]
    ranks = jnp.sum((same_owner & earlier).astype(jnp.int32), axis=1)
    return owner_map * capacity + ranks


far_groups = [[z * near + n for z in range(far)] for n in range(near)]
plane_groups = [[(z * near + n) * parts + m for n in range(near) for m in range(parts)] for z in range(far)]


def exchange(array, axis_name, groups):
    return lax.all_to_all(
        array, axis_name, split_axis=0, concat_axis=0, axis_index_groups=groups, tiled=True
    )


def split_two(array):
    high = array.astype(jnp.bfloat16)
    return high, (array - high.astype(jnp.float32)).astype(jnp.bfloat16)


tn = (((0,), (0,)), ((), ()))
nn = (((1,), (0,)), ((), ()))
nt = (((1,), (1,)), ((), ()))
dot = functools.partial(lax.dot_general, preferred_element_type=jnp.float32)


def pack_kernel(owner_ref, far_grad_ref, packed_ref, count_ref, grad_ref, sem):
    blocks = grad_ref.shape[0]
    slots = packed_ref.shape[0] // blocks
    copy = pltpu.make_async_copy(far_grad_ref, grad_ref, sem)
    copy.start()
    packed_ref[...] = jnp.zeros_like(packed_ref)
    for owner in range(blocks):
        count_ref[owner] = 0
    copy.wait()
    for b in range(blocks):
        owner = owner_ref[b]
        rank = count_ref[owner]
        count_ref[owner] = rank + 1
        packed_ref[owner * slots + rank] = grad_ref[b]


def pack(owner_map, gradient, slots):
    blocks = gradient.shape[0]
    packed = (blocks * slots,) + gradient.shape[1:]
    return pl.pallas_call(
        pack_kernel,
        grid_spec=pltpu.PrefetchScalarGridSpec(
            num_scalar_prefetch=1,
            grid=(1,),
            in_specs=[pl.BlockSpec(memory_space=pltpu.HBM)],
            out_specs=whole(packed),
            scratch_shapes=[
                pltpu.SMEM((blocks,), jnp.int32),
                pltpu.VMEM(gradient.shape, gradient.dtype),
                pltpu.SemaphoreType.DMA,
            ],
        ),
        out_shape=jax.ShapeDtypeStruct(packed, gradient.dtype),
        compiler_params=pltpu.CompilerParams(vmem_limit_bytes=16 * 1024 * 1024),
        cost_estimate=pl.CostEstimate(flops=0, bytes_accessed=1 << 20, transcendentals=0),
    )(pltpu.with_memory_space_constraint(owner_map, pltpu.HBM), pltpu.with_memory_space_constraint(gradient, pltpu.HBM))


def fan_kernel(plane_ref, fan_ref):
    for n in range(near):
        for slot in range(parts):
            if slot < plane_ref.shape[2]:
                fan_ref[n, slot] = plane_ref[:, n, slot]
            else:
                fan_ref[n, slot] = jnp.zeros(fan_ref.shape[2:], fan_ref.dtype)


def fan(in_plane):
    _, _, slots, rows, width = in_plane.shape
    return pl.pallas_call(
        fan_kernel,
        out_shape=jax.ShapeDtypeStruct((near, parts, far, rows, width), in_plane.dtype),
        in_specs=[pl.BlockSpec(memory_space=pltpu.VMEM)],
        out_specs=pl.BlockSpec(memory_space=pltpu.VMEM),
        compiler_params=pltpu.CompilerParams(vmem_limit_bytes=16 * 1024 * 1024),
        cost_estimate=pl.CostEstimate(flops=0, bytes_accessed=1 << 20, transcendentals=0),
    )(in_plane)


def roots_kernel(
    place_ref, left_ref, right_ref, one_ref, two_ref, three_ref,
    left_high_ref, left_low_ref, right_high_ref, right_low_ref, high_ref, low_ref,
):
    part = place_ref[1]
    width = left_ref.shape[1]

    def span(step):
        at = lax.rem(part + step, parts)
        return pl.ds(pl.multiple_of(at * width, width), width)

    def spread(root, own_ref, high_ref, low_ref):
        def put(row, col, block):
            high, low = split_two(block)
            high_ref[span(row), span(col)] = high
            low_ref[span(row), span(col)] = low

        def put_pair(row, col, block):
            put(row, col, block)
            put(col, row, block.T)

        put(0, 0, own_ref[0, :, span(0)])
        for step in range(1, parts):
            put_pair(0, step, own_ref[0, :, span(step)])
        put(1, 1, one_ref[root, :, :width])
        put_pair(1, 3, one_ref[root, :, width : 2 * width])
        put_pair(1, 2, one_ref[root, :, 2 * width :])
        put(2, 2, two_ref[root])
        put(3, 3, three_ref[root, :, :width])
        put_pair(3, 2, three_ref[root, :, width:])

    spread(0, left_ref, high_ref, low_ref)
    spread(1, right_ref, right_high_ref, right_low_ref)
    size = high_ref.shape[0]
    row = lax.broadcasted_iota(jnp.int32, (size, size), 0)
    col = lax.broadcasted_iota(jnp.int32, (size, size), 1)
    z = lax.shift_right_logical(row, 2) & (far - 1)
    source = z * (size // far) + lax.shift_right_logical(row, 6) * 4 + (row & 3)
    order = jnp.where(col == source, 1.0, 0.0).astype(jnp.bfloat16)
    left_high_ref[...] = dot(high_ref[...], order, nt).astype(jnp.bfloat16)
    left_low_ref[...] = dot(low_ref[...], order, nt).astype(jnp.bfloat16)


in_vmem = pl.BlockSpec(memory_space=pltpu.VMEM)
in_smem = pl.BlockSpec(memory_space=pltpu.SMEM)


def whole(shape):
    return pl.BlockSpec(shape, lambda i, *_: (0,) * len(shape))


def spread_roots(place, left_root, right_root, others):
    _, width, order = right_root.shape
    mine = pl.BlockSpec((1, width, order), lambda i, place: (place[2], 0, 0))
    out = jax.ShapeDtypeStruct((order, order), jnp.bfloat16)
    return pl.pallas_call(
        roots_kernel,
        grid_spec=pltpu.PrefetchScalarGridSpec(
            num_scalar_prefetch=1,
            grid=(1,),
            in_specs=[mine, mine] + [whole(other.shape) for other in others],
            out_specs=[whole(out.shape)] * 4,
            scratch_shapes=[pltpu.VMEM(out.shape, out.dtype)] * 2,
        ),
        out_shape=[out] * 4,
        compiler_params=pltpu.CompilerParams(vmem_limit_bytes=32 * 1024 * 1024),
        cost_estimate=pl.CostEstimate(flops=0, bytes_accessed=5 << 20, transcendentals=0),
    )(place, left_root, right_root, *others)


def power(exponent):
    half = jnp.floor(exponent * 0.5)
    return jnp.exp2(half), jnp.exp2(exponent - half)


def coded(value):
    value = jnp.maximum(value, 1e-37)
    exponent = jnp.floor(jnp.log2(value)) + 1.0
    one, two = power(-exponent)
    share = value * one * two * 16384.0
    high = jnp.floor(share)
    return exponent, high, jnp.floor((share - high) * 16384.0)


def decoded(exponent, high, low):
    one, two = power(exponent - 14.0)
    return jnp.where(high > 0, (high + low * (1.0 / 16384.0)) * one * two, 0.0)


def square_root_code(value, top):
    root = jnp.sqrt(jnp.abs(value) * (code_top * code_top / top))
    return jnp.round(jnp.where(value < 0, -root, root)).astype(jnp.int32)


def precondition_kernel(
    place_ref, grad_ref, left_high_ref, left_low_ref, right_high_ref, right_low_ref, message_ref, late_ref, sems
):
    order = left_high_ref.shape[0]
    far_refs = (left_low_ref, right_high_ref, right_low_ref)
    left_late, right_late, last = [
        pltpu.make_async_copy(far_refs[i], late_ref.at[i], sems.at[i]) for i in range(3)
    ]
    for copy in (left_late, right_late, last):
        copy.start()
    grad = jnp.concatenate([grad_ref[:, m].reshape(order, -1) for m in range(parts)], axis=1)
    half = dot(left_high_ref[...], grad, nn)
    left_late.wait()
    half += dot(late_ref[0], grad, nn)
    half_high, half_low = split_two(half)
    right_late.wait()
    right_high = late_ref[1]
    result = dot(half_high, right_high, nn) + dot(half_low, right_high, nn)
    last.wait()
    result += dot(half_high, late_ref[2], nn)
    taken = place_ref[3]
    result = jnp.where(taken > 0, result, 0.0)
    top = jnp.maximum(jnp.max(jnp.abs(result)), 1e-30)
    code = square_root_code(result, top)
    deep, width = message_ref.shape[2:]
    for z in range(far):
        for device in range(near):
            for m in range(parts):
                row = (z * near + device) * deep
                message_ref[device * parts + m, z] = code[row : row + deep, m * width : (m + 1) * width].astype(
                    jnp.int16
                )

    wide = grad.astype(jnp.float32)
    grad_sum = jnp.where(taken > 0, jnp.sum(wide * wide), 0.0)
    upd_sum = jnp.sum(result * result)
    row = lax.broadcasted_iota(jnp.int32, (8, 128), 0)
    at = lax.broadcasted_iota(jnp.int32, (8, 128), 1) - place_ref[0] * 16
    sum_at = at - place_ref[1] * 4
    top_at = at - place_ref[1] * 3
    is_up = jnp.where(taken > 1, 1, 0)
    exponent, high, low = coded(
        jnp.where(sum_at == is_up, grad_sum, jnp.where(sum_at == 2 + is_up, upd_sum, 0.0))
    )
    in_sums = (sum_at >= 0) & (sum_at < 4)
    sums = jnp.where(in_sums, jnp.where(row == 0, exponent, jnp.where(row == 1, high, low)), 0.0)
    exponent, high, low = coded(jnp.full((8, 128), top))
    in_tops = (top_at >= 0) & (top_at < 3) & (place_ref[1] < parts - 1)
    tops = jnp.where(in_tops, jnp.where(top_at == 0, exponent, jnp.where(top_at == 1, high, low)), 0.0)
    facts = jnp.where(row < 3, sums, tops)[:deep].astype(jnp.int32).astype(jnp.int16)
    for device in range(near * parts):
        message_ref[device, far] = facts


def precondition(place, landed, roots):
    _, rows, width = landed.shape
    order = near * rows
    landed = landed.reshape(near, parts, rows, width)
    message = (near * parts, far + 1, rows // far, width)
    return pl.pallas_call(
        precondition_kernel,
        in_specs=[in_smem] + [in_vmem] * 2 + [pl.BlockSpec(memory_space=pltpu.HBM)] * 3,
        out_specs=in_vmem,
        scratch_shapes=[pltpu.VMEM((3, order, order), jnp.bfloat16), pltpu.SemaphoreType.DMA((3,))],
        out_shape=jax.ShapeDtypeStruct(message, jnp.int16),
        compiler_params=pltpu.CompilerParams(vmem_limit_bytes=32 * 1024 * 1024),
        cost_estimate=pl.CostEstimate(flops=10 * order**3, bytes_accessed=4 << 20, transcendentals=0),
    )(place, landed, roots[0], *(pltpu.with_memory_space_constraint(root, pltpu.HBM) for root in roots[1:]))


def terms_kernel(place_ref, block_ref, own_ref, one_ref, two_ref, three_ref, term_ref):
    block = block_ref[...]
    out_refs = (own_ref, one_ref, two_ref, three_ref)
    width = own_ref.shape[1] - 16
    row = lax.broadcasted_iota(jnp.int32, (16, block.shape[1]), 0)
    for side in range(2):
        term = dot(block, block, nt if side == 0 else tn)
        top = jnp.maximum(jnp.max(jnp.abs(term)), 1e-30)
        term_ref[...] = square_root_code(term, top)
        exponent, high, low = coded(jnp.full(row.shape, top))
        scale = jnp.where(row == 0, exponent, jnp.where(row == 1, high, low)).astype(jnp.int32).astype(jnp.int16)
        for step in range(parts):
            at = lax.rem(place_ref[1] + step, parts)
            out_refs[step][side, :width] = term_ref[pl.ds(pl.multiple_of(at * width, width), width), :].astype(
                jnp.int16
            )
            out_refs[step][side, width:] = scale


def terms(place, block):
    order = block.shape[0]
    out = jax.ShapeDtypeStruct((2, order // parts + 16, order), jnp.int16)
    return pl.pallas_call(
        terms_kernel,
        grid_spec=pltpu.PrefetchScalarGridSpec(
            num_scalar_prefetch=1,
            grid=(1,),
            in_specs=[whole(block.shape)],
            out_specs=[whole(out.shape)] * parts,
            scratch_shapes=[pltpu.VMEM((order, order), jnp.int32)],
        ),
        out_shape=[out] * parts,
        compiler_params=pltpu.CompilerParams(vmem_limit_bytes=32 * 1024 * 1024),
        cost_estimate=pl.CostEstimate(flops=4 * order**3, bytes_accessed=2 << 20, transcendentals=0),
    )(place, block)


def stats_kernel(place_ref, own_ref, one_ref, two_ref, three_ref, left_ref, right_ref, left_new_ref, right_new_ref):
    slots, width, order = left_ref.shape
    sides = ((left_ref, left_new_ref), (right_ref, right_new_ref))
    for slot in range(slots):
        steps = lax.rem(place_ref[1] + parts - slot, parts)
        taken = place_ref[4 + slot]
        for step, terms_ref in enumerate((own_ref, one_ref, two_ref, three_ref)):

            @pl.when((steps == step) & (taken > 0))
            def _(terms_ref=terms_ref):
                for side, (old_ref, new_ref) in enumerate(sides):
                    code = terms_ref[side, :width].astype(jnp.int32).astype(jnp.float32)
                    scale = terms_ref[side, width:].astype(jnp.int32).astype(jnp.float32)
                    top = decoded(scale[0:1], scale[1:2], scale[2:3])
                    gain = top * ((1.0 - decay_rate) / order / (code_top * code_top))
                    new_ref[slot] = decay_rate * old_ref[slot] + code * jnp.abs(code) * gain

        @pl.when(taken == 0)
        def _():
            for old_ref, new_ref in sides:
                new_ref[slot] = old_ref[slot]


def new_stats(place, coded_terms, left_stats, right_stats):
    out = jax.ShapeDtypeStruct(left_stats.shape, jnp.float32)
    return pl.pallas_call(
        stats_kernel,
        grid_spec=pltpu.PrefetchScalarGridSpec(
            num_scalar_prefetch=1,
            grid=(1,),
            in_specs=[whole(coded_terms[0].shape)] * parts + [whole(out.shape)] * 2,
            out_specs=[whole(out.shape)] * 2,
        ),
        out_shape=[out] * 2,
        compiler_params=pltpu.CompilerParams(vmem_limit_bytes=32 * 1024 * 1024),
        cost_estimate=pl.CostEstimate(flops=0, bytes_accessed=5 << 20, transcendentals=0),
    )(place, *coded_terms, left_stats, right_stats)


def repack_kernel(back_ref, ahead_ref):
    cells = ahead_ref.shape[1] - 1
    slots = cells // near
    for device in range(near):
        for slot in range(slots):
            ahead_ref[:, device * slots + slot] = back_ref[device * parts + slot, :far]
    wide = [back_ref[device, far].astype(jnp.int32) for device in range(near * parts)]
    facts = functools.reduce(jnp.add, wide).astype(jnp.int16)
    for z in range(far):
        ahead_ref[z, cells] = facts


def repack(back, slots):
    return pl.pallas_call(
        repack_kernel,
        out_shape=jax.ShapeDtypeStruct((far, near * slots + 1) + back.shape[2:], back.dtype),
        in_specs=[pl.BlockSpec(memory_space=pltpu.VMEM)],
        out_specs=pl.BlockSpec(memory_space=pltpu.VMEM),
        compiler_params=pltpu.CompilerParams(vmem_limit_bytes=16 * 1024 * 1024),
        cost_estimate=pl.CostEstimate(flops=0, bytes_accessed=1 << 20, transcendentals=0),
    )(back)


def finish_kernel(at_ref, spot_ref, up_ref, arrived_ref, update_ref, factor_ref):
    cells = arrived_ref.shape[1] - 1
    facts = [arrived_ref[z, cells].astype(jnp.int32).astype(jnp.float32) for z in range(far)]
    row = lambda r: jnp.concatenate([fact[r : r + 1] for fact in facts], axis=0)
    sums = jnp.sum(decoded(row(0), row(1), row(2)), axis=0, keepdims=True)
    kind = lax.rem(lax.broadcasted_iota(jnp.int32, sums.shape, 1), 4)
    total = lambda k: jnp.sum(jnp.where(kind == k, sums, 0.0), axis=1, keepdims=True)
    gate_scale = jnp.sqrt(total(0) / total(2))
    up_scale = jnp.sqrt(total(1) / total(3))
    tops = row(3)
    lanes = tops.shape[1]
    steps = decoded(tops, pltpu.roll(tops, lanes - 1, 1), pltpu.roll(tops, lanes - 2, 1))
    steps = steps * (1.0 / (code_top * code_top))
    spot = spot_ref[...]
    lane = lax.broadcasted_iota(jnp.int32, spot.shape, 1)
    mine = jnp.zeros(spot.shape, jnp.float32)
    for z in range(far):
        mine += jnp.where(spot == lane + z * lanes, steps[z : z + 1], 0.0)
    step = jnp.sum(mine, axis=1, keepdims=True)
    factor_ref[...] = jnp.where(up_ref[...] > 0, up_scale, gate_scale) * step

    for b in range(update_ref.shape[0]):
        at = at_ref[b]
        code = arrived_ref[at // cells, lax.rem(at, cells)].astype(jnp.int32).astype(jnp.float32)
        update_ref[b] = (code * jnp.abs(code) * factor_ref[b : b + 1, :]).astype(jnp.bfloat16)


def finish(cell_ids, spot, up, arrived):
    blocks = cell_ids.shape[0]
    return pl.pallas_call(
        finish_kernel,
        in_specs=[in_smem] + [in_vmem] * 3,
        out_specs=in_vmem,
        scratch_shapes=[pltpu.VMEM((blocks, arrived.shape[3]), jnp.float32)],
        out_shape=jax.ShapeDtypeStruct((blocks,) + arrived.shape[2:], jnp.bfloat16),
        compiler_params=pltpu.CompilerParams(vmem_limit_bytes=16 * 1024 * 1024),
        cost_estimate=pl.CostEstimate(flops=0, bytes_accessed=1 << 20, transcendentals=0),
    )(cell_ids, spot, up, arrived)


def on_device(gradient, owner_map, left_stats, right_stats, left_root, right_root):
    block_count, row_share, col_share = gradient.shape
    capacity, part_rows, block_size = left_stats.shape
    my_owner = lax.axis_index("fsdp")
    my_part = lax.axis_index("mp")

    packed = pack(owner_map, gradient, capacity).reshape(far, near, capacity, row_share, col_share)
    in_plane = exchange(packed, "fsdp", far_groups)

    def send(steps, k):
        slot = jnp.minimum((my_part + k) % parts, capacity - 1)

        def column(root, step):
            start = (my_part + step) % parts * part_rows
            return lax.dynamic_slice(root, (slot, 0, start), (1, part_rows, part_rows))

        rows = [jnp.concatenate([column(root, step) for step in steps], axis=2) for root in (left_root, right_root)]
        pairs = [(i, (i + k) % parts) for i in range(parts)]
        return lax.ppermute(jnp.concatenate(rows, axis=0), "mp", pairs)

    three = send((0, 3), 1)
    two = send((0,), 2)
    one = send((0, 2, 1), 3)
    in_plane, one, two, three, owner_map = lax.optimization_barrier((in_plane, one, two, three, owner_map))
    my_slot = jnp.minimum(my_part, capacity - 1)
    place = jnp.stack([my_owner % near, my_part, my_slot])
    roots = spread_roots(place, left_root, right_root, (one, two, three))

    fanned = fan(in_plane).reshape(near * parts, far * row_share, col_share)
    landed = exchange(fanned, ("fsdp", "mp"), plane_groups)

    cell_ids = cell_index(owner_map, capacity)
    up_block = jnp.arange(block_count, dtype=jnp.int32) >= block_count // 2
    my_cells = my_owner * capacity + jnp.arange(capacity, dtype=jnp.int32)
    holding = cell_ids[None, :] == my_cells[:, None]
    taken = jnp.max(jnp.where(holding, 1 + up_block.astype(jnp.int32)[None, :], 0), axis=1)
    my_taken = jnp.where(my_part < capacity, taken[my_slot], 0)
    place = jnp.concatenate([place, my_taken[None], taken])
    message = precondition(place, landed, roots)
    landed, message = lax.optimization_barrier((landed, message))
    back = exchange(message, ("fsdp", "mp"), plane_groups)

    block = landed.reshape(near, parts, far, row_share, col_share).transpose(2, 0, 3, 1, 4)
    made = terms(place, block.reshape(block_size, block_size))
    back, own_terms, *other_terms = lax.optimization_barrier((back, *made))
    coded_terms = [own_terms]
    for k, other in enumerate(other_terms, 1):
        coded_terms.append(lax.ppermute(other, "mp", [(i, (i + k) % parts) for i in range(parts)]))
    arrived = exchange(repack(back, capacity), "fsdp", far_groups)
    left_new, right_new = new_stats(place, coded_terms, left_stats, right_stats)

    cells = near * capacity
    spot = cell_ids // cells * 128 + cell_ids % cells // capacity * 16 + cell_ids % capacity * 3
    across = lambda array: jnp.broadcast_to(array.astype(jnp.int32)[:, None], (block_count, 128))
    update = finish(cell_ids, across(spot), across(up_block), arrived)
    return (update, left_new, right_new)


def solution(mesh):
    placed = (
        P(None, "fsdp", "mp"),
        P(),
        P("fsdp", "mp", None),
        P("fsdp", "mp", None),
        P("fsdp", "mp", None),
        P("fsdp", "mp", None),
    )
    return jax.shard_map(
        on_device,
        mesh=mesh,
        in_specs=placed,
        out_specs=(P(None, "fsdp", "mp"), P("fsdp", "mp", None), P("fsdp", "mp", None)),
        check_vma=False,
    )
```

```python
import functools

import jax
import jax.numpy as jnp
from jax import lax
from jax.experimental import pallas as pl
from jax.experimental.pallas import tpu as pltpu
from jax.sharding import PartitionSpec as P

decay_rate = 0.95
code_top = 32767.0
parts = 4
near = 8
far = 16


def cell_index(owner_map, capacity):
    total_rows = owner_map.shape[0]
    positions = jnp.arange(total_rows, dtype=jnp.int32)
    same_owner = owner_map[None, :] == owner_map[:, None]
    earlier = positions[None, :] < positions[:, None]
    ranks = jnp.sum((same_owner & earlier).astype(jnp.int32), axis=1)
    return owner_map * capacity + ranks


far_groups = [[z * near + n for z in range(far)] for n in range(near)]
plane_groups = [[(z * near + n) * parts + m for n in range(near) for m in range(parts)] for z in range(far)]


def exchange(array, axis_name, groups):
    return lax.all_to_all(
        array, axis_name, split_axis=0, concat_axis=0, axis_index_groups=groups, tiled=True
    )


def split_two(array):
    high = array.astype(jnp.bfloat16)
    return high, (array - high.astype(jnp.float32)).astype(jnp.bfloat16)


tn = (((0,), (0,)), ((), ()))
nn = (((1,), (0,)), ((), ()))
nt = (((1,), (1,)), ((), ()))
dot = functools.partial(lax.dot_general, preferred_element_type=jnp.float32)


def pack_kernel(owner_ref, far_grad_ref, packed_ref, count_ref, grad_ref, sem):
    blocks = grad_ref.shape[0]
    slots = packed_ref.shape[0] // blocks
    copy = pltpu.make_async_copy(far_grad_ref, grad_ref, sem)
    copy.start()
    packed_ref[...] = jnp.zeros_like(packed_ref)
    for owner in range(blocks):
        count_ref[owner] = 0
    copy.wait()
    for b in range(blocks):
        owner = owner_ref[b]
        rank = count_ref[owner]
        count_ref[owner] = rank + 1
        packed_ref[owner * slots + rank] = grad_ref[b]


def pack(owner_map, gradient, slots):
    blocks = gradient.shape[0]
    packed = (blocks * slots,) + gradient.shape[1:]
    return pl.pallas_call(
        pack_kernel,
        grid_spec=pltpu.PrefetchScalarGridSpec(
            num_scalar_prefetch=1,
            grid=(1,),
            in_specs=[pl.BlockSpec(memory_space=pltpu.HBM)],
            out_specs=whole(packed),
            scratch_shapes=[
                pltpu.SMEM((blocks,), jnp.int32),
                pltpu.VMEM(gradient.shape, gradient.dtype),
                pltpu.SemaphoreType.DMA,
            ],
        ),
        out_shape=jax.ShapeDtypeStruct(packed, gradient.dtype),
        compiler_params=pltpu.CompilerParams(vmem_limit_bytes=16 * 1024 * 1024),
        cost_estimate=pl.CostEstimate(flops=0, bytes_accessed=1 << 20, transcendentals=0),
    )(pltpu.with_memory_space_constraint(owner_map, pltpu.HBM), pltpu.with_memory_space_constraint(gradient, pltpu.HBM))


def fan_kernel(plane_ref, fan_ref):
    for n in range(near):
        for slot in range(parts):
            if slot < plane_ref.shape[2]:
                fan_ref[n, slot] = plane_ref[:, n, slot]
            else:
                fan_ref[n, slot] = jnp.zeros(fan_ref.shape[2:], fan_ref.dtype)


def fan(in_plane):
    _, _, slots, rows, width = in_plane.shape
    return pl.pallas_call(
        fan_kernel,
        out_shape=jax.ShapeDtypeStruct((near, parts, far, rows, width), in_plane.dtype),
        in_specs=[pl.BlockSpec(memory_space=pltpu.VMEM)],
        out_specs=pl.BlockSpec(memory_space=pltpu.VMEM),
        compiler_params=pltpu.CompilerParams(vmem_limit_bytes=16 * 1024 * 1024),
        cost_estimate=pl.CostEstimate(flops=0, bytes_accessed=1 << 20, transcendentals=0),
    )(in_plane)


def roots_kernel(
    place_ref, left_ref, right_ref, one_ref, two_ref, three_ref,
    left_high_ref, left_low_ref, right_high_ref, right_low_ref, high_ref, low_ref,
):
    part = place_ref[1]
    width = left_ref.shape[1]

    def span(step):
        at = lax.rem(part + step, parts)
        return pl.ds(pl.multiple_of(at * width, width), width)

    def spread(root, own_ref, high_ref, low_ref):
        def put(row, col, block):
            high, low = split_two(block)
            high_ref[span(row), span(col)] = high
            low_ref[span(row), span(col)] = low

        def put_pair(row, col, block):
            put(row, col, block)
            put(col, row, block.T)

        put(0, 0, own_ref[0, :, span(0)])
        for step in range(1, parts):
            put_pair(0, step, own_ref[0, :, span(step)])
        put(1, 1, one_ref[root, :, :width])
        put_pair(1, 3, one_ref[root, :, width : 2 * width])
        put_pair(1, 2, one_ref[root, :, 2 * width :])
        put(2, 2, two_ref[root])
        put(3, 3, three_ref[root, :, :width])
        put_pair(3, 2, three_ref[root, :, width:])

    spread(0, left_ref, high_ref, low_ref)
    spread(1, right_ref, right_high_ref, right_low_ref)
    size = high_ref.shape[0]
    row = lax.broadcasted_iota(jnp.int32, (size, size), 0)
    col = lax.broadcasted_iota(jnp.int32, (size, size), 1)
    z = lax.shift_right_logical(row, 2) & (far - 1)
    source = z * (size // far) + lax.shift_right_logical(row, 6) * 4 + (row & 3)
    order = jnp.where(col == source, 1.0, 0.0).astype(jnp.bfloat16)
    left_high_ref[...] = dot(high_ref[...], order, nt).astype(jnp.bfloat16)
    left_low_ref[...] = dot(low_ref[...], order, nt).astype(jnp.bfloat16)


in_vmem = pl.BlockSpec(memory_space=pltpu.VMEM)
in_smem = pl.BlockSpec(memory_space=pltpu.SMEM)


def whole(shape):
    return pl.BlockSpec(shape, lambda i, *_: (0,) * len(shape))


def spread_roots(place, left_root, right_root, others):
    _, width, order = right_root.shape
    mine = pl.BlockSpec((1, width, order), lambda i, place: (place[2], 0, 0))
    out = jax.ShapeDtypeStruct((order, order), jnp.bfloat16)
    return pl.pallas_call(
        roots_kernel,
        grid_spec=pltpu.PrefetchScalarGridSpec(
            num_scalar_prefetch=1,
            grid=(1,),
            in_specs=[mine, mine] + [whole(other.shape) for other in others],
            out_specs=[whole(out.shape)] * 4,
            scratch_shapes=[pltpu.VMEM(out.shape, out.dtype)] * 2,
        ),
        out_shape=[out] * 4,
        compiler_params=pltpu.CompilerParams(vmem_limit_bytes=32 * 1024 * 1024),
        cost_estimate=pl.CostEstimate(flops=0, bytes_accessed=5 << 20, transcendentals=0),
    )(place, left_root, right_root, *others)


def power(exponent):
    half = jnp.floor(exponent * 0.5)
    return jnp.exp2(half), jnp.exp2(exponent - half)


def coded(value):
    value = jnp.maximum(value, 1e-37)
    exponent = jnp.floor(jnp.log2(value)) + 1.0
    one, two = power(-exponent)
    share = value * one * two * 16384.0
    high = jnp.floor(share)
    return exponent, high, jnp.floor((share - high) * 16384.0)


def decoded(exponent, high, low):
    one, two = power(exponent - 14.0)
    return jnp.where(high > 0, (high + low * (1.0 / 16384.0)) * one * two, 0.0)


def square_root_code(value, top):
    root = jnp.sqrt(jnp.abs(value) * (code_top * code_top / top))
    return jnp.round(jnp.where(value < 0, -root, root)).astype(jnp.int32)


def precondition_kernel(
    place_ref, grad_ref, left_high_ref, left_low_ref, right_high_ref, right_low_ref, message_ref, late_ref, sems
):
    order = left_high_ref.shape[0]
    late = pltpu.make_async_copy(right_high_ref, late_ref.at[0], sems.at[0])
    last = pltpu.make_async_copy(right_low_ref, late_ref.at[1], sems.at[1])
    late.start()
    last.start()
    grad = jnp.concatenate([grad_ref[:, m].reshape(order, -1) for m in range(parts)], axis=1)
    half = dot(left_high_ref[...], grad, nn) + dot(left_low_ref[...], grad, nn)
    half_high, half_low = split_two(half)
    late.wait()
    right_high = late_ref[0]
    result = dot(half_high, right_high, nn) + dot(half_low, right_high, nn)
    last.wait()
    result += dot(half_high, late_ref[1], nn)
    taken = place_ref[3]
    result = jnp.where(taken > 0, result, 0.0)
    top = jnp.maximum(jnp.max(jnp.abs(result)), 1e-30)
    code = square_root_code(result, top)
    deep, width = message_ref.shape[2:]
    for z in range(far):
        for device in range(near):
            for m in range(parts):
                row = (z * near + device) * deep
                message_ref[device * parts + m, z] = code[row : row + deep, m * width : (m + 1) * width].astype(
                    jnp.int16
                )

    wide = grad.astype(jnp.float32)
    grad_sum = jnp.where(taken > 0, jnp.sum(wide * wide), 0.0)
    upd_sum = jnp.sum(result * result)
    row = lax.broadcasted_iota(jnp.int32, (8, 128), 0)
    at = lax.broadcasted_iota(jnp.int32, (8, 128), 1) - place_ref[0] * 16
    sum_at = at - place_ref[1] * 4
    top_at = at - place_ref[1] * 3
    is_up = jnp.where(taken > 1, 1, 0)
    exponent, high, low = coded(
        jnp.where(sum_at == is_up, grad_sum, jnp.where(sum_at == 2 + is_up, upd_sum, 0.0))
    )
    in_sums = (sum_at >= 0) & (sum_at < 4)
    sums = jnp.where(in_sums, jnp.where(row == 0, exponent, jnp.where(row == 1, high, low)), 0.0)
    exponent, high, low = coded(jnp.full((8, 128), top))
    in_tops = (top_at >= 0) & (top_at < 3) & (place_ref[1] < parts - 1)
    tops = jnp.where(in_tops, jnp.where(top_at == 0, exponent, jnp.where(top_at == 1, high, low)), 0.0)
    facts = jnp.where(row < 3, sums, tops)[:deep].astype(jnp.int32).astype(jnp.int16)
    for device in range(near * parts):
        message_ref[device, far] = facts


def precondition(place, landed, roots):
    _, rows, width = landed.shape
    order = near * rows
    landed = landed.reshape(near, parts, rows, width)
    message = (near * parts, far + 1, rows // far, width)
    return pl.pallas_call(
        precondition_kernel,
        in_specs=[in_smem] + [in_vmem] * 3 + [pl.BlockSpec(memory_space=pltpu.HBM)] * 2,
        out_specs=in_vmem,
        scratch_shapes=[pltpu.VMEM((2, order, order), jnp.bfloat16), pltpu.SemaphoreType.DMA((2,))],
        out_shape=jax.ShapeDtypeStruct(message, jnp.int16),
        compiler_params=pltpu.CompilerParams(vmem_limit_bytes=32 * 1024 * 1024),
        cost_estimate=pl.CostEstimate(flops=10 * order**3, bytes_accessed=4 << 20, transcendentals=0),
    )(place, landed, *roots[:2], *(pltpu.with_memory_space_constraint(root, pltpu.HBM) for root in roots[2:]))


def terms_kernel(place_ref, block_ref, own_ref, one_ref, two_ref, three_ref, term_ref):
    block = block_ref[...]
    out_refs = (own_ref, one_ref, two_ref, three_ref)
    width = own_ref.shape[1] - 16
    row = lax.broadcasted_iota(jnp.int32, (16, block.shape[1]), 0)
    for side in range(2):
        term = dot(block, block, nt if side == 0 else tn)
        top = jnp.maximum(jnp.max(jnp.abs(term)), 1e-30)
        term_ref[...] = square_root_code(term, top)
        exponent, high, low = coded(jnp.full(row.shape, top))
        scale = jnp.where(row == 0, exponent, jnp.where(row == 1, high, low)).astype(jnp.int32).astype(jnp.int16)
        for step in range(parts):
            at = lax.rem(place_ref[1] + step, parts)
            out_refs[step][side, :width] = term_ref[pl.ds(pl.multiple_of(at * width, width), width), :].astype(
                jnp.int16
            )
            out_refs[step][side, width:] = scale


def terms(place, block):
    order = block.shape[0]
    out = jax.ShapeDtypeStruct((2, order // parts + 16, order), jnp.int16)
    return pl.pallas_call(
        terms_kernel,
        grid_spec=pltpu.PrefetchScalarGridSpec(
            num_scalar_prefetch=1,
            grid=(1,),
            in_specs=[whole(block.shape)],
            out_specs=[whole(out.shape)] * parts,
            scratch_shapes=[pltpu.VMEM((order, order), jnp.int32)],
        ),
        out_shape=[out] * parts,
        compiler_params=pltpu.CompilerParams(vmem_limit_bytes=32 * 1024 * 1024),
        cost_estimate=pl.CostEstimate(flops=4 * order**3, bytes_accessed=2 << 20, transcendentals=0),
    )(place, block)


def stats_kernel(place_ref, own_ref, one_ref, two_ref, three_ref, left_ref, right_ref, left_new_ref, right_new_ref):
    slots, width, order = left_ref.shape
    sides = ((left_ref, left_new_ref), (right_ref, right_new_ref))
    for slot in range(slots):
        steps = lax.rem(place_ref[1] + parts - slot, parts)
        taken = place_ref[4 + slot]
        for step, terms_ref in enumerate((own_ref, one_ref, two_ref, three_ref)):

            @pl.when((steps == step) & (taken > 0))
            def _(terms_ref=terms_ref):
                for side, (old_ref, new_ref) in enumerate(sides):
                    code = terms_ref[side, :width].astype(jnp.int32).astype(jnp.float32)
                    scale = terms_ref[side, width:].astype(jnp.int32).astype(jnp.float32)
                    top = decoded(scale[0:1], scale[1:2], scale[2:3])
                    gain = top * ((1.0 - decay_rate) / order / (code_top * code_top))
                    new_ref[slot] = decay_rate * old_ref[slot] + code * jnp.abs(code) * gain

        @pl.when(taken == 0)
        def _():
            for old_ref, new_ref in sides:
                new_ref[slot] = old_ref[slot]


def new_stats(place, coded_terms, left_stats, right_stats):
    out = jax.ShapeDtypeStruct(left_stats.shape, jnp.float32)
    return pl.pallas_call(
        stats_kernel,
        grid_spec=pltpu.PrefetchScalarGridSpec(
            num_scalar_prefetch=1,
            grid=(1,),
            in_specs=[whole(coded_terms[0].shape)] * parts + [whole(out.shape)] * 2,
            out_specs=[whole(out.shape)] * 2,
        ),
        out_shape=[out] * 2,
        compiler_params=pltpu.CompilerParams(vmem_limit_bytes=32 * 1024 * 1024),
        cost_estimate=pl.CostEstimate(flops=0, bytes_accessed=5 << 20, transcendentals=0),
    )(place, *coded_terms, left_stats, right_stats)


def repack_kernel(back_ref, ahead_ref):
    cells = ahead_ref.shape[1] - 1
    slots = cells // near
    for device in range(near):
        for slot in range(slots):
            ahead_ref[:, device * slots + slot] = back_ref[device * parts + slot, :far]
    wide = [back_ref[device, far].astype(jnp.int32) for device in range(near * parts)]
    facts = functools.reduce(jnp.add, wide).astype(jnp.int16)
    for z in range(far):
        ahead_ref[z, cells] = facts


def repack(back, slots):
    return pl.pallas_call(
        repack_kernel,
        out_shape=jax.ShapeDtypeStruct((far, near * slots + 1) + back.shape[2:], back.dtype),
        in_specs=[pl.BlockSpec(memory_space=pltpu.VMEM)],
        out_specs=pl.BlockSpec(memory_space=pltpu.VMEM),
        compiler_params=pltpu.CompilerParams(vmem_limit_bytes=16 * 1024 * 1024),
        cost_estimate=pl.CostEstimate(flops=0, bytes_accessed=1 << 20, transcendentals=0),
    )(back)


def finish_kernel(at_ref, spot_ref, up_ref, arrived_ref, update_ref, factor_ref):
    groups = arrived_ref.shape[0] // far
    facts = [arrived_ref[z * groups + groups - 1].astype(jnp.int32).astype(jnp.float32) for z in range(far)]
    row = lambda r: jnp.concatenate([fact[r : r + 1] for fact in facts], axis=0)
    sums = jnp.sum(decoded(row(0), row(1), row(2)), axis=0, keepdims=True)
    kind = lax.rem(lax.broadcasted_iota(jnp.int32, sums.shape, 1), 4)
    total = lambda k: jnp.sum(jnp.where(kind == k, sums, 0.0), axis=1, keepdims=True)
    gate_scale = jnp.sqrt(total(0) / total(2))
    up_scale = jnp.sqrt(total(1) / total(3))
    tops = row(3)
    lanes = tops.shape[1]
    steps = decoded(tops, pltpu.roll(tops, lanes - 1, 1), pltpu.roll(tops, lanes - 2, 1))
    steps = steps * (1.0 / (code_top * code_top))
    spot = spot_ref[...]
    lane = lax.broadcasted_iota(jnp.int32, spot.shape, 1)
    mine = jnp.zeros(spot.shape, jnp.float32)
    for z in range(far):
        mine += jnp.where(spot == lane + z * lanes, steps[z : z + 1], 0.0)
    step = jnp.sum(mine, axis=1, keepdims=True)
    factor_ref[...] = jnp.where(up_ref[...] > 0, up_scale, gate_scale) * step

    for b in range(update_ref.shape[0]):
        code = arrived_ref[at_ref[b]].astype(jnp.int32).astype(jnp.float32)
        update_ref[b] = (code * jnp.abs(code) * factor_ref[b : b + 1, :]).astype(jnp.bfloat16)


def finish(cell_ids, spot, up, arrived):
    blocks = cell_ids.shape[0]
    return pl.pallas_call(
        finish_kernel,
        in_specs=[in_smem] + [in_vmem] * 3,
        out_specs=in_vmem,
        scratch_shapes=[pltpu.VMEM((blocks, arrived.shape[2]), jnp.float32)],
        out_shape=jax.ShapeDtypeStruct((blocks,) + arrived.shape[1:], jnp.bfloat16),
        compiler_params=pltpu.CompilerParams(vmem_limit_bytes=16 * 1024 * 1024),
        cost_estimate=pl.CostEstimate(flops=0, bytes_accessed=1 << 20, transcendentals=0),
    )(cell_ids, spot, up, arrived)


def on_device(gradient, owner_map, left_stats, right_stats, left_root, right_root):
    block_count, row_share, col_share = gradient.shape
    capacity, part_rows, block_size = left_stats.shape
    my_owner = lax.axis_index("fsdp")
    my_part = lax.axis_index("mp")

    packed = pack(owner_map, gradient, capacity).reshape(far, near, capacity, row_share, col_share)
    in_plane = exchange(packed, "fsdp", far_groups)

    def send(steps, k):
        slot = jnp.minimum((my_part + k) % parts, capacity - 1)

        def column(root, step):
            start = (my_part + step) % parts * part_rows
            return lax.dynamic_slice(root, (slot, 0, start), (1, part_rows, part_rows))

        rows = [jnp.concatenate([column(root, step) for step in steps], axis=2) for root in (left_root, right_root)]
        pairs = [(i, (i + k) % parts) for i in range(parts)]
        return lax.ppermute(jnp.concatenate(rows, axis=0), "mp", pairs)

    three = send((0, 3), 1)
    two = send((0,), 2)
    one = send((0, 2, 1), 3)
    in_plane, one, two, three, owner_map = lax.optimization_barrier((in_plane, one, two, three, owner_map))
    my_slot = jnp.minimum(my_part, capacity - 1)
    place = jnp.stack([my_owner % near, my_part, my_slot])
    roots = spread_roots(place, left_root, right_root, (one, two, three))

    fanned = fan(in_plane).reshape(near * parts, far * row_share, col_share)
    landed = exchange(fanned, ("fsdp", "mp"), plane_groups)

    cell_ids = cell_index(owner_map, capacity)
    up_block = jnp.arange(block_count, dtype=jnp.int32) >= block_count // 2
    my_cells = my_owner * capacity + jnp.arange(capacity, dtype=jnp.int32)
    holding = cell_ids[None, :] == my_cells[:, None]
    taken = jnp.max(jnp.where(holding, 1 + up_block.astype(jnp.int32)[None, :], 0), axis=1)
    my_taken = jnp.where(my_part < capacity, taken[my_slot], 0)
    place = jnp.concatenate([place, my_taken[None], taken])
    message = precondition(place, landed, roots)
    landed, message = lax.optimization_barrier((landed, message))
    back = exchange(message, ("fsdp", "mp"), plane_groups)

    block = landed.reshape(near, parts, far, row_share, col_share).transpose(2, 0, 3, 1, 4)
    made = terms(place, block.reshape(block_size, block_size))
    back, own_terms, *other_terms = lax.optimization_barrier((back, *made))
    coded_terms = [own_terms]
    for k, other in enumerate(other_terms, 1):
        coded_terms.append(lax.ppermute(other, "mp", [(i, (i + k) % parts) for i in range(parts)]))
    arrived = exchange(repack(back, capacity), "fsdp", far_groups)
    left_new, right_new = new_stats(place, coded_terms, left_stats, right_stats)

    cells = near * capacity
    spot = cell_ids // cells * 128 + cell_ids % cells // capacity * 16 + cell_ids % capacity * 3
    across = lambda array: jnp.broadcast_to(array.astype(jnp.int32)[:, None], (block_count, 128))
    arrived = arrived.reshape(far * (cells + 1), row_share, col_share)
    update = finish(cell_ids + cell_ids // cells, across(spot), across(up_block), arrived)
    return (update, left_new, right_new)


def solution(mesh):
    placed = (
        P(None, "fsdp", "mp"),
        P(),
        P("fsdp", "mp", None),
        P("fsdp", "mp", None),
        P("fsdp", "mp", None),
        P("fsdp", "mp", None),
    )
    return jax.shard_map(
        on_device,
        mesh=mesh,
        in_specs=placed,
        out_specs=(P(None, "fsdp", "mp"), P("fsdp", "mp", None), P("fsdp", "mp", None)),
        check_vma=False,
    )
```
